256 devices in a mesh: dp: 64 (over z, y, core), mp: 4 (over x).
Axes of the slice: x: 4, y: 4, z: 8, core: 2. Of those that a mesh axis runs over, the one named last changes fastest.
Arguments:
- queries: bfloat16 [8192, 64, 576], P('dp', 'mp'), may hold values from -17 to 17
- latents: bfloat16 [8192, 576], P('dp'), may hold values from -6 to 6
- doc_ids: int32 [8192], replicated, may hold values from 0 to 127, never falling along the last dimension, each value on 1 to 128 neighbouring positions
- hidden_rows: bfloat16 [8192, 5120], P('dp', 'mp'), may hold values from -6 to 6
- expert_ids: int32 [8192, 6], P('dp'), may hold values from 0 to 31, all different within a row; in each aligned block of 128 rows (0 to 127, 128 to 255, ...) at most 30 rows name the same one
- gate_scores: float32 [8192, 6], P('dp'), may hold values from 0.05 to 0.6
- gate_weight: bfloat16 [64, 2560, 1536], P('dp', None, 'mp'), may hold values from -0.078125 to 0.078125
- up_weight: bfloat16 [64, 2560, 1536], P('dp', None, 'mp'), may hold values from -0.078125 to 0.078125
- down_weight: bfloat16 [64, 1536, 2560], P('dp', 'mp'), may hold values from -0.15625 to 0.15625
Outputs:
- attn_out: bfloat16 [8192, 64, 512], P('dp', 'mp')
- moe_out: bfloat16 [8192, 5120], P('dp', 'mp')
The draws below stay inside these ranges and needn't reach their ends.
Inputs may be any that keep to these rules, and one draw needn't show every extreme that they name: `doc_ids`: document numbers never fall along the tokens; every document has 1 to 128 tokens. `expert_ids`: each token names 6 different experts; no expert is named by more than 30 tokens of one aligned block of 128 tokens.
All inputs are finite; a program needn't handle non-finite values.
Results may differ from the reference program's by a relative error of at most 0.015.
Values may be sent and summed in bfloat16 or wider, within the bound.
A program may use at most 128 MiB of HBM per device.

```python
import math
import jax
import jax.numpy as jnp
import numpy as np
from jax import lax

D = 5120
FF = 1536
TOP = 6
LAT = 512
HEADS = 64
TOK_DEV = 128
KV_DIM = 576
TOKENS = 8192
DOCS = 128
EXPERTS = 32
CAP = 30
HID_DEV = 384
PIECE = 640
N_DP = 64
N_MP = 4


def shared_normal(key):
    return jax.random.truncated_normal(jax.random.fold_in(key, 11), -6.0, 6.0, (TOKENS, KV_DIM), jnp.float32)


def draw_latents(key, part):
    base = shared_normal(key)
    return base.astype(jnp.bfloat16)


def draw_queries(key, part):
    key = jax.random.fold_in(key, 5)
    values = jax.random.truncated_normal(key, -6.0, 6.0, (TOKENS, HEADS, KV_DIM), jnp.float32)
    return values.astype(jnp.bfloat16)


def steps_of(key, shape, shards, smallest, top_value):
    gain = 1.0
    for axis_at, shards_of in shards:
        heights = jax.random.uniform(jax.random.fold_in(jax.random.fold_in(key, 6), axis_at), (shards_of,), jnp.float32, smallest / len(shards), top_value / len(shards))
        gain = gain * jnp.repeat(jnp.exp(heights), shape[axis_at] // shards_of).reshape((-1,) + (1,) * (len(shape) - 1 - axis_at))
    return gain


def profile(number_of, total, most, lean):
    portions = [(1 << 20) // math.isqrt(grade ** lean) + 1 for grade in range(2, number_of + 1)]
    surplus, counts = total - most - (number_of - 1), [1] * (number_of - 1)
    while surplus > 0:
        movable = [i for i in range(number_of - 1) if counts[i] < most]
        pool, budget = sum([portions[i] for i in movable]), surplus
        for i in movable:
            more = min(most - counts[i], max(1, budget * portions[i] // pool), surplus)
            counts[i] = counts[i] + more
            surplus = surplus - more
    return np.array([most] + counts)


def uneven(rng, amount, total, bound, skew):
    if amount == 2:
        one = jax.random.randint(rng, (), max(1, total - bound), min(bound, total - 1) + 1)
        return jnp.stack([one, total - one])
    lengths = jnp.asarray(profile(amount, total, bound, skew), jnp.int32)
    couples = (amount - 1) // 2
    source_of, sink = lengths[1:1 + 2 * couples:2], lengths[2:2 + 2 * couples:2]
    room = jnp.minimum(source_of - 1, bound - sink)
    passed = jax.random.randint(jax.random.fold_in(rng, 1), (couples,), 0, 1 << 20) % (room + 1)
    lengths = lengths.at[1:1 + 2 * couples:2].set(source_of - passed).at[2:2 + 2 * couples:2].set(sink + passed)
    return lengths[jax.random.permutation(jax.random.fold_in(rng, 2), amount)]


def assign_block(key, own, number, rows, number_of, top, reach, lean):
    sequence = jax.random.permutation(key, number_of)
    packed, usual = shares(number_of, rows * top, reach, lean, True), shares(number_of, rows * top, reach, lean, False)
    places = jnp.arange(number_of)

    def named(lengths, turn):
        used = int((lengths > 0).sum())
        fixed = max(1, used // 4)
        moved = fixed + (places - fixed + turn * (used - fixed)) % max(1, number_of - fixed)
        return jnp.zeros((number_of,), jnp.int32).at[sequence[jnp.where(places < fixed, places, moved)]].set(jnp.asarray(lengths, jnp.int32))

    lengths = jnp.where(number % 4 == 0, named(packed, number // 4), named(usual, number - number // 4 - 1))
    mixed = jax.random.permutation(jax.random.fold_in(own, 3), number_of)
    donor, sink = mixed[0:number_of // 2 * 2:2], mixed[1:number_of // 2 * 2:2]
    room = jnp.minimum(lengths[donor] - 1, reach - lengths[sink]) // 2
    room = jnp.where((donor == sequence[0]) | (sink == sequence[0]) | (lengths[sink] == 0), 0, jnp.maximum(room, 0))
    moved = jax.random.randint(jax.random.fold_in(own, 4), (number_of // 2,), 0, 1 << 20) % (room + 1)
    lengths = lengths.at[donor].add(-moved).at[sink].add(moved)
    labels = jnp.searchsorted(jnp.cumsum(lengths), jnp.arange(rows * top), side="right").astype(jnp.int32)
    listing = labels.reshape(top, rows).T
    listing = listing[jax.random.permutation(jax.random.fold_in(own, 1), rows)]
    turn = jax.random.randint(jax.random.fold_in(own, 2), (rows, 1), 0, top)
    return jnp.take_along_axis(listing, (jnp.arange(top)[None, :] + turn) % top, axis=1)


def shares(amount, total, limit, skew, full):
    portions = [(1 << 20) // math.isqrt(grade ** skew) + 1 for grade in range(1, amount + 1)]
    largest = limit if full else min(limit, max(-(-total // amount), total * portions[0] // sum(portions)))
    least = 1 if total - largest >= amount - 1 else 0
    given, rest = [largest] + [least] * (amount - 1), total - largest - least * (amount - 1)
    while rest > 0:
        free = [i for i in range(1, amount) if given[i] < largest] or [i for i in range(1, amount) if given[i] < limit]
        pool, left = sum([portions[i] for i in free]), rest
        for i in free:
            more = min(limit - given[i], max(1, left * portions[i] // pool), rest)
            given[i] = given[i] + more
            rest = rest - more
    return np.array(given)


def centred(stream_key, extent, scale, most, split=(), kind=jnp.bfloat16):
    array = jax.random.normal(stream_key, extent, jnp.float32) * scale
    if len(split) > 0:
        array = steps_of(stream_key, extent, split, -0.22, 0.18) * array
    return jnp.clip(array, min=-most, max=most).astype(kind)


def setup_inputs(seed: int = 0) -> dict:
    streams_of = jax.random.split(jax.random.key(seed), 10)
    queries = draw_queries(jax.random.fold_in(streams_of[9], 71), 0)
    latents = draw_latents(jax.random.fold_in(streams_of[9], 71), 0)
    doc_ids = jnp.searchsorted(jnp.cumsum(uneven(streams_of[2], DOCS, TOKENS, TOK_DEV, 2)), jnp.arange(TOKENS), side="right").astype(jnp.int32)
    hidden_rows = centred(streams_of[3], (TOKENS, D), 1.0, 6.0, ((0, 64), (1, 4)))
    expert_ids_keys = jax.random.split(jax.random.fold_in(streams_of[4], 1), TOKENS // TOK_DEV)
    expert_ids_turns = jax.random.permutation(jax.random.fold_in(streams_of[4], 3), TOKENS // TOK_DEV)
    expert_ids = jax.vmap(lambda own, number: assign_block(jax.random.fold_in(streams_of[4], 2), own, number, TOK_DEV, EXPERTS, TOP, CAP, 1))(expert_ids_keys, expert_ids_turns).reshape((TOKENS, TOP))
    gate_scores = jnp.clip(0.05 + 0.55 * jax.random.uniform(streams_of[5], (TOKENS, TOP), jnp.float32) ** steps_of(streams_of[5], (TOKENS, TOP), ((0, 64),), -0.2, 0.2), 0.05, 0.6)
    gate_weight = centred(streams_of[6], (2 * EXPERTS, D // 2, FF), D ** -0.5, 0.078125, ((0, 64), (2, 4)))
    up_weight = centred(streams_of[7], (2 * EXPERTS, D // 2, FF), D ** -0.5, 0.078125, ((0, 64), (2, 4)))
    down_weight = centred(streams_of[8], (2 * EXPERTS, FF, D // 2), FF ** -0.5, 0.15625, ((0, 64), (1, 4)))
    return dict(queries=queries, latents=latents, doc_ids=doc_ids, hidden_rows=hidden_rows, expert_ids=expert_ids, gate_scores=gate_scores, gate_weight=gate_weight, up_weight=up_weight, down_weight=down_weight)


score_scale = 1.0 / math.sqrt(192.0)
neg_large = -1e+30

def softmax_rows(scores, allowed):
    masked = jnp.where(allowed, scores, neg_large)
    row_top = lax.optimization_barrier(jnp.max(masked, axis=-1, keepdims=True))
    lifted = jnp.where(allowed, jnp.exp(masked - row_top), 0.0)
    return (lifted / lax.optimization_barrier(jnp.sum(lifted, axis=-1, keepdims=True))).astype(jnp.bfloat16)

def reference(queries, latents, doc_ids, hidden_rows, expert_ids, gate_scores, gate_weight, up_weight, down_weight):
    doc_index = doc_ids.astype(jnp.int32)
    padded_lat = jnp.concatenate([jnp.zeros((TOK_DEV, KV_DIM), latents.dtype), latents], 0)
    padded_ids = jnp.concatenate([jnp.full((TOK_DEV,), -1, jnp.int32), doc_index], 0)

    def attend(block):
        start = (block * TOK_DEV).astype(jnp.int32)
        query_blk = lax.dynamic_slice_in_dim(queries, start, TOK_DEV, 0)
        keys = lax.dynamic_slice_in_dim(padded_lat, start, 2 * TOK_DEV, 0)
        key_ids = lax.dynamic_slice_in_dim(padded_ids, start, 2 * TOK_DEV, 0)
        query_ids = lax.dynamic_slice_in_dim(doc_index, start, TOK_DEV, 0)
        query_pos = jnp.arange(TOK_DEV, dtype=jnp.int32) + TOK_DEV
        key_pos = jnp.arange(2 * TOK_DEV, dtype=jnp.int32)
        allowed = (query_ids[:, None] == key_ids[None, :]) & (key_pos[None, :] <= query_pos[:, None])
        scores = jnp.einsum('thf,uf->thu', query_blk.astype(jnp.float32), keys.astype(jnp.float32)) * score_scale
        probs = softmax_rows(scores, allowed[:, None, :])
        return jnp.einsum('thu,uf->thf', probs.astype(jnp.float32), keys[:, :LAT].astype(jnp.float32)).astype(jnp.bfloat16)
    attn_out = lax.map(attend, jnp.arange(N_DP, dtype=jnp.int32)).reshape(TOKENS, HEADS, LAT)
    routes = expert_ids.astype(jnp.int32).reshape(N_DP, TOK_DEV * TOP)
    onehot = (routes[:, :, None] == jnp.arange(EXPERTS, dtype=jnp.int32)[None, None, :]).astype(jnp.int32)
    earlier = jnp.cumsum(onehot, axis=1) - onehot
    slots = lax.optimization_barrier(jnp.sum(earlier * onehot, axis=2))
    sources = jnp.arange(N_DP, dtype=jnp.int32)[:, None]
    owners = sources * TOK_DEV + jnp.arange(TOK_DEV * TOP, dtype=jnp.int32)[None, :] // TOP
    places = ((routes * N_DP + sources) * CAP + slots).reshape(-1)
    table = jnp.full((EXPERTS * N_DP * CAP,), -1, jnp.int32).at[places].set(owners.reshape(-1))
    weights = jnp.zeros((EXPERTS * N_DP * CAP,), jnp.float32).at[places].set(gate_scores.reshape(-1).astype(jnp.float32))
    rows_count = N_DP * CAP

    def expert_step(total, expert):
        picked = lax.dynamic_slice_in_dim(table, expert * rows_count, rows_count, 0)
        scales = lax.dynamic_slice_in_dim(weights, expert * rows_count, rows_count, 0)
        safe = jnp.maximum(picked, 0)
        rows = hidden_rows[safe]
        gate_full = lax.dynamic_slice_in_dim(gate_weight, 2 * expert, 2, 0).reshape(D, FF)
        up_full = lax.dynamic_slice_in_dim(up_weight, 2 * expert, 2, 0).reshape(D, FF)
        down_pair = lax.dynamic_slice_in_dim(down_weight, 2 * expert, 2, 0)
        down_full = down_pair.reshape(2, FF, N_MP, PIECE).transpose(1, 2, 0, 3).reshape(FF, D)
        gate = jnp.dot(rows, gate_full, preferred_element_type=jnp.float32)
        upper = jnp.dot(rows, up_full, preferred_element_type=jnp.float32)
        hidden = (jax.nn.silu(gate) * upper).astype(jnp.bfloat16)
        result = jnp.zeros((rows_count, D), jnp.float32)
        for quarter in range(N_MP):
            lower_unit = quarter * HID_DEV
            part = jnp.dot(hidden[:, lower_unit:lower_unit + HID_DEV], down_full[lower_unit:lower_unit + HID_DEV], preferred_element_type=jnp.float32).astype(jnp.bfloat16)
            result = result + lax.optimization_barrier(part).astype(jnp.float32)
        total = total.at[safe].add(scales[:, None] * result)
        return (total, None)
    moe_total, _ = lax.scan(expert_step, jnp.zeros((TOKENS, D), jnp.float32), jnp.arange(EXPERTS, dtype=jnp.int32))
    return (attn_out, moe_total.astype(jnp.bfloat16))
```

```python
import functools
import math

import jax
import jax.numpy as jnp
from jax import lax
from jax.experimental import pallas as pl
from jax.experimental.pallas import tpu as pltpu
from jax.sharding import PartitionSpec as P

LAT = 512
SLOTS = 32
NX = 4
NY = 4
Z_ORDER = {8: (1, -2, 2, -3, 3, 4, -1, 0), 4: (1, 2, -1, 0), 2: (1, 0)}

score_scale = 1.0 / math.sqrt(192.0)
neg_large = -1e30
MESH = pl.DeviceIdType.MESH


def layer_kernel(
    nz,
    ny,
    ids_ref,
    score_ref,
    tok_ref,
    gate_ref,
    up_ref,
    down_ref,
    query_ref,
    latent_ref,
    doc_ref,
    out_ref,
    attn_ref,
    disp,
    rows,
    gu,
    dn,
    relay_dn,
    hid,
    outb,
    ret,
    acc,
    place_ref,
    ghi_ref,
    glo_ref,
    query,
    attn,
    keys,
    bias,
    local_sem,
    q_sem,
    lat_send,
    lat_recv,
    w_send,
    w_recv,
    disp_send,
    disp_recv,
    x_send,
    x_recv,
    h_send,
    h_recv,
    ret_send,
    ret_recv,
):
    top, tokens = ids_ref.shape
    heads = query_ref.shape[0]
    width = tok_ref.shape[1]
    half_in, units = gate_ref.shape
    piece = down_ref.shape[1] // NX
    experts = nz * ny
    chunk = ny * SLOTS
    half = chunk // 2
    f32, bf16 = jnp.float32, jnp.bfloat16

    d = lax.axis_index("dp")
    x = lax.axis_index("mp")
    s = lax.rem(d, 2)
    p = lax.div(d, 2)
    z = lax.div(p, ny)
    y = lax.rem(p, ny)
    right = lax.rem(x + 1, NX)
    left = lax.rem(x + NX - 1, NX)
    opposite = lax.rem(x + 2, NX)
    mate = d + 1 - 2 * s

    def dev(zz, yy):
        return (zz * ny + yy) * 2 + s

    def offset(c):
        total = 0
        for at, by in enumerate(Z_ORDER[nz]):
            total = total + jnp.where(c == at, by, 0)
        return total

    def remote(src, dst, send, recv, dd, xx):
        return pltpu.make_async_remote_copy(
            src_ref=src, dst_ref=dst, send_sem=send, recv_sem=recv,
            device_id=(dd, xx), device_id_type=MESH,
        )

    def wait_in(ref, sem):
        pltpu.make_async_copy(ref, ref, sem).wait()

    own_in = pl.ds(pl.multiple_of(s * half_in, half_in), half_in)
    mate_in = pl.ds(pl.multiple_of((1 - s) * half_in, half_in), half_in)
    own_out = pl.ds(pl.multiple_of(s * piece, piece), piece)
    mate_out = pl.ds(pl.multiple_of((1 - s) * piece, piece), piece)
    gate_cols, up_cols = pl.ds(0, units), pl.ds(units, units)

    def unit_rows(q, start, count):
        return pl.ds(pl.multiple_of(q * units + start, units // 2), count)

    def unit_cols(q):
        return pl.ds(pl.multiple_of(q * units, units), units)

    def down_cols(q):
        return pl.ds(pl.multiple_of(q * piece, piece), piece)

    local_gate = pltpu.make_async_copy(gate_ref, gu.at[own_in, gate_cols], local_sem.at[0])
    local_up = pltpu.make_async_copy(up_ref, gu.at[own_in, up_cols], local_sem.at[1])
    local_down = pltpu.make_async_copy(
        down_ref.at[:, down_cols(x)], dn.at[unit_rows(x, 0, units), own_out], local_sem.at[2]
    )
    local_gate.start()
    local_up.start()
    local_down.start()
    local_query = pltpu.make_async_copy(query_ref, query, q_sem.at[0])
    local_query.start()

    barrier = pltpu.get_barrier_semaphore()

    def greet(dd, xx):
        pl.semaphore_signal(barrier, inc=1, device_id=(dd, xx), device_id_type=MESH)

    ring = experts * 2
    beside = lax.rem(d + 2 * s - 1 + ring, ring)
    following = lax.rem(d + 1, ring)
    greet(mate, x)
    greet(beside, x)
    greet(d, right)
    greet(d, left)

    def greet_peer(k, carry):
        greet(lax.rem(p + k, experts) * 2 + s, x)
        return carry

    lax.fori_loop(1, experts, greet_peer, 0)

    expert_at = lax.broadcasted_iota(jnp.int32, (experts, tokens), 0)
    named = jnp.zeros((experts, tokens), f32)
    weight = jnp.zeros((experts, tokens), f32)
    for k in range(top):
        hit = ids_ref[k : k + 1, :] == expert_at
        named = named + jnp.where(hit, 1.0, 0.0)
        weight = weight + jnp.where(hit, score_ref[k : k + 1, :], 0.0)
    row_at = lax.broadcasted_iota(jnp.int32, (tokens, tokens), 0)
    col_at = lax.broadcasted_iota(jnp.int32, (tokens, tokens), 1)
    before = jnp.dot(
        named.astype(bf16),
        jnp.where(row_at < col_at, 1.0, 0.0).astype(bf16),
        preferred_element_type=f32,
    )
    place_ref[...] = jnp.where(named > 0.5, before, -1.0).astype(bf16)
    whole = weight.astype(bf16)
    ghi_ref[...] = whole
    glo_ref[...] = (weight - whole.astype(f32)).astype(bf16)

    same = row_at == col_at
    keys[tokens:, :] = lax.dot_general(
        jnp.where(same, 1.0, 0.0).astype(bf16), latent_ref[...], (((1,), (1,)), ((), ())),
        preferred_element_type=f32,
    ).astype(bf16)
    lat_copy = remote(
        keys.at[pl.ds(tokens, tokens)], keys.at[pl.ds(0, tokens)],
        lat_send.at[0], lat_recv.at[0], following, x,
    )
    own_ids = doc_ref[pl.ds(d, 1), :]
    old_ids = doc_ref[pl.ds(lax.rem(d + ring - 1, ring), 1), :]
    own_col = jnp.sum(jnp.where(same, own_ids, 0).astype(f32), axis=1, keepdims=True)
    old_col = jnp.sum(jnp.where(same, old_ids, 0).astype(f32), axis=1, keepdims=True)
    old_col = old_col - jnp.where(d == 0, 1000.0, 0.0)
    ids_row = own_ids.astype(f32)
    bias[:tokens, :] = jnp.where(old_col == ids_row, 0.0, neg_large)
    bias[tokens:, :] = jnp.where((own_col == ids_row) & (row_at <= col_at), 0.0, neg_large)

    pl.semaphore_wait(barrier, experts - 1 + 4)

    to_mate = [
        remote(gate_ref, gu.at[own_in, gate_cols], w_send.at[0], w_recv.at[0], mate, x),
        remote(up_ref, gu.at[own_in, up_cols], w_send.at[1], w_recv.at[1], mate, x),
    ]
    halfu = units // 2
    to_side = [
        remote(
            down_ref.at[:, down_cols(right)], dn.at[unit_rows(x, 0, units), own_out],
            w_send.at[2], w_recv.at[2], d, right,
        ),
        remote(
            down_ref.at[:, down_cols(left)], dn.at[unit_rows(x, 0, units), own_out],
            w_send.at[3], w_recv.at[3], d, left,
        ),
        remote(
            down_ref.at[pl.ds(0, halfu), down_cols(opposite)], relay_dn.at[0],
            w_send.at[4], w_recv.at[4], d, right,
        ),
        remote(
            down_ref.at[pl.ds(halfu, halfu), down_cols(opposite)], relay_dn.at[1],
            w_send.at[5], w_recv.at[5], d, left,
        ),
    ]
    relays = [
        remote(
            relay_dn.at[0], dn.at[unit_rows(left, 0, halfu), own_out],
            w_send.at[6], w_recv.at[6], d, right,
        ),
        remote(
            relay_dn.at[1], dn.at[unit_rows(right, halfu, halfu), own_out],
            w_send.at[7], w_recv.at[7], d, left,
        ),
    ]
    down_to_mate = remote(
        dn.at[:, own_out], dn.at[:, own_out], w_send.at[8], w_recv.at[8], mate, x
    )

    def chunk_rows(c):
        return pl.ds(pl.multiple_of(c * chunk, chunk), chunk)

    def block_rows(c, dy):
        return pl.ds(pl.multiple_of(c * chunk + dy * SLOTS, SLOTS), SLOTS)

    def spread(c):
        zz = lax.rem(z + offset(c) + nz, nz)
        row = lax.broadcasted_iota(jnp.int32, (chunk, experts), 0)
        dest = zz * ny + ((y + (row // SLOTS)) % ny)
        return jnp.where(
            lax.broadcasted_iota(jnp.int32, (chunk, experts), 1) == dest, 1.0, 0.0
        ).astype(bf16)

    def chosen(sel):
        slot = (lax.broadcasted_iota(jnp.int32, (chunk, tokens), 0) % SLOTS).astype(f32)
        return jnp.dot(sel, place_ref[...], preferred_element_type=f32) == slot

    def disp_copy(c, dy):
        zz = lax.rem(z + offset(c) + nz, nz)
        return remote(
            disp.at[block_rows(c, dy)], rows.at[x, block_rows(c, dy)],
            disp_send.at[c], disp_recv.at[c], dev(zz, lax.rem(y + dy, ny)), x,
        )

    def dispatch(c):
        pick = jnp.where(chosen(spread(c)), 1.0, 0.0).astype(bf16)
        block = jnp.dot(pick, tok_ref[...], preferred_element_type=f32).astype(bf16)
        disp[chunk_rows(c), :] = block
        for dy in range(1, ny):
            disp_copy(c, dy).start()

        @pl.when(c < nz - 1)
        def _():
            disp_copy(c, 0).start()

        @pl.when(c == nz - 1)
        def _():
            rows[x, block_rows(c, 0), :] = block[:SLOTS, :]

    ahead = min(2, nz)
    lat_copy.start()
    dispatch(0)
    for copy in to_side:
        copy.start()
    for c in range(1, ahead):
        dispatch(c)
    for copy in to_mate:
        copy.start()

    def head(h, carry):
        scores = jnp.dot(keys[...], query[h], preferred_element_type=f32) * score_scale + bias[...]
        lifted = jnp.exp(scores - jnp.max(scores, axis=0, keepdims=True))
        probs = (lifted / jnp.sum(lifted, axis=0, keepdims=True)).astype(bf16)
        attn[h] = lax.dot_general(
            probs, keys[:, :LAT], (((0,), (0,)), ((), ())), preferred_element_type=f32
        ).astype(bf16)
        return carry

    def first_half(c):
        return pl.ds(pl.multiple_of(c * chunk, chunk), half)

    def second_half(c):
        return pl.ds(pl.multiple_of(c * chunk + half, half), half)

    def x_copies(c):
        here = rows.at[x, chunk_rows(c)]
        return (
            remote(here, here, x_send.at[0, c], x_recv.at[0, c], d, right),
            remote(here, here, x_send.at[1, c], x_recv.at[1, c], d, left),
        )

    def x_relays(c):
        from_left, from_right = rows.at[left, first_half(c)], rows.at[right, second_half(c)]
        return (
            remote(from_left, from_left, x_send.at[2, c], x_recv.at[2, c], d, right),
            remote(from_right, from_right, x_send.at[3, c], x_recv.at[3, c], d, left),
        )

    def h_copies(c):
        here = hid.at[chunk_rows(c), unit_cols(x)]
        return (
            remote(here, here, h_send.at[0, c], h_recv.at[0, c], d, right),
            remote(here, here, h_send.at[1, c], h_recv.at[1, c], d, left),
        )

    def h_relays(c):
        from_left = hid.at[first_half(c), unit_cols(left)]
        from_right = hid.at[second_half(c), unit_cols(right)]
        return (
            remote(from_left, from_left, h_send.at[2, c], h_recv.at[2, c], d, right),
            remote(from_right, from_right, h_send.at[3, c], h_recv.at[3, c], d, left),
        )

    def ret_copy(c, dy):
        zz = lax.rem(z - offset(c) + nz, nz)
        return remote(
            outb.at[block_rows(c, dy)], ret.at[block_rows(c, dy)],
            ret_send.at[c], ret_recv.at[c], dev(zz, lax.rem(y - dy + ny, ny)), x,
        )

    def stage_arrive(c):
        @pl.when(c < nz - 1)
        def _():
            wait_in(rows.at[x, chunk_rows(c)], disp_recv.at[c])

        @pl.when(c == nz - 1)
        def _():
            wait_in(rows.at[x, pl.ds((nz - 1) * chunk, chunk - SLOTS)], disp_recv.at[c])

        for copy in x_copies(c):
            copy.start()

    def stage_relay(c):
        wait_in(rows.at[left, chunk_rows(c)], x_recv.at[0, c])
        wait_in(rows.at[right, chunk_rows(c)], x_recv.at[1, c])
        for copy in x_relays(c):
            copy.start()

    def stage_up(c):
        wait_in(rows.at[opposite, first_half(c)], x_recv.at[2, c])
        wait_in(rows.at[opposite, second_half(c)], x_recv.at[3, c])
        total = jnp.zeros((chunk, 2 * units), f32)
        for m in range(NX):
            total = total + jnp.dot(
                rows[m, chunk_rows(c), :], gu[m * width : (m + 1) * width, :],
                preferred_element_type=f32,
            )
        gate, upper = total[:, :units], total[:, units:]
        hid[chunk_rows(c), unit_cols(x)] = (gate / (1.0 + jnp.exp(-gate)) * upper).astype(bf16)
        for copy in h_copies(c):
            copy.start()

    def stage_hid(c):
        wait_in(hid.at[chunk_rows(c), unit_cols(left)], h_recv.at[0, c])
        wait_in(hid.at[chunk_rows(c), unit_cols(right)], h_recv.at[1, c])
        for copy in h_relays(c):
            copy.start()

    def stage_down(c):
        wait_in(hid.at[first_half(c), unit_cols(opposite)], h_recv.at[2, c])
        wait_in(hid.at[second_half(c), unit_cols(opposite)], h_recv.at[3, c])
        result = jnp.dot(hid[chunk_rows(c), :], dn[...], preferred_element_type=f32).astype(bf16)
        outb[chunk_rows(c), :] = result
        for dy in range(1, ny):
            ret_copy(c, dy).start()

        @pl.when(c < nz - 1)
        def _():
            ret_copy(c, 0).start()

        @pl.when(c == nz - 1)
        def _():
            ret[block_rows(c, 0), :] = result[:SLOTS, :]

    def stage_combine(c):
        @pl.when(c < nz - 1)
        def _():
            wait_in(ret.at[chunk_rows(c)], ret_recv.at[c])

        @pl.when(c == nz - 1)
        def _():
            wait_in(ret.at[pl.ds((nz - 1) * chunk + SLOTS, chunk - SLOTS)], ret_recv.at[c])

        sel = spread(c)
        taken = chosen(sel)
        back = ret[chunk_rows(c), :]
        total = acc[...]
        for part in (ghi_ref, glo_ref):
            scale = jnp.dot(sel, part[...], preferred_element_type=f32)
            scale = jnp.where(taken, scale, 0.0).astype(bf16)
            total = total + lax.dot_general(
                scale, back, (((0,), (0,)), ((), ())), preferred_element_type=f32
            )
        acc[...] = total

    acc[...] = jnp.zeros_like(acc)

    parts = min(4, nz)
    attn_copy = pltpu.make_async_copy(attn, attn_ref, q_sem.at[1])

    def step(t, carry):
        def at(delay, stage):
            @pl.when((t >= delay) & (t < delay + nz))
            def _():
                stage(t - delay)

        at(0, stage_arrive)

        @pl.when((t == 0) & (ahead < nz))
        def _():
            dispatch(ahead)

        @pl.when(t + ahead + 1 < nz)
        def _():
            dispatch(t + ahead + 1)

        at(2, stage_relay)

        @pl.when(t == 1)
        def _():
            wait_in(relay_dn.at[0], w_recv.at[4])
            wait_in(relay_dn.at[1], w_recv.at[5])
            for copy in relays:
                copy.start()

        @pl.when(t == 0)
        def _():
            local_query.wait()
            wait_in(keys.at[pl.ds(0, tokens)], lat_recv.at[0])

        @pl.when(t < parts)
        def _():
            lax.fori_loop(t * (heads // parts), (t + 1) * (heads // parts), head, 0)

        @pl.when(t == parts)
        def _():
            attn_copy.start()

        @pl.when(t == 3)
        def _():
            local_gate.wait()
            local_up.wait()
            wait_in(gu.at[mate_in, gate_cols], w_recv.at[0])
            wait_in(gu.at[mate_in, up_cols], w_recv.at[1])

        at(4, stage_hid)
        at(3, stage_up)

        @pl.when(t == 3)
        def _():
            local_down.wait()
            wait_in(dn.at[unit_rows(left, 0, units), own_out], w_recv.at[2])
            wait_in(dn.at[unit_rows(right, 0, units), own_out], w_recv.at[3])
            wait_in(dn.at[unit_rows(opposite, 0, halfu), own_out], w_recv.at[6])
            wait_in(dn.at[unit_rows(opposite, halfu, halfu), own_out], w_recv.at[7])
            down_to_mate.start()

        @pl.when(t == 5)
        def _():
            wait_in(dn.at[:, mate_out], w_recv.at[8])

        at(5, stage_down)
        at(7, stage_combine)
        return carry

    lax.fori_loop(0, nz + 7, step, 0)
    out_ref[...] = acc[...].astype(out_ref.dtype)

    attn_copy.wait()
    lat_copy.wait_send()
    for copy in to_side + to_mate + relays + [down_to_mate]:
        copy.wait_send()

    def drain(c, carry):
        for copy in x_copies(c) + x_relays(c) + h_copies(c) + h_relays(c):
            copy.wait_send()

        @pl.when(c < nz - 1)
        def _():
            wait_in(disp.at[chunk_rows(c)], disp_send.at[c])
            wait_in(outb.at[chunk_rows(c)], ret_send.at[c])

        @pl.when(c == nz - 1)
        def _():
            rest = pl.ds((nz - 1) * chunk + SLOTS, chunk - SLOTS)
            wait_in(disp.at[rest], disp_send.at[c])
            wait_in(outb.at[rest], ret_send.at[c])

        return carry

    lax.fori_loop(0, nz, drain, 0)


def layer(nz, ny, ids, scores, tok, gate, up, down, query, latent, docs):
    tokens, width = tok.shape
    units = gate.shape[1]
    piece = down.shape[1] // NX
    experts = nz * ny
    count = experts * SLOTS
    heads, feats, _ = query.shape
    vmem = pl.BlockSpec(memory_space=pltpu.VMEM)
    away = pl.BlockSpec(memory_space=pl.ANY)
    bf16 = jnp.bfloat16
    dma = pltpu.SemaphoreType.DMA
    return pl.pallas_call(
        functools.partial(layer_kernel, nz, ny),
        out_shape=(
            jax.ShapeDtypeStruct((tokens, width), bf16),
            jax.ShapeDtypeStruct((heads, tokens, LAT), bf16),
        ),
        in_specs=[vmem, vmem, vmem, away, away, away, away, vmem, vmem],
        out_specs=(vmem, away),
        scratch_shapes=[
            pltpu.VMEM((count, width), bf16),
            pltpu.VMEM((NX, count, width), bf16),
            pltpu.VMEM((NX * width, 2 * units), bf16),
            pltpu.VMEM((NX * units, width), bf16),
            pltpu.VMEM((2, units // 2, piece), bf16),
            pltpu.VMEM((count, NX * units), bf16),
            pltpu.VMEM((count, width), bf16),
            pltpu.VMEM((count, width), bf16),
            pltpu.VMEM((tokens, width), jnp.float32),
            pltpu.VMEM((experts, tokens), bf16),
            pltpu.VMEM((experts, tokens), bf16),
            pltpu.VMEM((experts, tokens), bf16),
            pltpu.VMEM((heads, feats, tokens), bf16),
            pltpu.VMEM((heads, tokens, LAT), bf16),
            pltpu.VMEM((2 * tokens, feats), bf16),
            pltpu.VMEM((2 * tokens, tokens), jnp.float32),
            dma((3,)),
            dma((2,)),
            dma((1,)),
            dma((1,)),
            dma((9,)),
            dma((9,)),
            dma((nz,)),
            dma((nz,)),
            dma((4, nz)),
            dma((4, nz)),
            dma((4, nz)),
            dma((4, nz)),
            dma((nz,)),
            dma((nz,)),
        ],
        compiler_params=pltpu.CompilerParams(
            collective_id=0, has_side_effects=True, vmem_limit_bytes=58 * 1024 * 1024
        ),
        name="layer",
    )(ids, scores, tok, gate, up, down, query, latent, docs)


def shards(
    queries,
    latents,
    doc_ids,
    hidden_rows,
    expert_ids,
    gate_scores,
    gate_weight,
    up_weight,
    down_weight,
):
    length = lax.axis_size("dp")
    moe_out, heads_out = layer(
        length // (2 * NY),
        NY,
        expert_ids.T,
        gate_scores.T,
        hidden_rows,
        gate_weight[0],
        up_weight[0],
        down_weight[0],
        queries.transpose(1, 2, 0),
        latents.T,
        doc_ids.reshape(length, -1),
    )
    return (heads_out.transpose(1, 0, 2), moe_out)


def solution(mesh):
    placed = (
        P("dp", "mp", None),
        P("dp", None),
        P(),
        P("dp", "mp"),
        P("dp", None),
        P("dp", None),
        P("dp", None, "mp"),
        P("dp", None, "mp"),
        P("dp", "mp", None),
    )
    return jax.shard_map(
        shards,
        mesh=mesh,
        in_specs=placed,
        out_specs=(P("dp", "mp", None), P("dp", "mp")),
        check_vma=False,
    )
```

```python
import functools
import math

import jax
import jax.numpy as jnp
from jax import lax
from jax.experimental import pallas as pl
from jax.experimental.pallas import tpu as pltpu
from jax.sharding import PartitionSpec as P

LAT = 512
LANES = 128
SLOTS = 32
NX = 4
NY = 4
Z_ORDER = {8: (-2, 3, -3, 4, 2, 1, -1, 0), 4: (1, 2, -1, 0), 2: (1, 0)}

score_scale = 1.0 / math.sqrt(192.0)
neg_large = -1e30
MESH = pl.DeviceIdType.MESH


def layer_kernel(
    nz,
    ny,
    ids_ref,
    score_ref,
    tok_ref,
    gate_ref,
    up_ref,
    down_ref,
    query_ref,
    latent_ref,
    doc_ref,
    out_ref,
    attn_ref,
    disp,
    rows,
    gu,
    dn,
    relay_dn,
    hid,
    outb,
    ret,
    acc,
    place_ref,
    ghi_ref,
    glo_ref,
    query,
    wide,
    attn,
    keys,
    bias,
    local_sem,
    q_sem,
    lat_send,
    lat_recv,
    w_send,
    w_recv,
    disp_send,
    disp_recv,
    x_send,
    x_recv,
    h_send,
    h_recv,
    ret_send,
    ret_recv,
):
    top, tokens = ids_ref.shape
    heads = query_ref.shape[0]
    width = tok_ref.shape[1]
    half_in, units = gate_ref.shape
    piece = down_ref.shape[1] // NX
    experts = nz * ny
    chunk = ny * SLOTS
    half = chunk // 2
    f32, bf16 = jnp.float32, jnp.bfloat16

    d = lax.axis_index("dp")
    x = lax.axis_index("mp")
    s = lax.rem(d, 2)
    p = lax.div(d, 2)
    z = lax.div(p, ny)
    y = lax.rem(p, ny)
    right = lax.rem(x + 1, NX)
    left = lax.rem(x + NX - 1, NX)
    opposite = lax.rem(x + 2, NX)
    mate = d + 1 - 2 * s

    def dev(zz, yy):
        return (zz * ny + yy) * 2 + s

    def offset(c):
        total = 0
        for at, by in enumerate(Z_ORDER[nz]):
            total = total + jnp.where(c == at, by, 0)
        return total

    def remote(src, dst, send, recv, dd, xx):
        return pltpu.make_async_remote_copy(
            src_ref=src, dst_ref=dst, send_sem=send, recv_sem=recv,
            device_id=(dd, xx), device_id_type=MESH,
        )

    def wait_in(ref, sem):
        pltpu.make_async_copy(ref, ref, sem).wait()

    own_in = pl.ds(pl.multiple_of(s * half_in, half_in), half_in)
    mate_in = pl.ds(pl.multiple_of((1 - s) * half_in, half_in), half_in)
    own_out = pl.ds(pl.multiple_of(s * piece, piece), piece)
    mate_out = pl.ds(pl.multiple_of((1 - s) * piece, piece), piece)
    gate_cols, up_cols = pl.ds(0, units), pl.ds(units, units)

    def unit_rows(q, start, count):
        return pl.ds(pl.multiple_of(q * units + start, units // 2), count)

    def unit_cols(q):
        return pl.ds(pl.multiple_of(q * units, units), units)

    def down_cols(q):
        return pl.ds(pl.multiple_of(q * piece, piece), piece)

    local_gate = pltpu.make_async_copy(gate_ref, gu.at[own_in, gate_cols], local_sem.at[0])
    local_up = pltpu.make_async_copy(up_ref, gu.at[own_in, up_cols], local_sem.at[1])
    local_down = pltpu.make_async_copy(
        down_ref.at[:, down_cols(x)], dn.at[unit_rows(x, 0, units), own_out], local_sem.at[2]
    )
    local_gate.start()
    local_up.start()
    local_down.start()
    local_query = pltpu.make_async_copy(query_ref, query, q_sem.at[0])
    local_query.start()

    barrier = pltpu.get_barrier_semaphore()

    def greet(dd, xx):
        pl.semaphore_signal(barrier, inc=1, device_id=(dd, xx), device_id_type=MESH)

    ring = experts * 2
    beside = lax.rem(d + 2 * s - 1 + ring, ring)
    following = lax.rem(d + 1, ring)
    greet(mate, x)
    greet(beside, x)
    greet(d, right)
    greet(d, left)

    def greet_peer(k, carry):
        greet(lax.rem(p + k, experts) * 2 + s, x)
        return carry

    lax.fori_loop(1, experts, greet_peer, 0)

    expert_at = lax.broadcasted_iota(jnp.int32, (experts, tokens), 0)
    named = jnp.zeros((experts, tokens), f32)
    weight = jnp.zeros((experts, tokens), f32)
    for k in range(top):
        hit = ids_ref[k : k + 1, :] == expert_at
        named = named + jnp.where(hit, 1.0, 0.0)
        weight = weight + jnp.where(hit, score_ref[k : k + 1, :], 0.0)
    row_at = lax.broadcasted_iota(jnp.int32, (tokens, tokens), 0)
    col_at = lax.broadcasted_iota(jnp.int32, (tokens, tokens), 1)
    before = jnp.dot(
        named.astype(bf16),
        jnp.where(row_at < col_at, 1.0, 0.0).astype(bf16),
        preferred_element_type=f32,
    )
    place_ref[...] = jnp.where(named > 0.5, before, -1.0).astype(bf16)
    whole = weight.astype(bf16)
    ghi_ref[...] = whole
    glo_ref[...] = (weight - whole.astype(f32)).astype(bf16)

    same = row_at == col_at
    keys[tokens:, :] = lax.dot_general(
        jnp.where(same, 1.0, 0.0).astype(bf16), latent_ref[...], (((1,), (1,)), ((), ())),
        preferred_element_type=f32,
    ).astype(bf16)
    lat_copy = remote(
        keys.at[pl.ds(tokens, tokens)], keys.at[pl.ds(0, tokens)],
        lat_send.at[0], lat_recv.at[0], following, x,
    )
    own_ids = doc_ref[pl.ds(d, 1), :]
    old_ids = doc_ref[pl.ds(lax.rem(d + ring - 1, ring), 1), :]
    own_col = jnp.sum(jnp.where(same, own_ids, 0).astype(f32), axis=1, keepdims=True)
    old_col = jnp.sum(jnp.where(same, old_ids, 0).astype(f32), axis=1, keepdims=True)
    old_col = old_col - jnp.where(d == 0, 1000.0, 0.0)
    ids_row = own_ids.astype(f32)
    bias[:tokens, :] = jnp.where(old_col == ids_row, 0.0, neg_large)
    bias[tokens:, :] = jnp.where((own_col == ids_row) & (row_at <= col_at), 0.0, neg_large)

    to_mate = [
        remote(gate_ref, gu.at[own_in, gate_cols], w_send.at[0], w_recv.at[0], mate, x),
        remote(up_ref, gu.at[own_in, up_cols], w_send.at[1], w_recv.at[1], mate, x),
    ]
    halfu = units // 2
    to_side = [
        remote(
            down_ref.at[:, down_cols(right)], dn.at[unit_rows(x, 0, units), own_out],
            w_send.at[2], w_recv.at[2], d, right,
        ),
        remote(
            down_ref.at[:, down_cols(left)], dn.at[unit_rows(x, 0, units), own_out],
            w_send.at[3], w_recv.at[3], d, left,
        ),
        remote(
            down_ref.at[pl.ds(0, halfu), down_cols(opposite)], relay_dn.at[0],
            w_send.at[4], w_recv.at[4], d, right,
        ),
        remote(
            down_ref.at[pl.ds(halfu, halfu), down_cols(opposite)], relay_dn.at[1],
            w_send.at[5], w_recv.at[5], d, left,
        ),
    ]
    relays = [
        remote(
            relay_dn.at[0], dn.at[unit_rows(left, 0, halfu), own_out],
            w_send.at[6], w_recv.at[6], d, right,
        ),
        remote(
            relay_dn.at[1], dn.at[unit_rows(right, halfu, halfu), own_out],
            w_send.at[7], w_recv.at[7], d, left,
        ),
    ]
    down_to_mate = remote(
        dn.at[:, own_out], dn.at[:, own_out], w_send.at[8], w_recv.at[8], mate, x
    )

    def chunk_rows(c):
        return pl.ds(pl.multiple_of(c * chunk, chunk), chunk)

    def block_rows(c, dy):
        return pl.ds(pl.multiple_of(c * chunk + dy * SLOTS, SLOTS), SLOTS)

    def spread(c):
        zz = lax.rem(z + offset(c) + nz, nz)
        row = lax.broadcasted_iota(jnp.int32, (chunk, experts), 0)
        dest = zz * ny + ((y + (row // SLOTS)) % ny)
        return jnp.where(
            lax.broadcasted_iota(jnp.int32, (chunk, experts), 1) == dest, 1.0, 0.0
        ).astype(bf16)

    def chosen(sel):
        slot = (lax.broadcasted_iota(jnp.int32, (chunk, tokens), 0) % SLOTS).astype(f32)
        return jnp.dot(sel, place_ref[...], preferred_element_type=f32) == slot

    def disp_copy(c, dy):
        zz = lax.rem(z + offset(c) + nz, nz)
        return remote(
            disp.at[block_rows(c, dy)], rows.at[x, block_rows(c, dy)],
            disp_send.at[c], disp_recv.at[c], dev(zz, lax.rem(y + dy, ny)), x,
        )

    def build(c):
        pick = jnp.where(chosen(spread(c)), 1.0, 0.0).astype(bf16)
        block = jnp.dot(pick, tok_ref[...], preferred_element_type=f32).astype(bf16)
        disp[chunk_rows(c), :] = block

    def dispatch(c):
        for dy in range(1, ny):
            disp_copy(c, dy).start()

        @pl.when(c < nz - 1)
        def _():
            disp_copy(c, 0).start()

        @pl.when(c == nz - 1)
        def _():
            rows[x, block_rows(c, 0), :] = disp[block_rows(c, 0), :]

    ahead = min(2, nz)
    for c in range(ahead):
        build(c)

    pl.semaphore_wait(barrier, experts - 1 + 4)

    for copy in to_side[:2]:
        copy.start()
    for c in range(ahead):
        dispatch(c)
    for copy in to_side[2:] + [lat_copy] + to_mate:
        copy.start()

    def head(h, carry):
        scores = jnp.dot(keys[...], query[h], preferred_element_type=f32) * score_scale + bias[...]
        lifted = jnp.exp(scores - jnp.max(scores, axis=0, keepdims=True))
        probs = (lifted / jnp.sum(lifted, axis=0, keepdims=True)).astype(bf16)
        value = lax.dot_general(
            probs, keys[:, :LAT], (((0,), (0,)), ((), ())), preferred_element_type=f32
        )
        for k in range(LAT // LANES):
            wide[k, pl.ds(h, tokens, stride=heads), :] = value[:, k * LANES : (k + 1) * LANES]
        return carry

    def first_half(c):
        return pl.ds(pl.multiple_of(c * chunk, chunk), half)

    def second_half(c):
        return pl.ds(pl.multiple_of(c * chunk + half, half), half)

    def x_copies(c):
        here = rows.at[x, chunk_rows(c)]
        return (
            remote(here, here, x_send.at[0, c], x_recv.at[0, c], d, right),
            remote(here, here, x_send.at[1, c], x_recv.at[1, c], d, left),
        )

    def x_relays(c):
        from_left, from_right = rows.at[left, first_half(c)], rows.at[right, second_half(c)]
        return (
            remote(from_left, from_left, x_send.at[2, c], x_recv.at[2, c], d, right),
            remote(from_right, from_right, x_send.at[3, c], x_recv.at[3, c], d, left),
        )

    def h_copies(c):
        here = hid.at[chunk_rows(c), unit_cols(x)]
        return (
            remote(here, here, h_send.at[0, c], h_recv.at[0, c], d, right),
            remote(here, here, h_send.at[1, c], h_recv.at[1, c], d, left),
        )

    def h_relays(c):
        from_left = hid.at[first_half(c), unit_cols(left)]
        from_right = hid.at[second_half(c), unit_cols(right)]
        return (
            remote(from_left, from_left, h_send.at[2, c], h_recv.at[2, c], d, right),
            remote(from_right, from_right, h_send.at[3, c], h_recv.at[3, c], d, left),
        )

    def ret_copy(c, dy):
        zz = lax.rem(z - offset(c) + nz, nz)
        return remote(
            outb.at[block_rows(c, dy)], ret.at[block_rows(c, dy)],
            ret_send.at[c], ret_recv.at[c], dev(zz, lax.rem(y - dy + ny, ny)), x,
        )

    def stage_arrive(c):
        @pl.when(c < nz - 1)
        def _():
            wait_in(rows.at[x, chunk_rows(c)], disp_recv.at[c])

        @pl.when(c == nz - 1)
        def _():
            wait_in(rows.at[x, pl.ds((nz - 1) * chunk, chunk - SLOTS)], disp_recv.at[c])

        for copy in x_copies(c):
            copy.start()

    def stage_relay(c):
        wait_in(rows.at[left, chunk_rows(c)], x_recv.at[0, c])
        wait_in(rows.at[right, chunk_rows(c)], x_recv.at[1, c])
        for copy in x_relays(c):
            copy.start()

    def stage_up(c):
        wait_in(rows.at[opposite, first_half(c)], x_recv.at[2, c])
        wait_in(rows.at[opposite, second_half(c)], x_recv.at[3, c])
        total = jnp.zeros((chunk, 2 * units), f32)
        for m in range(NX):
            total = total + jnp.dot(
                rows[m, chunk_rows(c), :], gu[m * width : (m + 1) * width, :],
                preferred_element_type=f32,
            )
        gate, upper = total[:, :units], total[:, units:]
        hid[chunk_rows(c), unit_cols(x)] = (gate / (1.0 + jnp.exp(-gate)) * upper).astype(bf16)
        for copy in h_copies(c):
            copy.start()

    def stage_hid(c):
        wait_in(hid.at[chunk_rows(c), unit_cols(left)], h_recv.at[0, c])
        wait_in(hid.at[chunk_rows(c), unit_cols(right)], h_recv.at[1, c])
        for copy in h_relays(c):
            copy.start()

    def stage_down(c):
        wait_in(hid.at[first_half(c), unit_cols(opposite)], h_recv.at[2, c])
        wait_in(hid.at[second_half(c), unit_cols(opposite)], h_recv.at[3, c])
        result = jnp.dot(hid[chunk_rows(c), :], dn[...], preferred_element_type=f32).astype(bf16)
        outb[chunk_rows(c), :] = result
        for dy in range(1, ny):
            ret_copy(c, dy).start()

        @pl.when(c < nz - 1)
        def _():
            ret_copy(c, 0).start()

        @pl.when(c == nz - 1)
        def _():
            ret[block_rows(c, 0), :] = result[:SLOTS, :]

    def stage_combine(c):
        @pl.when(c < nz - 1)
        def _():
            wait_in(ret.at[chunk_rows(c)], ret_recv.at[c])

        @pl.when(c == nz - 1)
        def _():
            wait_in(ret.at[pl.ds((nz - 1) * chunk + SLOTS, chunk - SLOTS)], ret_recv.at[c])

        sel = spread(c)
        taken = chosen(sel)
        back = ret[chunk_rows(c), :]
        total = acc[...]
        for part in (ghi_ref, glo_ref):
            scale = jnp.dot(sel, part[...], preferred_element_type=f32)
            scale = jnp.where(taken, scale, 0.0).astype(bf16)
            total = total + lax.dot_general(
                scale, back, (((0,), (0,)), ((), ())), preferred_element_type=f32
            )
        acc[...] = total

    acc[...] = jnp.zeros_like(acc)

    parts = min(4, nz)
    attn_copy = pltpu.make_async_copy(attn, attn_ref, q_sem.at[1])

    def step(t, carry):
        def at(delay, stage, count=nz):
            @pl.when((t >= delay) & (t < delay + count))
            def _():
                stage(t - delay)

        at(1, stage_relay)
        at(0, stage_arrive)

        @pl.when((t == 0) & (ahead < nz))
        def _():
            build(ahead)
            dispatch(ahead)

        @pl.when(t + ahead + 1 < nz)
        def _():
            build(t + ahead + 1)
            dispatch(t + ahead + 1)

        @pl.when(t == 1)
        def _():
            wait_in(relay_dn.at[0], w_recv.at[4])
            wait_in(relay_dn.at[1], w_recv.at[5])
            for copy in relays:
                copy.start()

        @pl.when(t == 0)
        def _():
            local_query.wait()
            wait_in(keys.at[pl.ds(0, tokens)], lat_recv.at[0])

        @pl.when(t < parts)
        def _():
            lax.fori_loop(t * (heads // parts), (t + 1) * (heads // parts), head, 0)

        @pl.when(t == parts)
        def _():
            def narrow(i, carry):
                some = pl.ds(pl.multiple_of(i * tokens, tokens), tokens)
                for k in range(LAT // LANES):
                    attn[some, k * LANES : (k + 1) * LANES] = wide[k, some, :].astype(bf16)
                return carry

            lax.fori_loop(0, heads, narrow, 0)
            attn_copy.start()

        at(2, stage_hid)

        @pl.when(t == 1)
        def _():
            local_gate.wait()
            local_up.wait()
            wait_in(gu.at[mate_in, gate_cols], w_recv.at[0])
            wait_in(gu.at[mate_in, up_cols], w_recv.at[1])

        at(1, stage_up)

        @pl.when(t == 2)
        def _():
            local_down.wait()
            wait_in(dn.at[unit_rows(left, 0, units), own_out], w_recv.at[2])
            wait_in(dn.at[unit_rows(right, 0, units), own_out], w_recv.at[3])
            wait_in(dn.at[unit_rows(opposite, 0, halfu), own_out], w_recv.at[6])
            wait_in(dn.at[unit_rows(opposite, halfu, halfu), own_out], w_recv.at[7])
            down_to_mate.start()

        @pl.when(t == 3)
        def _():
            wait_in(dn.at[:, mate_out], w_recv.at[8])

        at(3, stage_down)
        at(6, stage_combine, early)
        return carry

    early = min(3, nz - 1)
    lax.fori_loop(0, nz + 3, step, 0)

    def finish(c, carry):
        stage_combine(c)
        return carry

    lax.fori_loop(early, nz, finish, 0)
    out_ref[...] = acc[...].astype(out_ref.dtype)

    attn_copy.wait()
    lat_copy.wait_send()
    for copy in to_side + to_mate + relays + [down_to_mate]:
        copy.wait_send()

    def drain(c, carry):
        for copy in x_copies(c) + x_relays(c) + h_copies(c) + h_relays(c):
            copy.wait_send()

        @pl.when(c < nz - 1)
        def _():
            wait_in(disp.at[chunk_rows(c)], disp_send.at[c])
            wait_in(outb.at[chunk_rows(c)], ret_send.at[c])

        @pl.when(c == nz - 1)
        def _():
            rest = pl.ds((nz - 1) * chunk + SLOTS, chunk - SLOTS)
            wait_in(disp.at[rest], disp_send.at[c])
            wait_in(outb.at[rest], ret_send.at[c])

        return carry

    lax.fori_loop(0, nz, drain, 0)


def layer(nz, ny, ids, scores, tok, gate, up, down, query, latent, docs):
    tokens, width = tok.shape
    units = gate.shape[1]
    piece = down.shape[1] // NX
    experts = nz * ny
    count = experts * SLOTS
    heads, feats, _ = query.shape
    vmem = pl.BlockSpec(memory_space=pltpu.VMEM)
    away = pl.BlockSpec(memory_space=pl.ANY)
    bf16 = jnp.bfloat16
    dma = pltpu.SemaphoreType.DMA
    return pl.pallas_call(
        functools.partial(layer_kernel, nz, ny),
        out_shape=(
            jax.ShapeDtypeStruct((tokens, width), bf16),
            jax.ShapeDtypeStruct((tokens * heads, LAT), bf16),
        ),
        in_specs=[vmem, vmem, vmem, away, away, away, away, vmem, vmem],
        out_specs=(vmem, away),
        scratch_shapes=[
            pltpu.VMEM((count, width), bf16),
            pltpu.VMEM((NX, count, width), bf16),
            pltpu.VMEM((NX * width, 2 * units), bf16),
            pltpu.VMEM((NX * units, width), bf16),
            pltpu.VMEM((2, units // 2, piece), bf16),
            pltpu.VMEM((count, NX * units), bf16),
            pltpu.VMEM((count, width), bf16),
            pltpu.VMEM((count, width), bf16),
            pltpu.VMEM((tokens, width), jnp.float32),
            pltpu.VMEM((experts, tokens), bf16),
            pltpu.VMEM((experts, tokens), bf16),
            pltpu.VMEM((experts, tokens), bf16),
            pltpu.VMEM((heads, feats, tokens), bf16),
            pltpu.VMEM((LAT // LANES, tokens * heads, LANES), jnp.float32),
            pltpu.VMEM((tokens * heads, LAT), bf16),
            pltpu.VMEM((2 * tokens, feats), bf16),
            pltpu.VMEM((2 * tokens, tokens), jnp.float32),
            dma((3,)),
            dma((2,)),
            dma((1,)),
            dma((1,)),
            dma((9,)),
            dma((9,)),
            dma((nz,)),
            dma((nz,)),
            dma((4, nz)),
            dma((4, nz)),
            dma((4, nz)),
            dma((4, nz)),
            dma((nz,)),
            dma((nz,)),
        ],
        compiler_params=pltpu.CompilerParams(
            collective_id=0, has_side_effects=True, vmem_limit_bytes=58 * 1024 * 1024
        ),
        name="layer",
    )(ids, scores, tok, gate, up, down, query, latent, docs)


def shards(
    queries,
    latents,
    doc_ids,
    hidden_rows,
    expert_ids,
    gate_scores,
    gate_weight,
    up_weight,
    down_weight,
):
    length = lax.axis_size("dp")
    moe_out, attn_out = layer(
        length // (2 * NY),
        NY,
        expert_ids.T,
        gate_scores.T,
        hidden_rows,
        gate_weight[0],
        up_weight[0],
        down_weight[0],
        queries.transpose(1, 2, 0),
        latents.T,
        doc_ids.reshape(length, -1),
    )
    return (attn_out.reshape(queries.shape[:2] + (LAT,)), moe_out)


def solution(mesh):
    placed = (
        P("dp", "mp", None),
        P("dp", None),
        P(),
        P("dp", "mp"),
        P("dp", None),
        P("dp", None),
        P("dp", None, "mp"),
        P("dp", None, "mp"),
        P("dp", "mp", None),
    )
    return jax.shard_map(
        shards,
        mesh=mesh,
        in_specs=placed,
        out_specs=(P("dp", "mp", None), P("dp", "mp")),
        check_vma=False,
    )
```

```python
import functools
import math

import jax
import jax.numpy as jnp
from jax import lax
from jax.experimental import pallas as pl
from jax.experimental.pallas import tpu as pltpu
from jax.sharding import PartitionSpec as P

LAT = 512
LANES = 128
SLOTS = 32
CAP = 30
CHUNK = 64
NX = 4
NY = 4
Z_ORDER = {8: (0, -2, 4, 3, -3, 2, 1, -1), 4: (0, 2, 1, -1), 2: (0, 1)}

score_scale = 1.0 / math.sqrt(192.0)
neg_large = -1e30
MESH = pl.DeviceIdType.MESH


def layer_kernel(
    nz,
    ny,
    ids_ref,
    score_ref,
    tok_ref,
    gate_ref,
    up_ref,
    down_ref,
    query_ref,
    latent_ref,
    doc_ref,
    out_ref,
    attn_ref,
    disp,
    land,
    rows,
    gu,
    dn,
    relay_dn,
    hid,
    outb,
    ret,
    acc,
    place_ref,
    ghi_ref,
    glo_ref,
    query,
    wide,
    attn,
    keys,
    bias,
    local_sem,
    q_sem,
    lat_send,
    lat_recv,
    w_send,
    w_recv,
    disp_send,
    disp_recv,
    x_send,
    x_recv,
    h_send,
    h_recv,
    ret_send,
    ret_recv,
):
    top, tokens = ids_ref.shape
    heads = query_ref.shape[0]
    width = tok_ref.shape[1]
    half_in, units = gate_ref.shape
    piece = down_ref.shape[1] // NX
    experts = nz * ny
    plane = ny * SLOTS
    chunk, half = CHUNK, CHUNK // 2
    per = CHUNK // SLOTS
    sent, packed = experts * SLOTS // chunk, experts * CAP // chunk
    own_chunk = Z_ORDER[nz].index(0) * (plane // chunk)
    f32, bf16 = jnp.float32, jnp.bfloat16

    d = lax.axis_index("dp")
    x = lax.axis_index("mp")
    s = lax.rem(d, 2)
    p = lax.div(d, 2)
    z = lax.div(p, ny)
    y = lax.rem(p, ny)
    right = lax.rem(x + 1, NX)
    left = lax.rem(x + NX - 1, NX)
    opposite = lax.rem(x + 2, NX)
    mate = d + 1 - 2 * s

    def dev(zz, yy):
        return (zz * ny + yy) * 2 + s

    def offset(c):
        total = 0
        for at, by in enumerate(Z_ORDER[nz]):
            total = total + jnp.where(c == at, by, 0)
        return total

    def remote(src, dst, send, recv, dd, xx):
        return pltpu.make_async_remote_copy(
            src_ref=src, dst_ref=dst, send_sem=send, recv_sem=recv,
            device_id=(dd, xx), device_id_type=MESH,
        )

    def wait_in(ref, sem):
        pltpu.make_async_copy(ref, ref, sem).wait()

    own_in = pl.ds(pl.multiple_of(s * half_in, half_in), half_in)
    mate_in = pl.ds(pl.multiple_of((1 - s) * half_in, half_in), half_in)
    own_out = pl.ds(pl.multiple_of(s * piece, piece), piece)
    mate_out = pl.ds(pl.multiple_of((1 - s) * piece, piece), piece)
    gate_cols, up_cols = pl.ds(0, units), pl.ds(units, units)

    def unit_rows(q, start, count):
        return pl.ds(pl.multiple_of(q * units + start, units // 2), count)

    def unit_cols(q):
        return pl.ds(pl.multiple_of(q * units, units), units)

    def down_cols(q):
        return pl.ds(pl.multiple_of(q * piece, piece), piece)

    local_gate = pltpu.make_async_copy(gate_ref, gu.at[own_in, gate_cols], local_sem.at[0])
    local_up = pltpu.make_async_copy(up_ref, gu.at[own_in, up_cols], local_sem.at[1])
    local_down = pltpu.make_async_copy(
        down_ref.at[:, down_cols(x)], dn.at[unit_rows(x, 0, units), own_out], local_sem.at[2]
    )
    local_gate.start()
    local_up.start()
    local_down.start()
    local_query = pltpu.make_async_copy(query_ref, query, q_sem.at[0])
    local_query.start()

    barrier = pltpu.get_barrier_semaphore()

    def greet(dd, xx):
        pl.semaphore_signal(barrier, inc=1, device_id=(dd, xx), device_id_type=MESH)

    ring = experts * 2
    beside = lax.rem(d + 2 * s - 1 + ring, ring)
    following = lax.rem(d + 1, ring)
    greet(mate, x)
    greet(beside, x)
    greet(d, right)
    greet(d, left)

    def greet_peer(k, carry):
        greet(lax.rem(p + k, experts) * 2 + s, x)
        return carry

    lax.fori_loop(1, experts, greet_peer, 0)

    expert_at = lax.broadcasted_iota(jnp.int32, (experts, tokens), 0)
    named = jnp.zeros((experts, tokens), f32)
    weight = jnp.zeros((experts, tokens), f32)
    for k in range(top):
        hit = ids_ref[k : k + 1, :] == expert_at
        named = named + jnp.where(hit, 1.0, 0.0)
        weight = weight + jnp.where(hit, score_ref[k : k + 1, :], 0.0)
    row_at = lax.broadcasted_iota(jnp.int32, (tokens, tokens), 0)
    col_at = lax.broadcasted_iota(jnp.int32, (tokens, tokens), 1)
    before = jnp.dot(
        named.astype(bf16),
        jnp.where(row_at < col_at, 1.0, 0.0).astype(bf16),
        preferred_element_type=f32,
    )
    place_ref[...] = jnp.where(named > 0.5, before, -1.0).astype(bf16)
    whole = weight.astype(bf16)
    ghi_ref[...] = whole
    glo_ref[...] = (weight - whole.astype(f32)).astype(bf16)

    same = row_at == col_at
    keys[tokens:, :] = lax.dot_general(
        jnp.where(same, 1.0, 0.0).astype(bf16), latent_ref[...], (((1,), (1,)), ((), ())),
        preferred_element_type=f32,
    ).astype(bf16)
    lat_copy = remote(
        keys.at[pl.ds(tokens, tokens)], keys.at[pl.ds(0, tokens)],
        lat_send.at[0], lat_recv.at[0], following, x,
    )
    own_ids = doc_ref[pl.ds(d, 1), :]
    old_ids = doc_ref[pl.ds(lax.rem(d + ring - 1, ring), 1), :]
    own_col = jnp.sum(jnp.where(same, own_ids, 0).astype(f32), axis=1, keepdims=True)
    old_col = jnp.sum(jnp.where(same, old_ids, 0).astype(f32), axis=1, keepdims=True)
    old_col = old_col - jnp.where(d == 0, 1000.0, 0.0)
    ids_row = own_ids.astype(f32)
    bias[:tokens, :] = jnp.where(old_col == ids_row, 0.0, neg_large)
    bias[tokens:, :] = jnp.where((own_col == ids_row) & (row_at <= col_at), 0.0, neg_large)

    to_mate = [
        remote(gate_ref, gu.at[own_in, gate_cols], w_send.at[0], w_recv.at[0], mate, x),
        remote(up_ref, gu.at[own_in, up_cols], w_send.at[1], w_recv.at[1], mate, x),
    ]
    halfu = units // 2
    to_side = [
        remote(
            down_ref.at[:, down_cols(right)], dn.at[unit_rows(x, 0, units), own_out],
            w_send.at[2], w_recv.at[2], d, right,
        ),
        remote(
            down_ref.at[:, down_cols(left)], dn.at[unit_rows(x, 0, units), own_out],
            w_send.at[3], w_recv.at[3], d, left,
        ),
        remote(
            down_ref.at[pl.ds(0, halfu), down_cols(opposite)], relay_dn.at[0],
            w_send.at[4], w_recv.at[4], d, right,
        ),
        remote(
            down_ref.at[pl.ds(halfu, halfu), down_cols(opposite)], relay_dn.at[1],
            w_send.at[5], w_recv.at[5], d, left,
        ),
    ]
    relays = [
        remote(
            relay_dn.at[0], dn.at[unit_rows(left, 0, halfu), own_out],
            w_send.at[6], w_recv.at[6], d, right,
        ),
        remote(
            relay_dn.at[1], dn.at[unit_rows(right, halfu, halfu), own_out],
            w_send.at[7], w_recv.at[7], d, left,
        ),
    ]
    down_to_mate = remote(
        dn.at[:, own_out], dn.at[:, own_out], w_send.at[8], w_recv.at[8], mate, x
    )

    def chunk_rows(c):
        return pl.ds(pl.multiple_of(c * chunk, chunk), chunk)

    def block_rows(b):
        return pl.ds(pl.multiple_of(b * SLOTS, SLOTS), SLOTS)

    def peer(b, way):
        zz = lax.rem(z + way * offset(lax.div(b, ny)) + nz, nz)
        return dev(zz, lax.rem(y + way * lax.rem(b, ny) + ny, ny))

    def spread(at, first, count):
        zz = lax.rem(z + offset(at) + nz, nz)
        row = lax.broadcasted_iota(jnp.int32, (count, experts), 0)
        dest = zz * ny + ((y + first + (row // SLOTS)) % ny)
        return jnp.where(
            lax.broadcasted_iota(jnp.int32, (count, experts), 1) == dest, 1.0, 0.0
        ).astype(bf16)

    def chosen(sel):
        count = sel.shape[0]
        slot = (lax.broadcasted_iota(jnp.int32, (count, tokens), 0) % SLOTS).astype(f32)
        return jnp.dot(sel, place_ref[...], preferred_element_type=f32) == slot

    def build(c):
        first = c * per
        sel = spread(lax.div(first, ny), lax.rem(first, ny), chunk)
        pick = jnp.where(chosen(sel), 1.0, 0.0).astype(bf16)
        block = jnp.dot(pick, tok_ref[...], preferred_element_type=f32).astype(bf16)
        disp[chunk_rows(c), :] = block

    def disp_copy(c, i):
        b = c * per + i
        return remote(
            disp.at[block_rows(b)], land.at[block_rows(b)],
            disp_send.at[c], disp_recv.at[c], peer(b, 1), x,
        )

    def own_block(c):
        return pl.ds(pl.multiple_of(c * chunk, chunk), SLOTS)

    def other_blocks(c):
        return pl.ds(pl.multiple_of(c * chunk + SLOTS, SLOTS), chunk - SLOTS)

    def per_chunk(c, yes, no):
        pl.when(c == own_chunk)(yes)
        pl.when(c != own_chunk)(no)

    def dispatch(c):
        for i in range(1, per):
            disp_copy(c, i).start()

        def keep():
            land[own_block(c), :] = disp[own_block(c), :]

        per_chunk(c, keep, lambda: disp_copy(c, 0).start())

    ahead = min(6, sent)
    for c in range(2):
        build(jnp.int32(c))

    pl.semaphore_wait(barrier, experts - 1 + 4)

    for copy in to_side[:2]:
        copy.start()
    for c in range(ahead):
        if c >= 2:
            build(jnp.int32(c))
        dispatch(jnp.int32(c))
        if c == 1:
            for copy in to_side[2:] + [lat_copy] + to_mate:
                copy.start()

    def first_half(c):
        return pl.ds(pl.multiple_of(c * chunk, chunk), half)

    def second_half(c):
        return pl.ds(pl.multiple_of(c * chunk + half, half), half)

    def x_copies(c):
        here = rows.at[x, chunk_rows(c)]
        return (
            remote(here, here, x_send.at[0, c], x_recv.at[0, c], d, right),
            remote(here, here, x_send.at[1, c], x_recv.at[1, c], d, left),
        )

    def x_relays(c):
        from_left, from_right = rows.at[left, first_half(c)], rows.at[right, second_half(c)]
        return (
            remote(from_left, from_left, x_send.at[2, c], x_recv.at[2, c], d, right),
            remote(from_right, from_right, x_send.at[3, c], x_recv.at[3, c], d, left),
        )

    def h_copies(c):
        here = hid.at[chunk_rows(c + 1), unit_cols(x)]
        return (
            remote(here, here, h_send.at[0, c], h_recv.at[0, c], d, right),
            remote(here, here, h_send.at[1, c], h_recv.at[1, c], d, left),
        )

    def h_relays(c):
        from_left = hid.at[first_half(c + 1), unit_cols(left)]
        from_right = hid.at[second_half(c + 1), unit_cols(right)]
        return (
            remote(from_left, from_left, h_send.at[2, c], h_recv.at[2, c], d, right),
            remote(from_right, from_right, h_send.at[3, c], h_recv.at[3, c], d, left),
        )

    def ret_copy(c, i):
        b = c * per + i
        return remote(
            outb.at[block_rows(b)], ret.at[block_rows(b)],
            ret_send.at[c], ret_recv.at[c], peer(b, -1), x,
        )

    def arrived(c):
        per_chunk(
            c,
            lambda: wait_in(land.at[other_blocks(c)], disp_recv.at[c]),
            lambda: wait_in(land.at[chunk_rows(c)], disp_recv.at[c]),
        )

    def stage_pack(c):
        @pl.when(c == 0)
        def _():
            arrived(c)

        arrived(c + 1)
        row = lax.broadcasted_iota(jnp.int32, (chunk, 2 * chunk), 0)
        col = lax.broadcasted_iota(jnp.int32, (chunk, 2 * chunk), 1)
        take = col == row + (SLOTS - CAP) * ((row + c * chunk) // CAP)
        window = land[pl.ds(pl.multiple_of(c * chunk, chunk), 2 * chunk), :]
        rows[x, chunk_rows(c), :] = jnp.dot(
            jnp.where(take, 1.0, 0.0).astype(bf16), window, preferred_element_type=f32
        ).astype(bf16)
        for copy in x_copies(c):
            copy.start()

    def stage_relay(c):
        wait_in(rows.at[left, chunk_rows(c)], x_recv.at[0, c])
        wait_in(rows.at[right, chunk_rows(c)], x_recv.at[1, c])
        for copy in x_relays(c):
            copy.start()

    def stage_up(c):
        wait_in(rows.at[opposite, first_half(c)], x_recv.at[2, c])
        wait_in(rows.at[opposite, second_half(c)], x_recv.at[3, c])
        total = jnp.zeros((chunk, 2 * units), f32)
        for m in range(NX):
            total = total + jnp.dot(
                rows[m, chunk_rows(c), :], gu[m * width : (m + 1) * width, :],
                preferred_element_type=f32,
            )
        gate, upper = total[:, :units], total[:, units:]
        hid[chunk_rows(c + 1), unit_cols(x)] = (gate / (1.0 + jnp.exp(-gate)) * upper).astype(bf16)
        for copy in h_copies(c):
            copy.start()

    def stage_hid(c):
        wait_in(hid.at[chunk_rows(c + 1), unit_cols(left)], h_recv.at[0, c])
        wait_in(hid.at[chunk_rows(c + 1), unit_cols(right)], h_recv.at[1, c])
        for copy in h_relays(c):
            copy.start()

    def stage_down(c):
        @pl.when(c < packed)
        def _():
            wait_in(hid.at[first_half(c + 1), unit_cols(opposite)], h_recv.at[2, c])
            wait_in(hid.at[second_half(c + 1), unit_cols(opposite)], h_recv.at[3, c])

        row = lax.broadcasted_iota(jnp.int32, (chunk, 2 * chunk), 0)
        col = lax.broadcasted_iota(jnp.int32, (chunk, 2 * chunk), 1)
        place = c * chunk + row
        take = (col + (c - 1) * chunk == place - (SLOTS - CAP) * (place // SLOTS)) & (row % SLOTS < CAP)
        window = hid[pl.ds(pl.multiple_of(c * chunk, chunk), 2 * chunk), :]
        value = jnp.dot(
            jnp.where(take, 1.0, 0.0).astype(bf16), window, preferred_element_type=f32
        ).astype(bf16)
        outb[chunk_rows(c), :] = jnp.dot(value, dn[...], preferred_element_type=f32).astype(bf16)
        for i in range(1, per):
            ret_copy(c, i).start()

        def keep():
            ret[own_block(c), :] = outb[own_block(c), :]

        per_chunk(c, keep, lambda: ret_copy(c, 0).start())

    def stage_combine(at):
        for i in range(plane // chunk):
            c = at * (plane // chunk) + i
            per_chunk(
                c,
                lambda c=c: wait_in(ret.at[other_blocks(c)], ret_recv.at[c]),
                lambda c=c: wait_in(ret.at[chunk_rows(c)], ret_recv.at[c]),
            )
        sel = spread(at, 0, plane)
        taken = chosen(sel)
        back = ret[pl.ds(pl.multiple_of(at * plane, plane), plane), :]
        total = acc[...]
        for part in (ghi_ref, glo_ref):
            scale = jnp.dot(sel, part[...], preferred_element_type=f32)
            scale = jnp.where(taken, scale, 0.0).astype(bf16)
            total = total + lax.dot_general(
                scale, back, (((0,), (0,)), ((), ())), preferred_element_type=f32
            )
        acc[...] = total

    hid[:chunk, :] = jnp.zeros((chunk, hid.shape[1]), bf16)
    hid[(packed + 1) * chunk :, :] = jnp.zeros((chunk, hid.shape[1]), bf16)
    acc[...] = jnp.zeros_like(acc)

    def head(h, carry):
        scores = jnp.dot(keys[...], query[h], preferred_element_type=f32) * score_scale + bias[...]
        lifted = jnp.exp(scores - jnp.max(scores, axis=0, keepdims=True))
        probs = (lifted / jnp.sum(lifted, axis=0, keepdims=True)).astype(bf16)
        value = lax.dot_general(
            probs, keys[:, :LAT], (((0,), (0,)), ((), ())), preferred_element_type=f32
        )
        for k in range(LAT // LANES):
            wide[k, pl.ds(h, tokens, stride=heads), :] = value[:, k * LANES : (k + 1) * LANES]
        return carry

    parts = min(8, sent)
    attn_copy = pltpu.make_async_copy(attn, attn_ref, q_sem.at[1])
    early = min(2, nz)

    def step(t, carry):
        def at(delay, stage, count):
            @pl.when((t >= delay) & (t < delay + count))
            def _():
                stage(t - delay)

        at(0, stage_pack, packed)

        @pl.when(t + ahead < sent)
        def _():
            build(t + ahead)
            dispatch(t + ahead)

        at(1, stage_relay, packed)

        @pl.when(t == 2)
        def _():
            wait_in(relay_dn.at[0], w_recv.at[4])
            wait_in(relay_dn.at[1], w_recv.at[5])
            for copy in relays:
                copy.start()

        @pl.when(t == 0)
        def _():
            local_query.wait()
            wait_in(keys.at[pl.ds(0, tokens)], lat_recv.at[0])

        @pl.when(t < parts)
        def _():
            lax.fori_loop(t * (heads // parts), (t + 1) * (heads // parts), head, 0)

        @pl.when(t == parts)
        def _():
            def narrow(i, carry):
                some = pl.ds(pl.multiple_of(i * tokens, tokens), tokens)
                for k in range(LAT // LANES):
                    attn[some, k * LANES : (k + 1) * LANES] = wide[k, some, :].astype(bf16)
                return carry

            lax.fori_loop(0, heads, narrow, 0)
            attn_copy.start()

        @pl.when(t == 2)
        def _():
            local_gate.wait()
            local_up.wait()
            wait_in(gu.at[mate_in, gate_cols], w_recv.at[0])
            wait_in(gu.at[mate_in, up_cols], w_recv.at[1])

        at(2, stage_up, packed)
        at(3, stage_hid, packed)

        @pl.when(t == 3)
        def _():
            local_down.wait()
            wait_in(dn.at[unit_rows(left, 0, units), own_out], w_recv.at[2])
            wait_in(dn.at[unit_rows(right, 0, units), own_out], w_recv.at[3])
            wait_in(dn.at[unit_rows(opposite, 0, halfu), own_out], w_recv.at[6])
            wait_in(dn.at[unit_rows(opposite, halfu, halfu), own_out], w_recv.at[7])
            down_to_mate.start()

        @pl.when(t == 4)
        def _():
            wait_in(dn.at[:, mate_out], w_recv.at[8])

        at(4, stage_down, sent)

        @pl.when(lax.rem(t, 2) == 0)
        def _():
            @pl.when((t >= 14) & (t < 14 + 2 * early))
            def _():
                stage_combine(lax.div(t - 14, 2))

        return carry

    lax.fori_loop(0, sent + 4, step, 0)

    def finish(at, carry):
        stage_combine(at)
        return carry

    lax.fori_loop(early, nz, finish, 0)
    out_ref[...] = acc[...].astype(out_ref.dtype)

    attn_copy.wait()
    lat_copy.wait_send()
    for copy in to_side + to_mate + relays + [down_to_mate]:
        copy.wait_send()

    def drain(c, carry):
        for copy in x_copies(c) + x_relays(c) + h_copies(c) + h_relays(c):
            copy.wait_send()
        return carry

    lax.fori_loop(0, packed, drain, 0)

    def drain_sent(c, carry):
        def some():
            wait_in(disp.at[other_blocks(c)], disp_send.at[c])
            wait_in(outb.at[other_blocks(c)], ret_send.at[c])

        def whole():
            wait_in(disp.at[chunk_rows(c)], disp_send.at[c])
            wait_in(outb.at[chunk_rows(c)], ret_send.at[c])

        per_chunk(c, some, whole)
        return carry

    lax.fori_loop(0, sent, drain_sent, 0)


def layer(nz, ny, ids, scores, tok, gate, up, down, query, latent, docs):
    tokens, width = tok.shape
    units = gate.shape[1]
    piece = down.shape[1] // NX
    experts = nz * ny
    count, packed = experts * SLOTS, experts * CAP
    sent_n, packed_n = count // CHUNK, packed // CHUNK
    heads, feats, _ = query.shape
    vmem = pl.BlockSpec(memory_space=pltpu.VMEM)
    away = pl.BlockSpec(memory_space=pl.ANY)
    bf16 = jnp.bfloat16
    dma = pltpu.SemaphoreType.DMA
    return pl.pallas_call(
        functools.partial(layer_kernel, nz, ny),
        out_shape=(
            jax.ShapeDtypeStruct((tokens, width), bf16),
            jax.ShapeDtypeStruct((tokens * heads, LAT), bf16),
        ),
        in_specs=[vmem, vmem, vmem, away, away, away, away, vmem, vmem],
        out_specs=(vmem, away),
        scratch_shapes=[
            pltpu.VMEM((count, width), bf16),
            pltpu.VMEM((count, width), bf16),
            pltpu.VMEM((NX, packed, width), bf16),
            pltpu.VMEM((NX * width, 2 * units), bf16),
            pltpu.VMEM((NX * units, width), bf16),
            pltpu.VMEM((2, units // 2, piece), bf16),
            pltpu.VMEM((packed + 2 * CHUNK, NX * units), bf16),
            pltpu.VMEM((count, width), bf16),
            pltpu.VMEM((count, width), bf16),
            pltpu.VMEM((tokens, width), jnp.float32),
            pltpu.VMEM((experts, tokens), bf16),
            pltpu.VMEM((experts, tokens), bf16),
            pltpu.VMEM((experts, tokens), bf16),
            pltpu.VMEM((heads, feats, tokens), bf16),
            pltpu.VMEM((LAT // LANES, tokens * heads, LANES), jnp.float32),
            pltpu.VMEM((tokens * heads, LAT), bf16),
            pltpu.VMEM((2 * tokens, feats), bf16),
            pltpu.VMEM((2 * tokens, tokens), jnp.float32),
            dma((3,)),
            dma((2,)),
            dma((1,)),
            dma((1,)),
            dma((9,)),
            dma((9,)),
            dma((sent_n,)),
            dma((sent_n,)),
            dma((4, packed_n)),
            dma((4, packed_n)),
            dma((4, packed_n)),
            dma((4, packed_n)),
            dma((sent_n,)),
            dma((sent_n,)),
        ],
        compiler_params=pltpu.CompilerParams(
            collective_id=0, has_side_effects=True, vmem_limit_bytes=58 * 1024 * 1024
        ),
        name="layer",
    )(ids, scores, tok, gate, up, down, query, latent, docs)


def shards(
    queries,
    latents,
    doc_ids,
    hidden_rows,
    expert_ids,
    gate_scores,
    gate_weight,
    up_weight,
    down_weight,
):
    length = lax.axis_size("dp")
    moe_out, attn_out = layer(
        length // (2 * NY),
        NY,
        expert_ids.T,
        gate_scores.T,
        hidden_rows,
        gate_weight[0],
        up_weight[0],
        down_weight[0],
        queries.transpose(1, 2, 0),
        latents.T,
        doc_ids.reshape(length, -1),
    )
    return (attn_out.reshape(queries.shape[:2] + (LAT,)), moe_out)


def solution(mesh):
    placed = (
        P("dp", "mp", None),
        P("dp", None),
        P(),
        P("dp", "mp"),
        P("dp", None),
        P("dp", None),
        P("dp", None, "mp"),
        P("dp", None, "mp"),
        P("dp", "mp", None),
    )
    return jax.shard_map(
        shards,
        mesh=mesh,
        in_specs=placed,
        out_specs=(P("dp", "mp", None), P("dp", "mp")),
        check_vma=False,
    )
```

```python
import functools
import math

import jax
import jax.numpy as jnp
from jax import lax
from jax.experimental import pallas as pl
from jax.experimental.pallas import tpu as pltpu
from jax.sharding import PartitionSpec as P

LAT = 512
LANES = 128
SLOTS = 32
CHUNK = 64
NX = 4
NY = 4
PLANES = (2, -2, 3, -3, 4, 1, -1, 0)
FAR = 5
CHUNKS = (0, 1, 2, 3, 4, 5, 10, 11, 6, 7, 12, 13, 8, 9, 14, 15)
BACK = (0, 1, 2, 5, 3, 6, 4, 7)

score_scale = 1.0 / math.sqrt(192.0)
neg_large = -1e30
MESH = pl.DeviceIdType.MESH


def layer_kernel(
    nz,
    ny,
    ids_ref,
    score_ref,
    tok_ref,
    gate_ref,
    up_ref,
    down_ref,
    query_ref,
    latent_ref,
    doc_ref,
    out_ref,
    attn_ref,
    far_disp,
    near_disp,
    tok,
    wide_tok,
    rows,
    gu,
    dn,
    relay_dn,
    hid,
    outb,
    ret,
    acc,
    place_ref,
    ghi_ref,
    glo_ref,
    query,
    wide,
    attn,
    keys,
    bias,
    local_sem,
    q_sem,
    lat_send,
    lat_recv,
    w_send,
    w_recv,
    t_send,
    t_recv,
    f_send,
    f_recv,
    disp_send,
    disp_recv,
    x_send,
    x_recv,
    h_send,
    h_recv,
    ret_send,
    ret_recv,
):
    top, tokens = ids_ref.shape
    heads = query_ref.shape[0]
    width = tok_ref.shape[1]
    half_in, units = gate_ref.shape
    piece = down_ref.shape[1] // NX
    experts = nz * ny
    named_rows = LANES
    plane = ny * SLOTS
    chunk, half = CHUNK, CHUNK // 2
    per = CHUNK // SLOTS
    per_plane = plane // chunk
    chunks, far = nz * per_plane, FAR * per_plane
    own_chunk = PLANES.index(0) * per_plane
    f32, bf16 = jnp.float32, jnp.bfloat16

    d = lax.axis_index("dp")
    x = lax.axis_index("mp")
    s = lax.rem(d, 2)
    p = lax.div(d, 2)
    z = lax.div(p, ny)
    y = lax.rem(p, ny)
    right = lax.rem(x + 1, NX)
    left = lax.rem(x + NX - 1, NX)
    opposite = lax.rem(x + 2, NX)
    mate = d + 1 - 2 * s

    def dev(zz, yy):
        return (zz * ny + yy) * 2 + s

    def entry(table, i):
        total = 0
        for at, value in enumerate(table):
            total = total + jnp.where(i == at, value, 0)
        return total

    def offset(at):
        return entry(PLANES, at)

    def remote(src, dst, send, recv, dd, xx):
        return pltpu.make_async_remote_copy(
            src_ref=src, dst_ref=dst, send_sem=send, recv_sem=recv,
            device_id=(dd, xx), device_id_type=MESH,
        )

    def wait_in(ref, sem):
        pltpu.make_async_copy(ref, ref, sem).wait()

    own_in = pl.ds(pl.multiple_of(s * half_in, half_in), half_in)
    mate_in = pl.ds(pl.multiple_of((1 - s) * half_in, half_in), half_in)
    own_out = pl.ds(pl.multiple_of(s * piece, piece), piece)
    mate_out = pl.ds(pl.multiple_of((1 - s) * piece, piece), piece)
    gate_cols, up_cols = pl.ds(0, units), pl.ds(units, units)

    def unit_rows(q, start, count):
        return pl.ds(pl.multiple_of(q * units + start, units // 2), count)

    def unit_cols(q):
        return pl.ds(pl.multiple_of(q * units, units), units)

    def down_cols(q):
        return pl.ds(pl.multiple_of(q * piece, piece), piece)

    local_gate = pltpu.make_async_copy(gate_ref, gu.at[own_in, gate_cols], local_sem.at[0])
    local_up = pltpu.make_async_copy(up_ref, gu.at[own_in, up_cols], local_sem.at[1])
    local_down = pltpu.make_async_copy(
        down_ref.at[:, down_cols(x)], dn.at[unit_rows(x, 0, units), own_out], local_sem.at[2]
    )
    local_gate.start()
    local_up.start()
    local_down.start()
    local_query = pltpu.make_async_copy(query_ref, query, q_sem.at[0])
    local_query.start()

    barrier = pltpu.get_barrier_semaphore()

    def greet(dd, xx):
        pl.semaphore_signal(barrier, inc=1, device_id=(dd, xx), device_id_type=MESH)

    ring = experts * 2
    beside = lax.rem(d + 2 * s - 1 + ring, ring)
    following = lax.rem(d + 1, ring)
    greet(mate, x)
    greet(beside, x)
    greet(d, right)
    greet(d, left)

    def greet_peer(k, carry):
        greet(lax.rem(p + k, experts) * 2 + s, x)
        return carry

    lax.fori_loop(1, experts, greet_peer, 0)

    expert_at = lax.broadcasted_iota(jnp.int32, (named_rows, tokens), 0)
    named = jnp.zeros((named_rows, tokens), f32)
    weight = jnp.zeros((named_rows, tokens), f32)
    for k in range(top):
        hit = ids_ref[k : k + 1, :] == expert_at
        named = named + jnp.where(hit, 1.0, 0.0)
        weight = weight + jnp.where(hit, score_ref[k : k + 1, :], 0.0)
    row_at = lax.broadcasted_iota(jnp.int32, (tokens, tokens), 0)
    col_at = lax.broadcasted_iota(jnp.int32, (tokens, tokens), 1)
    before = jnp.dot(
        named.astype(bf16),
        jnp.where(row_at < col_at, 1.0, 0.0).astype(bf16),
        preferred_element_type=f32,
    )
    place_ref[...] = jnp.where(named > 0.5, before, -1.0).astype(bf16)
    whole = weight.astype(bf16)
    ghi_ref[...] = whole
    glo_ref[...] = (weight - whole.astype(f32)).astype(bf16)

    same = row_at == col_at
    unit = jnp.where(same, 1.0, 0.0).astype(bf16)
    keys[tokens:, :] = lax.dot_general(
        unit, latent_ref[...], (((1,), (1,)), ((), ())), preferred_element_type=f32
    ).astype(bf16)
    tok[0, :, :width] = tok_ref[...]
    tok[0, :, width:] = lax.dot_general(
        unit, place_ref[...], (((1,), (1,)), ((), ())), preferred_element_type=f32
    ).astype(bf16)
    lat_copy = remote(
        keys.at[pl.ds(tokens, tokens)], keys.at[pl.ds(0, tokens)],
        lat_send.at[0], lat_recv.at[0], following, x,
    )
    own_ids = doc_ref[pl.ds(d, 1), :]
    old_ids = doc_ref[pl.ds(lax.rem(d + ring - 1, ring), 1), :]
    own_col = jnp.sum(jnp.where(same, own_ids, 0).astype(f32), axis=1, keepdims=True)
    old_col = jnp.sum(jnp.where(same, old_ids, 0).astype(f32), axis=1, keepdims=True)
    old_col = old_col - jnp.where(d == 0, 1000.0, 0.0)
    ids_row = own_ids.astype(f32)
    bias[:tokens, :] = jnp.where(old_col == ids_row, 0.0, neg_large)
    bias[tokens:, :] = jnp.where((own_col == ids_row) & (row_at <= col_at), 0.0, neg_large)

    to_mate = [
        remote(gate_ref, gu.at[own_in, gate_cols], w_send.at[0], w_recv.at[0], mate, x),
        remote(up_ref, gu.at[own_in, up_cols], w_send.at[1], w_recv.at[1], mate, x),
    ]
    halfu = units // 2
    to_side = [
        remote(
            down_ref.at[:, down_cols(right)], dn.at[unit_rows(x, 0, units), own_out],
            w_send.at[2], w_recv.at[2], d, right,
        ),
        remote(
            down_ref.at[:, down_cols(left)], dn.at[unit_rows(x, 0, units), own_out],
            w_send.at[3], w_recv.at[3], d, left,
        ),
        remote(
            down_ref.at[pl.ds(0, halfu), down_cols(opposite)], relay_dn.at[0],
            w_send.at[4], w_recv.at[4], d, right,
        ),
        remote(
            down_ref.at[pl.ds(halfu, halfu), down_cols(opposite)], relay_dn.at[1],
            w_send.at[5], w_recv.at[5], d, left,
        ),
    ]
    relays = [
        remote(
            relay_dn.at[0], dn.at[unit_rows(left, 0, halfu), own_out],
            w_send.at[6], w_recv.at[6], d, right,
        ),
        remote(
            relay_dn.at[1], dn.at[unit_rows(right, halfu, halfu), own_out],
            w_send.at[7], w_recv.at[7], d, left,
        ),
    ]
    down_to_mate = remote(
        dn.at[:, own_out], dn.at[:, own_out], w_send.at[8], w_recv.at[8], mate, x
    )

    def chunk_rows(c):
        return pl.ds(pl.multiple_of(c * chunk, chunk), chunk)

    def block_rows(b):
        return pl.ds(pl.multiple_of(b * SLOTS, SLOTS), SLOTS)

    def chosen(plane_z, first, count, place, how):
        row = lax.broadcasted_iota(jnp.int32, (count, named_rows), 0)
        dest = plane_z * ny + ((y + first + (row // SLOTS)) % ny)
        sel = jnp.where(
            lax.broadcasted_iota(jnp.int32, (count, named_rows), 1) == dest, 1.0, 0.0
        ).astype(bf16)
        slot = (lax.broadcasted_iota(jnp.int32, (count, tokens), 0) % SLOTS).astype(f32)
        held = lax.dot_general(sel, place, (((1,), (how,)), ((), ())), preferred_element_type=f32)
        return sel, held == slot

    z_up, z_down = dev(lax.rem(z + 1, nz), y), dev(lax.rem(z + nz - 1, nz), y)
    middle = nz // 2
    upper, lower = pl.ds(0, tokens // 2), pl.ds(tokens // 2, tokens // 2)

    def t_ref(way, hop, part=False):
        ref = tok.at[hop if way == 0 else (nz - hop) % nz]
        return ref.at[upper if way == 0 else lower] if part else ref

    def t_copy(way, hop):
        part = hop == middle
        return remote(
            t_ref(way, hop - 1, part), t_ref(way, hop, part),
            t_send.at[way, hop - 1], t_recv.at[way, hop - 1], (z_up, z_down)[way], x,
        )

    def hand_on(hop):
        for way in range(2):
            wait_in(t_ref(way, hop, hop == middle), t_recv.at[way, hop - 1])
            if hop < middle:
                t_copy(way, hop + 1).start()

    f_own = [
        remote(tok_ref, wide_tok.at[0, NX - 2], f_send.at[0], f_recv.at[0], d, right),
        remote(tok_ref, wide_tok.at[0, 0], f_send.at[1], f_recv.at[1], d, left),
    ]
    f_relays = [
        remote(
            wide_tok.at[0, NX - 2, upper], wide_tok.at[0, 1, upper],
            f_send.at[2], f_recv.at[2], d, right,
        ),
        remote(
            wide_tok.at[0, 0, lower], wide_tok.at[0, 1, lower],
            f_send.at[3], f_recv.at[3], d, left,
        ),
    ]
    f_planes = [
        remote(wide_tok.at[0], wide_tok.at[1], f_send.at[4], f_recv.at[4], z_up, x),
        remote(wide_tok.at[0], wide_tok.at[2], f_send.at[5], f_recv.at[5], z_down, x),
    ]

    def near_rows(c):
        return pl.ds(pl.multiple_of((c - far) * chunk, chunk), chunk)

    def near_block(b):
        return pl.ds(pl.multiple_of((b - far * per) * SLOTS, SLOTS), SLOTS)

    def build(c):
        at = lax.div(c, per_plane)
        source = lax.rem(offset(at) + nz, nz)
        _, hit = chosen(z, lax.rem(c, per_plane) * per, chunk, tok[source, :, width:], 1)
        pick = jnp.where(hit, 1.0, 0.0).astype(bf16)
        far_disp[chunk_rows(c), :] = jnp.dot(
            pick, tok[source, :, :width], preferred_element_type=f32
        ).astype(bf16)

        @pl.when(c >= far)
        def _():
            which = lax.rem(at - FAR + 1, nz - FAR)
            for j in range(NX - 1):
                near_disp[j, near_rows(c), :] = jnp.dot(
                    pick, wide_tok[which, j], preferred_element_type=f32
                ).astype(bf16)

    def disp_copy(b):
        c = lax.div(b, per)
        return remote(
            far_disp.at[block_rows(b)], rows.at[0, block_rows(b)],
            disp_send.at[c], disp_recv.at[c], dev(z, lax.rem(y + lax.rem(b, ny), ny)), x,
        )

    def near_copy(b):
        c = lax.div(b, per)
        return remote(
            near_disp.at[:, near_block(b)], rows.at[pl.ds(1, NX - 1), block_rows(b)],
            disp_send.at[c], disp_recv.at[c], dev(z, lax.rem(y + lax.rem(b, ny), ny)), x,
        )

    def dispatch(c):
        build(c)
        for i in range(per):
            b = c * per + i

            def send(b=b):
                disp_copy(b).start()

                @pl.when(c >= far)
                def _():
                    near_copy(b).start()

            def keep(b=b):
                rows[0, block_rows(b), :] = far_disp[block_rows(b), :]

                @pl.when(c >= far)
                def _():
                    for j in range(NX - 1):
                        rows[1 + j, block_rows(b), :] = near_disp[j, near_block(b), :]

            if i == 0:
                pl.when(lax.rem(c, per_plane) == 0)(keep)
                pl.when(lax.rem(c, per_plane) != 0)(send)
            else:
                send()

    def moved(c, sem):
        first = lax.rem(c, per_plane) == 0

        @pl.when((c < far) & first)
        def _():
            wait_in(rows.at[0, other_blocks(c)], sem)

        @pl.when((c < far) & (lax.rem(c, per_plane) != 0))
        def _():
            wait_in(rows.at[0, chunk_rows(c)], sem)

        @pl.when((c >= far) & first)
        def _():
            wait_in(rows.at[:, other_blocks(c)], sem)

        @pl.when((c >= far) & (lax.rem(c, per_plane) != 0))
        def _():
            wait_in(rows.at[:, chunk_rows(c)], sem)

    def own_block(c):
        return pl.ds(pl.multiple_of(c * chunk, chunk), SLOTS)

    def other_blocks(c):
        return pl.ds(pl.multiple_of(c * chunk + SLOTS, SLOTS), chunk - SLOTS)

    def per_chunk(c, yes, no):
        pl.when(c == own_chunk)(yes)
        pl.when(c != own_chunk)(no)

    def first_half(c):
        return pl.ds(pl.multiple_of(c * chunk, chunk), half)

    def second_half(c):
        return pl.ds(pl.multiple_of(c * chunk + half, half), half)

    def x_copies(c):
        here = rows.at[0, chunk_rows(c)]
        return (
            remote(here, rows.at[3, chunk_rows(c)], x_send.at[0, c], x_recv.at[0, c], d, right),
            remote(here, rows.at[1, chunk_rows(c)], x_send.at[1, c], x_recv.at[1, c], d, left),
        )

    def x_relays(c):
        from_left, from_right = rows.at[3, first_half(c)], rows.at[1, second_half(c)]
        return (
            remote(
                from_left, rows.at[2, first_half(c)], x_send.at[2, c], x_recv.at[2, c], d, right
            ),
            remote(
                from_right, rows.at[2, second_half(c)], x_send.at[3, c], x_recv.at[3, c], d, left
            ),
        )

    def h_copies(c):
        here = hid.at[chunk_rows(c), unit_cols(x)]
        return (
            remote(here, here, h_send.at[0, c], h_recv.at[0, c], d, right),
            remote(here, here, h_send.at[1, c], h_recv.at[1, c], d, left),
        )

    def h_relays(c):
        from_left = hid.at[first_half(c), unit_cols(left)]
        from_right = hid.at[second_half(c), unit_cols(right)]
        return (
            remote(from_left, from_left, h_send.at[2, c], h_recv.at[2, c], d, right),
            remote(from_right, from_right, h_send.at[3, c], h_recv.at[3, c], d, left),
        )

    def ret_copy(c, i):
        b = c * per + i
        zz = lax.rem(z - offset(lax.div(b, ny)) + nz, nz)
        return remote(
            outb.at[block_rows(b)], ret.at[block_rows(b)], ret_send.at[c], ret_recv.at[c],
            dev(zz, lax.rem(y - lax.rem(b, ny) + ny, ny)), x,
        )

    def stage_arrive(c):
        moved(c, disp_recv.at[c])
        for copy in x_copies(c):
            copy.start()

    def stage_relay(c):
        wait_in(rows.at[3, chunk_rows(c)], x_recv.at[0, c])
        wait_in(rows.at[1, chunk_rows(c)], x_recv.at[1, c])
        for copy in x_relays(c):
            copy.start()

    def stage_up(i):
        c = entry(CHUNKS, i)

        @pl.when(c < far)
        def _():
            wait_in(rows.at[2, first_half(c)], x_recv.at[2, c])
            wait_in(rows.at[2, second_half(c)], x_recv.at[3, c])

        @pl.when(c >= far)
        def _():
            moved(c, disp_recv.at[c])

        total = jnp.zeros((chunk, 2 * units), f32)
        for j in range(NX):
            features = pl.ds(pl.multiple_of(lax.rem(x + j, NX) * width, width), width)
            total = total + jnp.dot(
                rows[j, chunk_rows(c), :], gu[features, :], preferred_element_type=f32
            )
        gate, up = total[:, :units], total[:, units:]
        hid[chunk_rows(c), unit_cols(x)] = (gate / (1.0 + jnp.exp(-gate)) * up).astype(bf16)
        for copy in h_copies(c):
            copy.start()

    def stage_hid(i):
        c = entry(CHUNKS, i)
        wait_in(hid.at[chunk_rows(c), unit_cols(left)], h_recv.at[0, c])
        wait_in(hid.at[chunk_rows(c), unit_cols(right)], h_recv.at[1, c])
        for copy in h_relays(c):
            copy.start()

    def stage_down(i):
        c = entry(CHUNKS, i)
        wait_in(hid.at[first_half(c), unit_cols(opposite)], h_recv.at[2, c])
        wait_in(hid.at[second_half(c), unit_cols(opposite)], h_recv.at[3, c])
        outb[chunk_rows(c), :] = jnp.dot(
            hid[chunk_rows(c), :], dn[...], preferred_element_type=f32
        ).astype(bf16)
        for i in range(1, per):
            ret_copy(c, i).start()

        def keep():
            ret[own_block(c), :] = outb[own_block(c), :]

        per_chunk(c, keep, lambda: ret_copy(c, 0).start())

    def stage_combine(i):
        at = entry(BACK, i)
        for k in range(per_plane):
            c = at * per_plane + k
            per_chunk(
                c,
                lambda c=c: wait_in(ret.at[other_blocks(c)], ret_recv.at[c]),
                lambda c=c: wait_in(ret.at[chunk_rows(c)], ret_recv.at[c]),
            )
        zz = lax.rem(z + offset(at) + nz, nz)
        sel, taken = chosen(zz, 0, plane, place_ref[...], 0)
        back = ret[pl.ds(pl.multiple_of(at * plane, plane), plane), :]
        total = acc[...]
        for part in (ghi_ref, glo_ref):
            scale = jnp.dot(sel, part[...], preferred_element_type=f32)
            scale = jnp.where(taken, scale, 0.0).astype(bf16)
            total = total + lax.dot_general(
                scale, back, (((0,), (0,)), ((), ())), preferred_element_type=f32
            )
        acc[...] = total

    acc[...] = jnp.zeros_like(acc)

    def head(h, carry):
        scores = jnp.dot(keys[...], query[h], preferred_element_type=f32) * score_scale + bias[...]
        lifted = jnp.exp(scores - jnp.max(scores, axis=0, keepdims=True))
        probs = (lifted / jnp.sum(lifted, axis=0, keepdims=True)).astype(bf16)
        value = lax.dot_general(
            probs, keys[:, :LAT], (((0,), (0,)), ((), ())), preferred_element_type=f32
        )
        for k in range(LAT // LANES):
            wide[k, pl.ds(h, tokens, stride=heads), :] = value[:, k * LANES : (k + 1) * LANES]
        return carry

    def some_heads(first, count):
        lax.fori_loop(first, first + count, head, 0)

    pl.semaphore_wait(barrier, experts - 1 + 4)

    for copy in [t_copy(0, 1), t_copy(1, 1)] + f_own + [lat_copy] + to_side[:2] + to_mate:
        copy.start()
    local_query.wait()
    wait_in(keys.at[pl.ds(0, tokens)], lat_recv.at[0])
    some_heads(0, 4)
    hand_on(1)
    wait_in(wide_tok.at[0, NX - 2], f_recv.at[0])
    wait_in(wide_tok.at[0, 0], f_recv.at[1])
    for copy in f_relays + to_side[2:]:
        copy.start()
    some_heads(4, 4)
    hand_on(2)
    ahead = 4
    for c in range(ahead):
        dispatch(jnp.int32(c))

    attn_copy = pltpu.make_async_copy(attn, attn_ref, q_sem.at[1])

    def step(t, carry):
        def at(delay, stage, count):
            @pl.when((t >= delay) & (t < delay + count))
            def _():
                stage(t - delay)

        at(0, stage_arrive, far)

        @pl.when(t == 0)
        def _():
            hand_on(3)

        @pl.when(t == 1)
        def _():
            wait_in(wide_tok.at[0, 1, upper], f_recv.at[2])
            wait_in(wide_tok.at[0, 1, lower], f_recv.at[3])
            for copy in f_planes:
                copy.start()

        @pl.when(t == 2)
        def _():
            hand_on(middle)

        @pl.when(t == far - ahead)
        def _():
            wait_in(wide_tok.at[1], f_recv.at[4])
            wait_in(wide_tok.at[2], f_recv.at[5])

        @pl.when(t + ahead < chunks)
        def _():
            dispatch(t + ahead)

        at(1, stage_relay, far)

        @pl.when(t == 1)
        def _():
            wait_in(relay_dn.at[0], w_recv.at[4])
            wait_in(relay_dn.at[1], w_recv.at[5])
            for copy in relays:
                copy.start()

        @pl.when(t < 4)
        def _():
            some_heads(8 + 2 * t, 2)

        @pl.when(t == 4)
        def _():
            def narrow(i, carry):
                some = pl.ds(pl.multiple_of(i * tokens, tokens), tokens)
                for k in range(LAT // LANES):
                    attn[some, k * LANES : (k + 1) * LANES] = wide[k, some, :].astype(bf16)
                return carry

            lax.fori_loop(0, heads, narrow, 0)
            attn_copy.start()

        @pl.when(t == 2)
        def _():
            local_gate.wait()
            local_up.wait()
            wait_in(gu.at[mate_in, gate_cols], w_recv.at[0])
            wait_in(gu.at[mate_in, up_cols], w_recv.at[1])

        at(2, stage_up, chunks)
        at(3, stage_hid, chunks)

        @pl.when(t == 3)
        def _():
            local_down.wait()
            wait_in(dn.at[unit_rows(left, 0, units), own_out], w_recv.at[2])
            wait_in(dn.at[unit_rows(right, 0, units), own_out], w_recv.at[3])
            wait_in(dn.at[unit_rows(opposite, 0, halfu), own_out], w_recv.at[6])
            wait_in(dn.at[unit_rows(opposite, halfu, halfu), own_out], w_recv.at[7])
            down_to_mate.start()

        @pl.when(t == 4)
        def _():
            wait_in(dn.at[:, mate_out], w_recv.at[8])

        at(4, stage_down, chunks)

        @pl.when((lax.rem(t, 2) == 0) & (t >= 12) & (t < 12 + 2 * early))
        def _():
            stage_combine(lax.div(t - 12, 2))

        return carry

    early = 3
    lax.fori_loop(0, chunks + 4, step, 0)

    def finish(i, carry):
        stage_combine(i)
        return carry

    lax.fori_loop(early, nz, finish, 0)
    out_ref[...] = acc[...].astype(out_ref.dtype)

    attn_copy.wait()
    lat_copy.wait_send()
    for copy in to_side + to_mate + relays + [down_to_mate] + f_own + f_relays + f_planes:
        copy.wait_send()
    for hop in range(1, middle + 1):
        for way in range(2):
            t_copy(way, hop).wait_send()

    def drain_far(c, carry):
        for copy in x_copies(c) + x_relays(c):
            copy.wait_send()
        return carry

    lax.fori_loop(0, far, drain_far, 0)

    def drain(c, carry):
        for copy in h_copies(c) + h_relays(c):
            copy.wait_send()
        moved(c, disp_send.at[c])
        per_chunk(
            c,
            lambda: wait_in(outb.at[other_blocks(c)], ret_send.at[c]),
            lambda: wait_in(outb.at[chunk_rows(c)], ret_send.at[c]),
        )
        return carry

    lax.fori_loop(0, chunks, drain, 0)


def layer(nz, ny, ids, scores, tok, gate, up, down, query, latent, docs):
    tokens, width = tok.shape
    units = gate.shape[1]
    piece = down.shape[1] // NX
    experts = nz * ny
    count = experts * SLOTS
    chunks = count // CHUNK
    far = chunks * FAR // nz
    heads, feats, _ = query.shape
    vmem = pl.BlockSpec(memory_space=pltpu.VMEM)
    away = pl.BlockSpec(memory_space=pl.ANY)
    bf16 = jnp.bfloat16
    dma = pltpu.SemaphoreType.DMA
    return pl.pallas_call(
        functools.partial(layer_kernel, nz, ny),
        out_shape=(
            jax.ShapeDtypeStruct((tokens, width), bf16),
            jax.ShapeDtypeStruct((tokens * heads, LAT), bf16),
        ),
        in_specs=[vmem, vmem, vmem, away, away, away, away, vmem, vmem],
        out_specs=(vmem, away),
        scratch_shapes=[
            pltpu.VMEM((count, width), bf16),
            pltpu.VMEM((NX - 1, (chunks - far) * CHUNK, width), bf16),
            pltpu.VMEM((nz, tokens, width + LANES), bf16),
            pltpu.VMEM((nz - FAR, NX - 1, tokens, width), bf16),
            pltpu.VMEM((NX, count, width), bf16),
            pltpu.VMEM((NX * width, 2 * units), bf16),
            pltpu.VMEM((NX * units, width), bf16),
            pltpu.VMEM((2, units // 2, piece), bf16),
            pltpu.VMEM((count, NX * units), bf16),
            pltpu.VMEM((count, width), bf16),
            pltpu.VMEM((count, width), bf16),
            pltpu.VMEM((tokens, width), jnp.float32),
            pltpu.VMEM((LANES, tokens), bf16),
            pltpu.VMEM((LANES, tokens), bf16),
            pltpu.VMEM((LANES, tokens), bf16),
            pltpu.VMEM((heads, feats, tokens), bf16),
            pltpu.VMEM((LAT // LANES, tokens * heads, LANES), jnp.float32),
            pltpu.VMEM((tokens * heads, LAT), bf16),
            pltpu.VMEM((2 * tokens, feats), bf16),
            pltpu.VMEM((2 * tokens, tokens), jnp.float32),
            dma((3,)),
            dma((2,)),
            dma((1,)),
            dma((1,)),
            dma((9,)),
            dma((9,)),
            dma((2, nz // 2)),
            dma((2, nz // 2)),
            dma((6,)),
            dma((6,)),
            dma((chunks,)),
            dma((chunks,)),
            dma((4, far)),
            dma((4, far)),
            dma((4, chunks)),
            dma((4, chunks)),
            dma((chunks,)),
            dma((chunks,)),
        ],
        compiler_params=pltpu.CompilerParams(
            collective_id=0, has_side_effects=True, vmem_limit_bytes=58 * 1024 * 1024
        ),
        name="layer",
    )(ids, scores, tok, gate, up, down, query, latent, docs)


def shards(
    queries,
    latents,
    doc_ids,
    hidden_rows,
    expert_ids,
    gate_scores,
    gate_weight,
    up_weight,
    down_weight,
):
    length = lax.axis_size("dp")
    moe_out, attn_out = layer(
        length // (2 * NY),
        NY,
        expert_ids.T,
        gate_scores.T,
        hidden_rows,
        gate_weight[0],
        up_weight[0],
        down_weight[0],
        queries.transpose(1, 2, 0),
        latents.T,
        doc_ids.reshape(length, -1),
    )
    return (attn_out.reshape(queries.shape[:2] + (LAT,)), moe_out)


def solution(mesh):
    placed = (
        P("dp", "mp", None),
        P("dp", None),
        P(),
        P("dp", "mp"),
        P("dp", None),
        P("dp", None),
        P("dp", None, "mp"),
        P("dp", None, "mp"),
        P("dp", "mp", None),
    )
    return jax.shard_map(
        shards,
        mesh=mesh,
        in_specs=placed,
        out_specs=(P("dp", "mp", None), P("dp", "mp")),
        check_vma=False,
    )
```

```python
import functools
import math

import jax
import jax.numpy as jnp
from jax import lax
from jax.experimental import pallas as pl
from jax.experimental.pallas import tpu as pltpu
from jax.sharding import PartitionSpec as P

LAT = 512
LANES = 128
PIECES = 8
SLOTS = 32
CAP = 30
CHUNK = 64
NX = 4
NY = 4
Z_ORDER = {8: (1, -2, 4, 3, -3, 2, -1, 0), 4: (0, 2, 1, -1), 2: (0, 1)}

score_scale = 1.0 / math.sqrt(192.0)
neg_large = -1e30
MESH = pl.DeviceIdType.MESH


def layer_kernel(
    nz,
    ny,
    ids_in,
    score_in,
    tok_in,
    gate_ref,
    up_ref,
    down_ref,
    query_ref,
    latent_in,
    doc_in,
    out_ref,
    attn_ref,
    disp,
    land,
    rows,
    gu,
    dn,
    relay_dn,
    hid,
    outb,
    ret,
    acc,
    place_ref,
    ghi_ref,
    glo_ref,
    query,
    wide,
    attn,
    keys,
    bias,
    ids_ref,
    score_ref,
    tok_ref,
    latent_ref,
    doc_ref,
    in_sem,
    local_sem,
    q_sem,
    lat_send,
    lat_recv,
    w_send,
    w_recv,
    disp_send,
    disp_recv,
    x_send,
    x_recv,
    h_send,
    h_recv,
    ret_send,
    ret_recv,
):
    top, tokens = ids_in.shape
    heads = query_ref.shape[0]
    width = tok_in.shape[1]
    half_in, units = gate_ref.shape
    piece = down_ref.shape[1] // NX
    experts = nz * ny
    plane = ny * SLOTS
    chunk, half = CHUNK, CHUNK // 2
    per = CHUNK // SLOTS
    sent, packed = experts * SLOTS // chunk, experts * CAP // chunk
    own_chunk = Z_ORDER[nz].index(0) * (plane // chunk)
    f32, bf16 = jnp.float32, jnp.bfloat16

    d = lax.axis_index("dp")
    x = lax.axis_index("mp")
    s = lax.rem(d, 2)
    p = lax.div(d, 2)
    z = lax.div(p, ny)
    y = lax.rem(p, ny)
    right = lax.rem(x + 1, NX)
    left = lax.rem(x + NX - 1, NX)
    opposite = lax.rem(x + 2, NX)
    mate = d + 1 - 2 * s

    def dev(zz, yy):
        return (zz * ny + yy) * 2 + s

    def offset(c):
        total = 0
        for at, by in enumerate(Z_ORDER[nz]):
            total = total + jnp.where(c == at, by, 0)
        return total

    def remote(src, dst, send, recv, dd, xx):
        return pltpu.make_async_remote_copy(
            src_ref=src, dst_ref=dst, send_sem=send, recv_sem=recv,
            device_id=(dd, xx), device_id_type=MESH,
        )

    def wait_in(ref, sem):
        pltpu.make_async_copy(ref, ref, sem).wait()

    own_in = pl.ds(pl.multiple_of(s * half_in, half_in), half_in)
    mate_in = pl.ds(pl.multiple_of((1 - s) * half_in, half_in), half_in)
    own_out = pl.ds(pl.multiple_of(s * piece, piece), piece)
    mate_out = pl.ds(pl.multiple_of((1 - s) * piece, piece), piece)
    gate_cols, up_cols = pl.ds(0, units), pl.ds(units, units)

    def unit_rows(q, start, count):
        return pl.ds(pl.multiple_of(q * units + start, units // 2), count)

    def unit_cols(q):
        return pl.ds(pl.multiple_of(q * units, units), units)

    def down_cols(q):
        return pl.ds(pl.multiple_of(q * piece, piece), piece)

    local_gate = pltpu.make_async_copy(gate_ref, gu.at[own_in, gate_cols], local_sem.at[0])
    local_up = pltpu.make_async_copy(up_ref, gu.at[own_in, up_cols], local_sem.at[1])
    local_down = pltpu.make_async_copy(
        down_ref.at[:, down_cols(x)], dn.at[unit_rows(x, 0, units), own_out], local_sem.at[2]
    )
    local_query = pltpu.make_async_copy(query_ref, query, q_sem.at[0])
    inputs = [
        pltpu.make_async_copy(source, held, in_sem.at[k])
        for k, (source, held) in enumerate(
            (
                (ids_in, ids_ref),
                (score_in, score_ref),
                (tok_in, tok_ref),
                (latent_in, latent_ref),
                (doc_in, doc_ref),
            )
        )
    ]
    for copy in inputs:
        copy.start()

    barrier = pltpu.get_barrier_semaphore()

    def greet(dd, xx):
        pl.semaphore_signal(barrier, inc=1, device_id=(dd, xx), device_id_type=MESH)

    ring = experts * 2
    beside = lax.rem(d + 2 * s - 1 + ring, ring)
    following = lax.rem(d + 1, ring)
    greet(mate, x)
    greet(beside, x)
    greet(d, right)
    greet(d, left)

    def greet_peer(k, carry):
        greet(lax.rem(p + k, experts) * 2 + s, x)
        return carry

    lax.fori_loop(1, experts, greet_peer, 0)
    for copy in [local_gate, local_up, local_down, local_query]:
        copy.start()
    for copy in inputs:
        copy.wait()

    expert_at = lax.broadcasted_iota(jnp.int32, (experts, tokens), 0)
    named = jnp.zeros((experts, tokens), f32)
    weight = jnp.zeros((experts, tokens), f32)
    for k in range(top):
        hit = ids_ref[k : k + 1, :] == expert_at
        named = named + jnp.where(hit, 1.0, 0.0)
        weight = weight + jnp.where(hit, score_ref[k : k + 1, :], 0.0)
    row_at = lax.broadcasted_iota(jnp.int32, (tokens, tokens), 0)
    col_at = lax.broadcasted_iota(jnp.int32, (tokens, tokens), 1)
    before = jnp.dot(
        named.astype(bf16),
        jnp.where(row_at < col_at, 1.0, 0.0).astype(bf16),
        preferred_element_type=f32,
    )
    place_ref[...] = jnp.where(named > 0.5, before, -1.0).astype(bf16)
    whole = weight.astype(bf16)
    ghi_ref[...] = whole
    glo_ref[...] = (weight - whole.astype(f32)).astype(bf16)

    same = row_at == col_at
    keys[tokens:, :] = lax.dot_general(
        jnp.where(same, 1.0, 0.0).astype(bf16), latent_ref[...], (((1,), (1,)), ((), ())),
        preferred_element_type=f32,
    ).astype(bf16)
    lat_copy = remote(
        keys.at[pl.ds(tokens, tokens)], keys.at[pl.ds(0, tokens)],
        lat_send.at[0], lat_recv.at[0], following, x,
    )
    own_ids = doc_ref[pl.ds(d, 1), :]
    old_ids = doc_ref[pl.ds(lax.rem(d + ring - 1, ring), 1), :]
    own_col = jnp.sum(jnp.where(same, own_ids, 0).astype(f32), axis=1, keepdims=True)
    old_col = jnp.sum(jnp.where(same, old_ids, 0).astype(f32), axis=1, keepdims=True)
    old_col = old_col - jnp.where(d == 0, 1000.0, 0.0)
    ids_row = own_ids.astype(f32)
    bias[:tokens, :] = jnp.where(old_col == ids_row, 0.0, neg_large)
    bias[tokens:, :] = jnp.where((own_col == ids_row) & (row_at <= col_at), 0.0, neg_large)

    to_mate = [
        remote(gate_ref, gu.at[own_in, gate_cols], w_send.at[0], w_recv.at[0], mate, x),
        remote(up_ref, gu.at[own_in, up_cols], w_send.at[1], w_recv.at[1], mate, x),
    ]
    halfu = units // 2
    to_side = [
        remote(
            down_ref.at[:, down_cols(right)], dn.at[unit_rows(x, 0, units), own_out],
            w_send.at[2], w_recv.at[2], d, right,
        ),
        remote(
            down_ref.at[:, down_cols(left)], dn.at[unit_rows(x, 0, units), own_out],
            w_send.at[3], w_recv.at[3], d, left,
        ),
        remote(
            down_ref.at[pl.ds(0, halfu), down_cols(opposite)], relay_dn.at[0],
            w_send.at[4], w_recv.at[4], d, right,
        ),
        remote(
            down_ref.at[pl.ds(halfu, halfu), down_cols(opposite)], relay_dn.at[1],
            w_send.at[5], w_recv.at[5], d, left,
        ),
    ]
    relays = [
        remote(
            relay_dn.at[0], dn.at[unit_rows(left, 0, halfu), own_out],
            w_send.at[6], w_recv.at[6], d, right,
        ),
        remote(
            relay_dn.at[1], dn.at[unit_rows(right, halfu, halfu), own_out],
            w_send.at[7], w_recv.at[7], d, left,
        ),
    ]
    down_to_mate = remote(
        dn.at[:, own_out], dn.at[:, own_out], w_send.at[8], w_recv.at[8], mate, x
    )

    def chunk_rows(c):
        return pl.ds(pl.multiple_of(c * chunk, chunk), chunk)

    def block_rows(b):
        return pl.ds(pl.multiple_of(b * SLOTS, SLOTS), SLOTS)

    def peer(b, way):
        zz = lax.rem(z + way * offset(lax.div(b, ny)) + nz, nz)
        return dev(zz, lax.rem(y + way * lax.rem(b, ny) + ny, ny))

    def spread(at, first, count):
        zz = lax.rem(z + offset(at) + nz, nz)
        row = lax.broadcasted_iota(jnp.int32, (count, experts), 0)
        dest = zz * ny + ((y + first + (row // SLOTS)) % ny)
        return jnp.where(
            lax.broadcasted_iota(jnp.int32, (count, experts), 1) == dest, 1.0, 0.0
        ).astype(bf16)

    def chosen(sel):
        count = sel.shape[0]
        slot = (lax.broadcasted_iota(jnp.int32, (count, tokens), 0) % SLOTS).astype(f32)
        return jnp.dot(sel, place_ref[...], preferred_element_type=f32) == slot

    def build(c):
        first = c * per
        sel = spread(lax.div(first, ny), lax.rem(first, ny), chunk)
        pick = jnp.where(chosen(sel), 1.0, 0.0).astype(bf16)
        block = jnp.dot(pick, tok_ref[...], preferred_element_type=f32).astype(bf16)
        disp[chunk_rows(c), :] = block

    def disp_copy(c, i):
        b = c * per + i
        return remote(
            disp.at[block_rows(b)], land.at[block_rows(b)],
            disp_send.at[c], disp_recv.at[c], peer(b, 1), x,
        )

    def own_block(c):
        return pl.ds(pl.multiple_of(c * chunk, chunk), SLOTS)

    def other_blocks(c):
        return pl.ds(pl.multiple_of(c * chunk + SLOTS, SLOTS), chunk - SLOTS)

    def per_chunk(c, yes, no):
        pl.when(c == own_chunk)(yes)
        pl.when(c != own_chunk)(no)

    def dispatch(c):
        for i in range(1, per):
            disp_copy(c, i).start()

        def keep():
            land[own_block(c), :] = disp[own_block(c), :]

        per_chunk(c, keep, lambda: disp_copy(c, 0).start())

    ahead = min(6, sent)
    for c in range(4):
        build(jnp.int32(c))

    pl.semaphore_wait(barrier, experts - 1 + 4)

    for copy in to_side[:2]:
        copy.start()
    for c in range(ahead):
        if c >= 4:
            build(jnp.int32(c))
        dispatch(jnp.int32(c))
        if c == 1:
            for copy in to_side[2:] + [lat_copy] + to_mate:
                copy.start()

    def first_half(c):
        return pl.ds(pl.multiple_of(c * chunk, chunk), half)

    def second_half(c):
        return pl.ds(pl.multiple_of(c * chunk + half, half), half)

    def x_copies(c):
        here = rows.at[x, chunk_rows(c)]
        return (
            remote(here, here, x_send.at[0, c], x_recv.at[0, c], d, right),
            remote(here, here, x_send.at[1, c], x_recv.at[1, c], d, left),
        )

    def x_relays(c):
        from_left, from_right = rows.at[left, first_half(c)], rows.at[right, second_half(c)]
        return (
            remote(from_left, from_left, x_send.at[2, c], x_recv.at[2, c], d, right),
            remote(from_right, from_right, x_send.at[3, c], x_recv.at[3, c], d, left),
        )

    def h_copies(c):
        here = hid.at[chunk_rows(c + 1), unit_cols(x)]
        return (
            remote(here, here, h_send.at[0, c], h_recv.at[0, c], d, right),
            remote(here, here, h_send.at[1, c], h_recv.at[1, c], d, left),
        )

    def h_relays(c):
        from_left = hid.at[first_half(c + 1), unit_cols(left)]
        from_right = hid.at[second_half(c + 1), unit_cols(right)]
        return (
            remote(from_left, from_left, h_send.at[2, c], h_recv.at[2, c], d, right),
            remote(from_right, from_right, h_send.at[3, c], h_recv.at[3, c], d, left),
        )

    def ret_copy(c, i):
        b = c * per + i
        return remote(
            outb.at[block_rows(b)], ret.at[block_rows(b)],
            ret_send.at[c], ret_recv.at[c], peer(b, -1), x,
        )

    def arrived(c):
        per_chunk(
            c,
            lambda: wait_in(land.at[other_blocks(c)], disp_recv.at[c]),
            lambda: wait_in(land.at[chunk_rows(c)], disp_recv.at[c]),
        )

    def stage_pack(c):
        @pl.when(c == 0)
        def _():
            arrived(c)

        arrived(c + 1)
        row = lax.broadcasted_iota(jnp.int32, (chunk, 2 * chunk), 0)
        col = lax.broadcasted_iota(jnp.int32, (chunk, 2 * chunk), 1)
        take = col == row + (SLOTS - CAP) * ((row + c * chunk) // CAP)
        window = land[pl.ds(pl.multiple_of(c * chunk, chunk), 2 * chunk), :]
        rows[x, chunk_rows(c), :] = jnp.dot(
            jnp.where(take, 1.0, 0.0).astype(bf16), window, preferred_element_type=f32
        ).astype(bf16)
        for copy in x_copies(c):
            copy.start()

    def stage_relay(c):
        wait_in(rows.at[left, chunk_rows(c)], x_recv.at[0, c])
        wait_in(rows.at[right, chunk_rows(c)], x_recv.at[1, c])
        for copy in x_relays(c):
            copy.start()

    def stage_up(c):
        wait_in(rows.at[opposite, first_half(c)], x_recv.at[2, c])
        wait_in(rows.at[opposite, second_half(c)], x_recv.at[3, c])
        total = jnp.zeros((chunk, 2 * units), f32)
        for m in range(NX):
            total = total + jnp.dot(
                rows[m, chunk_rows(c), :], gu[m * width : (m + 1) * width, :],
                preferred_element_type=f32,
            )
        gate, upper = total[:, :units], total[:, units:]
        hid[chunk_rows(c + 1), unit_cols(x)] = (gate / (1.0 + jnp.exp(-gate)) * upper).astype(bf16)
        for copy in h_copies(c):
            copy.start()

    def stage_hid(c):
        wait_in(hid.at[chunk_rows(c + 1), unit_cols(left)], h_recv.at[0, c])
        wait_in(hid.at[chunk_rows(c + 1), unit_cols(right)], h_recv.at[1, c])
        for copy in h_relays(c):
            copy.start()

    def stage_down(c):
        @pl.when(c < packed)
        def _():
            wait_in(hid.at[first_half(c + 1), unit_cols(opposite)], h_recv.at[2, c])
            wait_in(hid.at[second_half(c + 1), unit_cols(opposite)], h_recv.at[3, c])

        row = lax.broadcasted_iota(jnp.int32, (chunk, 2 * chunk), 0)
        col = lax.broadcasted_iota(jnp.int32, (chunk, 2 * chunk), 1)
        place = c * chunk + row
        take = (col + (c - 1) * chunk == place - (SLOTS - CAP) * (place // SLOTS)) & (row % SLOTS < CAP)
        window = hid[pl.ds(pl.multiple_of(c * chunk, chunk), 2 * chunk), :]
        value = jnp.dot(
            jnp.where(take, 1.0, 0.0).astype(bf16), window, preferred_element_type=f32
        ).astype(bf16)
        outb[chunk_rows(c), :] = jnp.dot(value, dn[...], preferred_element_type=f32).astype(bf16)
        for i in range(1, per):
            ret_copy(c, i).start()

        def keep():
            ret[own_block(c), :] = outb[own_block(c), :]

        per_chunk(c, keep, lambda: ret_copy(c, 0).start())

    def stage_combine(at):
        for i in range(plane // chunk):
            c = at * (plane // chunk) + i
            per_chunk(
                c,
                lambda c=c: wait_in(ret.at[other_blocks(c)], ret_recv.at[c]),
                lambda c=c: wait_in(ret.at[chunk_rows(c)], ret_recv.at[c]),
            )
        sel = spread(at, 0, plane)
        taken = chosen(sel)
        back = ret[pl.ds(pl.multiple_of(at * plane, plane), plane), :]
        total = acc[...]
        for part in (ghi_ref, glo_ref):
            scale = jnp.dot(sel, part[...], preferred_element_type=f32)
            scale = jnp.where(taken, scale, 0.0).astype(bf16)
            total = total + lax.dot_general(
                scale, back, (((0,), (0,)), ((), ())), preferred_element_type=f32
            )
        acc[...] = total

    hid[:chunk, :] = jnp.zeros((chunk, hid.shape[1]), bf16)
    hid[(packed + 1) * chunk :, :] = jnp.zeros((chunk, hid.shape[1]), bf16)
    acc[...] = jnp.zeros_like(acc)

    def head(h, carry):
        scores = jnp.dot(keys[...], query[h], preferred_element_type=f32) * score_scale + bias[...]
        lifted = jnp.exp(scores - jnp.max(scores, axis=0, keepdims=True))
        probs = (lifted / jnp.sum(lifted, axis=0, keepdims=True)).astype(bf16)
        value = lax.dot_general(
            probs, keys[:, :LAT], (((0,), (0,)), ((), ())), preferred_element_type=f32
        )
        for k in range(LAT // LANES):
            wide[k, pl.ds(h, tokens, stride=heads), :] = value[:, k * LANES : (k + 1) * LANES]
        return carry

    parts = min(4, sent)
    attn_copy = pltpu.make_async_copy(attn, attn_ref, q_sem.at[1])
    early = min(5, nz)

    def step(t, carry):
        def at(delay, stage, count):
            @pl.when((t >= delay) & (t < delay + count))
            def _():
                stage(t - delay)

        at(0, stage_pack, packed)

        @pl.when(t + ahead < sent)
        def _():
            build(t + ahead)
            dispatch(t + ahead)

        at(1, stage_relay, packed)

        @pl.when(t == 2)
        def _():
            wait_in(relay_dn.at[0], w_recv.at[4])
            wait_in(relay_dn.at[1], w_recv.at[5])
            for copy in relays:
                copy.start()

        @pl.when(t == 0)
        def _():
            local_query.wait()
            wait_in(keys.at[pl.ds(0, tokens)], lat_recv.at[0])

        @pl.when(t < parts)
        def _():
            lax.fori_loop(t * (heads // parts), (t + 1) * (heads // parts), head, 0)

        @pl.when(t == parts)
        def _():
            def narrow(i, carry):
                some = pl.ds(pl.multiple_of(i * tokens, tokens), tokens)
                for k in range(LAT // LANES):
                    attn[some, k * LANES : (k + 1) * LANES] = wide[k, some, :].astype(bf16)
                return carry

            lax.fori_loop(0, heads, narrow, 0)
            attn_copy.start()

        @pl.when(t == 2)
        def _():
            local_gate.wait()
            local_up.wait()
            wait_in(gu.at[mate_in, gate_cols], w_recv.at[0])
            wait_in(gu.at[mate_in, up_cols], w_recv.at[1])

        at(2, stage_up, packed)
        at(3, stage_hid, packed)

        @pl.when(t == 3)
        def _():
            local_down.wait()
            wait_in(dn.at[unit_rows(left, 0, units), own_out], w_recv.at[2])
            wait_in(dn.at[unit_rows(right, 0, units), own_out], w_recv.at[3])
            wait_in(dn.at[unit_rows(opposite, 0, halfu), own_out], w_recv.at[6])
            wait_in(dn.at[unit_rows(opposite, halfu, halfu), own_out], w_recv.at[7])
            down_to_mate.start()

        @pl.when(t == 4)
        def _():
            wait_in(dn.at[:, mate_out], w_recv.at[8])

        at(4, stage_down, sent)

        @pl.when(lax.rem(t, 2) == 0)
        def _():
            @pl.when((t >= 10) & (t < 10 + 2 * early))
            def _():
                stage_combine(lax.div(t - 10, 2))

        return carry

    lax.fori_loop(0, sent + 4, step, 0)

    def finish(at, carry):
        stage_combine(at)
        return carry

    lax.fori_loop(early, nz, finish, 0)
    out_ref[...] = acc[...].astype(out_ref.dtype)

    attn_copy.wait()
    lat_copy.wait_send()
    for copy in to_side + to_mate + relays + [down_to_mate]:
        copy.wait_send()

    def drain(c, carry):
        for copy in x_copies(c) + x_relays(c) + h_copies(c) + h_relays(c):
            copy.wait_send()
        return carry

    lax.fori_loop(0, packed, drain, 0)

    def drain_sent(c, carry):
        def some():
            wait_in(disp.at[other_blocks(c)], disp_send.at[c])
            wait_in(outb.at[other_blocks(c)], ret_send.at[c])

        def whole():
            wait_in(disp.at[chunk_rows(c)], disp_send.at[c])
            wait_in(outb.at[chunk_rows(c)], ret_send.at[c])

        per_chunk(c, some, whole)
        return carry

    lax.fori_loop(0, sent, drain_sent, 0)


def layer(nz, ny, ids, scores, tok, gate, up, down, query, latent, docs):
    tokens, width = tok.shape
    units = gate.shape[1]
    piece = down.shape[1] // NX
    experts = nz * ny
    count, packed = experts * SLOTS, experts * CAP
    sent_n, packed_n = count // CHUNK, packed // CHUNK
    heads, feats, _ = query.shape
    vmem = pl.BlockSpec(memory_space=pltpu.VMEM)
    away = pl.BlockSpec(memory_space=pl.ANY)
    bf16 = jnp.bfloat16
    dma = pltpu.SemaphoreType.DMA
    return pl.pallas_call(
        functools.partial(layer_kernel, nz, ny),
        out_shape=(
            jax.ShapeDtypeStruct((tokens, width), bf16),
            jax.ShapeDtypeStruct((tokens * heads, LAT), bf16),
        ),
        in_specs=[away] * 9,
        out_specs=(vmem, away),
        scratch_shapes=[
            pltpu.VMEM((count, width), bf16),
            pltpu.VMEM((count, width), bf16),
            pltpu.VMEM((NX, packed, width), bf16),
            pltpu.VMEM((NX * width, 2 * units), bf16),
            pltpu.VMEM((NX * units, width), bf16),
            pltpu.VMEM((2, units // 2, piece), bf16),
            pltpu.VMEM((packed + 2 * CHUNK, NX * units), bf16),
            pltpu.VMEM((count, width), bf16),
            pltpu.VMEM((count, width), bf16),
            pltpu.VMEM((tokens, width), jnp.float32),
            pltpu.VMEM((experts, tokens), bf16),
            pltpu.VMEM((experts, tokens), bf16),
            pltpu.VMEM((experts, tokens), bf16),
            pltpu.VMEM((heads, feats, tokens), bf16),
            pltpu.VMEM((LAT // LANES, tokens * heads, LANES), jnp.float32),
            pltpu.VMEM((tokens * heads, LAT), bf16),
            pltpu.VMEM((2 * tokens, feats), bf16),
            pltpu.VMEM((2 * tokens, tokens), jnp.float32),
            pltpu.VMEM(ids.shape, ids.dtype),
            pltpu.VMEM(scores.shape, scores.dtype),
            pltpu.VMEM(tok.shape, tok.dtype),
            pltpu.VMEM(latent.shape, latent.dtype),
            pltpu.VMEM(docs.shape, docs.dtype),
            dma((5,)),
            dma((3,)),
            dma((2,)),
            dma((1,)),
            dma((1,)),
            dma((9,)),
            dma((9,)),
            dma((sent_n,)),
            dma((sent_n,)),
            dma((4, packed_n)),
            dma((4, packed_n)),
            dma((4, packed_n)),
            dma((4, packed_n)),
            dma((sent_n,)),
            dma((sent_n,)),
        ],
        compiler_params=pltpu.CompilerParams(
            collective_id=0, has_side_effects=True, vmem_limit_bytes=58 * 1024 * 1024
        ),
        name="layer",
    )(ids, scores, tok, gate, up, down, query, latent, docs)


def copy_kernel(first_in, second_in, first_out, second_out, first, second, in_sem, out_sem):
    rows = first_in.shape[0] // PIECES
    pieces = []
    for k in range(PIECES):
        part = pl.ds(k * rows, rows)
        pieces.append((first_in.at[part], first.at[part], first_out.at[part]))
    pieces.append((second_in, second, second_out))
    into, out = [], []
    for k, (source, held, target) in enumerate(pieces):
        into.append(pltpu.make_async_copy(source, held, in_sem.at[k]))
        out.append(pltpu.make_async_copy(held, target, out_sem.at[k]))
    for copy in into:
        copy.start()
    for arrival, departure in zip(into, out):
        arrival.wait()
        departure.start()
    for copy in out:
        copy.wait()


def handed_over(first, second):
    away = pl.BlockSpec(memory_space=pl.ANY)
    dma = pltpu.SemaphoreType.DMA
    return pl.pallas_call(
        copy_kernel,
        out_shape=tuple(jax.ShapeDtypeStruct(a.shape, a.dtype) for a in (first, second)),
        in_specs=[away, away],
        out_specs=(away, away),
        scratch_shapes=[
            pltpu.VMEM(first.shape, first.dtype),
            pltpu.VMEM(second.shape, second.dtype),
            dma((PIECES + 1,)),
            dma((PIECES + 1,)),
        ],
        compiler_params=pltpu.CompilerParams(vmem_limit_bytes=58 * 1024 * 1024),
        name="handed_over",
    )(first, second)


def shards(
    queries,
    latents,
    doc_ids,
    hidden_rows,
    expert_ids,
    gate_scores,
    gate_weight,
    up_weight,
    down_weight,
):
    length = lax.axis_size("dp")
    moe_out, attn_out = layer(
        length // (2 * NY),
        NY,
        expert_ids.T,
        gate_scores.T,
        hidden_rows,
        gate_weight[0],
        up_weight[0],
        down_weight[0],
        queries.transpose(1, 2, 0),
        latents.T,
        doc_ids.reshape(length, -1),
    )
    attn_out, moe_out = handed_over(attn_out, moe_out)
    return (attn_out.reshape(queries.shape[:2] + (LAT,)), moe_out)


def solution(mesh):
    placed = (
        P("dp", "mp", None),
        P("dp", None),
        P(),
        P("dp", "mp"),
        P("dp", None),
        P("dp", None),
        P("dp", None, "mp"),
        P("dp", None, "mp"),
        P("dp", "mp", None),
    )
    return jax.shard_map(
        shards,
        mesh=mesh,
        in_specs=placed,
        out_specs=(P("dp", "mp", None), P("dp", "mp")),
        check_vma=False,
    )
```

```python
import functools
import math

import jax
import jax.numpy as jnp
from jax import lax
from jax.experimental import pallas as pl
from jax.experimental.pallas import tpu as pltpu
from jax.sharding import PartitionSpec as P

LAT = 512
LANES = 128
PIECES = 8
SLOTS = 32
CAP = 30
CHUNK = 64
NX = 4
NY = 4
Z_ORDER = {8: (1, -2, 4, 3, -3, 2, -1, 0), 4: (0, 2, 1, -1), 2: (0, 1)}

score_scale = 1.0 / math.sqrt(192.0)
neg_large = -1e30
MESH = pl.DeviceIdType.MESH


def layer_kernel(
    nz,
    ny,
    ids_in,
    score_in,
    tok_in,
    gate_ref,
    up_ref,
    down_ref,
    query_ref,
    latent_in,
    doc_in,
    out_ref,
    attn_ref,
    disp,
    land,
    rows,
    gu,
    dn,
    relay_dn,
    hid,
    outb,
    ret,
    acc,
    place_ref,
    ghi_ref,
    glo_ref,
    scales,
    query,
    wide,
    attn,
    keys,
    bias,
    ids_ref,
    score_ref,
    tok_ref,
    latent_ref,
    doc_ref,
    in_sem,
    local_sem,
    q_sem,
    lat_send,
    lat_recv,
    w_send,
    w_recv,
    disp_send,
    disp_recv,
    x_send,
    x_recv,
    h_send,
    h_recv,
    ret_send,
    ret_recv,
):
    top, tokens = ids_in.shape
    heads = query_ref.shape[0]
    width = tok_in.shape[1]
    half_in, units = gate_ref.shape
    piece = down_ref.shape[1] // NX
    experts = nz * ny
    plane = ny * SLOTS
    chunk, half = CHUNK, CHUNK // 2
    per = CHUNK // SLOTS
    sent, packed = experts * SLOTS // chunk, experts * CAP // chunk
    own_chunk = Z_ORDER[nz].index(0) * (plane // chunk)
    f32, bf16 = jnp.float32, jnp.bfloat16

    d = lax.axis_index("dp")
    x = lax.axis_index("mp")
    s = lax.rem(d, 2)
    p = lax.div(d, 2)
    z = lax.div(p, ny)
    y = lax.rem(p, ny)
    right = lax.rem(x + 1, NX)
    left = lax.rem(x + NX - 1, NX)
    opposite = lax.rem(x + 2, NX)
    mate = d + 1 - 2 * s

    def dev(zz, yy):
        return (zz * ny + yy) * 2 + s

    def offset(c):
        total = 0
        for at, by in enumerate(Z_ORDER[nz]):
            total = total + jnp.where(c == at, by, 0)
        return total

    def remote(src, dst, send, recv, dd, xx):
        return pltpu.make_async_remote_copy(
            src_ref=src, dst_ref=dst, send_sem=send, recv_sem=recv,
            device_id=(dd, xx), device_id_type=MESH,
        )

    def wait_in(ref, sem):
        pltpu.make_async_copy(ref, ref, sem).wait()

    own_in = pl.ds(pl.multiple_of(s * half_in, half_in), half_in)
    mate_in = pl.ds(pl.multiple_of((1 - s) * half_in, half_in), half_in)
    own_out = pl.ds(pl.multiple_of(s * piece, piece), piece)
    mate_out = pl.ds(pl.multiple_of((1 - s) * piece, piece), piece)
    gate_cols, up_cols = pl.ds(0, units), pl.ds(units, units)

    def unit_rows(q, start, count):
        return pl.ds(pl.multiple_of(q * units + start, units // 2), count)

    def unit_cols(q):
        return pl.ds(pl.multiple_of(q * units, units), units)

    def down_cols(q):
        return pl.ds(pl.multiple_of(q * piece, piece), piece)

    local_gate = pltpu.make_async_copy(gate_ref, gu.at[own_in, gate_cols], local_sem.at[0])
    local_up = pltpu.make_async_copy(up_ref, gu.at[own_in, up_cols], local_sem.at[1])
    local_down = pltpu.make_async_copy(
        down_ref.at[:, down_cols(x)], dn.at[unit_rows(x, 0, units), own_out], local_sem.at[2]
    )
    local_query = pltpu.make_async_copy(query_ref, query, q_sem.at[0])
    inputs = [
        pltpu.make_async_copy(source, held, in_sem.at[k])
        for k, (source, held) in enumerate(
            (
                (ids_in, ids_ref),
                (score_in, score_ref),
                (tok_in, tok_ref),
                (latent_in, latent_ref),
                (doc_in, doc_ref),
            )
        )
    ]
    for copy in inputs:
        copy.start()

    barrier = pltpu.get_barrier_semaphore()

    def greet(dd, xx):
        pl.semaphore_signal(barrier, inc=1, device_id=(dd, xx), device_id_type=MESH)

    ring = experts * 2
    beside = lax.rem(d + 2 * s - 1 + ring, ring)
    following = lax.rem(d + 1, ring)
    greet(mate, x)
    greet(beside, x)
    greet(d, right)
    greet(d, left)

    def greet_peer(k, carry):
        greet(lax.rem(p + k, experts) * 2 + s, x)
        return carry

    lax.fori_loop(1, experts, greet_peer, 0)
    for copy in [local_gate, local_up, local_down, local_query]:
        copy.start()

    to_mate = [
        remote(gate_ref, gu.at[own_in, gate_cols], w_send.at[0], w_recv.at[0], mate, x),
        remote(up_ref, gu.at[own_in, up_cols], w_send.at[1], w_recv.at[1], mate, x),
    ]
    halfu = units // 2
    to_side = [
        remote(
            down_ref.at[:, down_cols(right)], dn.at[unit_rows(x, 0, units), own_out],
            w_send.at[2], w_recv.at[2], d, right,
        ),
        remote(
            down_ref.at[:, down_cols(left)], dn.at[unit_rows(x, 0, units), own_out],
            w_send.at[3], w_recv.at[3], d, left,
        ),
        remote(
            down_ref.at[pl.ds(0, halfu), down_cols(opposite)], relay_dn.at[0],
            w_send.at[4], w_recv.at[4], d, right,
        ),
        remote(
            down_ref.at[pl.ds(halfu, halfu), down_cols(opposite)], relay_dn.at[1],
            w_send.at[5], w_recv.at[5], d, left,
        ),
    ]
    relays = [
        remote(
            relay_dn.at[0], dn.at[unit_rows(left, 0, halfu), own_out],
            w_send.at[6], w_recv.at[6], d, right,
        ),
        remote(
            relay_dn.at[1], dn.at[unit_rows(right, halfu, halfu), own_out],
            w_send.at[7], w_recv.at[7], d, left,
        ),
    ]
    down_to_mate = remote(
        dn.at[:, own_out], dn.at[:, own_out], w_send.at[8], w_recv.at[8], mate, x
    )

    pl.semaphore_wait(barrier, experts - 1 + 4)
    for copy in to_side[:2] + to_mate + to_side[2:]:
        copy.start()

    for copy in inputs:
        copy.wait()

    expert_at = lax.broadcasted_iota(jnp.int32, (experts, tokens), 0)
    named = jnp.zeros((experts, tokens), f32)
    weight = jnp.zeros((experts, tokens), f32)
    for k in range(top):
        hit = ids_ref[k : k + 1, :] == expert_at
        named = named + jnp.where(hit, 1.0, 0.0)
        weight = weight + jnp.where(hit, score_ref[k : k + 1, :], 0.0)
    row_at = lax.broadcasted_iota(jnp.int32, (tokens, tokens), 0)
    col_at = lax.broadcasted_iota(jnp.int32, (tokens, tokens), 1)
    before = jnp.dot(
        named.astype(bf16),
        jnp.where(row_at < col_at, 1.0, 0.0).astype(bf16),
        preferred_element_type=f32,
    )
    place_ref[...] = jnp.where(named > 0.5, before, -1.0).astype(bf16)
    whole = weight.astype(bf16)
    ghi_ref[...] = whole
    glo_ref[...] = (weight - whole.astype(f32)).astype(bf16)

    def chunk_rows(c):
        return pl.ds(pl.multiple_of(c * chunk, chunk), chunk)

    def block_rows(b):
        return pl.ds(pl.multiple_of(b * SLOTS, SLOTS), SLOTS)

    def peer(b, way):
        zz = lax.rem(z + way * offset(lax.div(b, ny)) + nz, nz)
        return dev(zz, lax.rem(y + way * lax.rem(b, ny) + ny, ny))

    def spread(at, first, count):
        zz = lax.rem(z + offset(at) + nz, nz)
        row = lax.broadcasted_iota(jnp.int32, (count, experts), 0)
        dest = zz * ny + ((y + first + (row // SLOTS)) % ny)
        return jnp.where(
            lax.broadcasted_iota(jnp.int32, (count, experts), 1) == dest, 1.0, 0.0
        ).astype(bf16)

    def chosen(sel):
        count = sel.shape[0]
        slot = (lax.broadcasted_iota(jnp.int32, (count, tokens), 0) % SLOTS).astype(f32)
        return jnp.dot(sel, place_ref[...], preferred_element_type=f32) == slot

    def build(c):
        first = c * per
        sel = spread(lax.div(first, ny), lax.rem(first, ny), chunk)
        pick = jnp.where(chosen(sel), 1.0, 0.0).astype(bf16)
        block = jnp.dot(pick, tok_ref[...], preferred_element_type=f32).astype(bf16)
        disp[chunk_rows(c), :] = block

    def disp_copy(c, i):
        b = c * per + i
        return remote(
            disp.at[block_rows(b)], land.at[block_rows(b)],
            disp_send.at[c], disp_recv.at[c], peer(b, 1), x,
        )

    def own_block(c):
        return pl.ds(pl.multiple_of(c * chunk, chunk), SLOTS)

    def other_blocks(c):
        return pl.ds(pl.multiple_of(c * chunk + SLOTS, SLOTS), chunk - SLOTS)

    def per_chunk(c, yes, no):
        pl.when(c == own_chunk)(yes)
        pl.when(c != own_chunk)(no)

    def dispatch(c):
        for i in range(1, per):
            disp_copy(c, i).start()

        def keep():
            land[own_block(c), :] = disp[own_block(c), :]

        per_chunk(c, keep, lambda: disp_copy(c, 0).start())

    ahead = min(6, sent)
    for c in range(ahead):
        build(jnp.int32(c))
        dispatch(jnp.int32(c))

    same = row_at == col_at
    keys[tokens:, :] = lax.dot_general(
        jnp.where(same, 1.0, 0.0).astype(bf16), latent_ref[...], (((1,), (1,)), ((), ())),
        preferred_element_type=f32,
    ).astype(bf16)
    lat_copy = remote(
        keys.at[pl.ds(tokens, tokens)], keys.at[pl.ds(0, tokens)],
        lat_send.at[0], lat_recv.at[0], following, x,
    )
    own_ids = doc_ref[pl.ds(d, 1), :]
    old_ids = doc_ref[pl.ds(lax.rem(d + ring - 1, ring), 1), :]
    own_col = jnp.sum(jnp.where(same, own_ids, 0).astype(f32), axis=1, keepdims=True)
    old_col = jnp.sum(jnp.where(same, old_ids, 0).astype(f32), axis=1, keepdims=True)
    old_col = old_col - jnp.where(d == 0, 1000.0, 0.0)
    ids_row = own_ids.astype(f32)
    bias[:tokens, :] = jnp.where(old_col == ids_row, 0.0, neg_large)
    bias[tokens:, :] = jnp.where((own_col == ids_row) & (row_at <= col_at), 0.0, neg_large)
    lat_copy.start()

    def first_half(c):
        return pl.ds(pl.multiple_of(c * chunk, chunk), half)

    def second_half(c):
        return pl.ds(pl.multiple_of(c * chunk + half, half), half)

    def x_copies(c):
        here = rows.at[x, chunk_rows(c)]
        return (
            remote(here, here, x_send.at[0, c], x_recv.at[0, c], d, right),
            remote(here, here, x_send.at[1, c], x_recv.at[1, c], d, left),
        )

    def x_relays(c):
        from_left, from_right = rows.at[left, first_half(c)], rows.at[right, second_half(c)]
        return (
            remote(from_left, from_left, x_send.at[2, c], x_recv.at[2, c], d, right),
            remote(from_right, from_right, x_send.at[3, c], x_recv.at[3, c], d, left),
        )

    def h_copies(c):
        here = hid.at[chunk_rows(c + 1), unit_cols(x)]
        return (
            remote(here, here, h_send.at[0, c], h_recv.at[0, c], d, right),
            remote(here, here, h_send.at[1, c], h_recv.at[1, c], d, left),
        )

    def h_relays(c):
        from_left = hid.at[first_half(c + 1), unit_cols(left)]
        from_right = hid.at[second_half(c + 1), unit_cols(right)]
        return (
            remote(from_left, from_left, h_send.at[2, c], h_recv.at[2, c], d, right),
            remote(from_right, from_right, h_send.at[3, c], h_recv.at[3, c], d, left),
        )

    def ret_copy(c, i):
        b = c * per + i
        return remote(
            outb.at[block_rows(b)], ret.at[block_rows(b)],
            ret_send.at[c], ret_recv.at[c], peer(b, -1), x,
        )

    def arrived(c):
        per_chunk(
            c,
            lambda: wait_in(land.at[other_blocks(c)], disp_recv.at[c]),
            lambda: wait_in(land.at[chunk_rows(c)], disp_recv.at[c]),
        )

    def stage_pack(c):
        @pl.when(c == 0)
        def _():
            arrived(c)

        arrived(c + 1)
        row = lax.broadcasted_iota(jnp.int32, (chunk, 2 * chunk), 0)
        col = lax.broadcasted_iota(jnp.int32, (chunk, 2 * chunk), 1)
        take = col == row + (SLOTS - CAP) * ((row + c * chunk) // CAP)
        window = land[pl.ds(pl.multiple_of(c * chunk, chunk), 2 * chunk), :]
        rows[x, chunk_rows(c), :] = jnp.dot(
            jnp.where(take, 1.0, 0.0).astype(bf16), window, preferred_element_type=f32
        ).astype(bf16)
        for copy in x_copies(c):
            copy.start()

    def stage_relay(c):
        wait_in(rows.at[left, chunk_rows(c)], x_recv.at[0, c])
        wait_in(rows.at[right, chunk_rows(c)], x_recv.at[1, c])
        for copy in x_relays(c):
            copy.start()

    def stage_up(c):
        wait_in(rows.at[opposite, first_half(c)], x_recv.at[2, c])
        wait_in(rows.at[opposite, second_half(c)], x_recv.at[3, c])
        total = jnp.zeros((chunk, 2 * units), f32)
        for m in range(NX):
            total = total + jnp.dot(
                rows[m, chunk_rows(c), :], gu[m * width : (m + 1) * width, :],
                preferred_element_type=f32,
            )
        gate, upper = total[:, :units], total[:, units:]
        hid[chunk_rows(c + 1), unit_cols(x)] = (gate / (1.0 + jnp.exp(-gate)) * upper).astype(bf16)
        for copy in h_copies(c):
            copy.start()

    def stage_hid(c):
        wait_in(hid.at[chunk_rows(c + 1), unit_cols(left)], h_recv.at[0, c])
        wait_in(hid.at[chunk_rows(c + 1), unit_cols(right)], h_recv.at[1, c])
        for copy in h_relays(c):
            copy.start()

    def stage_down(c):
        @pl.when(c < packed)
        def _():
            wait_in(hid.at[first_half(c + 1), unit_cols(opposite)], h_recv.at[2, c])
            wait_in(hid.at[second_half(c + 1), unit_cols(opposite)], h_recv.at[3, c])

        row = lax.broadcasted_iota(jnp.int32, (chunk, 2 * chunk), 0)
        col = lax.broadcasted_iota(jnp.int32, (chunk, 2 * chunk), 1)
        place = c * chunk + row
        take = (col + (c - 1) * chunk == place - (SLOTS - CAP) * (place // SLOTS)) & (row % SLOTS < CAP)
        window = hid[pl.ds(pl.multiple_of(c * chunk, chunk), 2 * chunk), :]
        value = jnp.dot(
            jnp.where(take, 1.0, 0.0).astype(bf16), window, preferred_element_type=f32
        ).astype(bf16)
        outb[chunk_rows(c), :] = jnp.dot(value, dn[...], preferred_element_type=f32).astype(bf16)
        for i in range(1, per):
            ret_copy(c, i).start()

        def keep():
            ret[own_block(c), :] = outb[own_block(c), :]

        per_chunk(c, keep, lambda: ret_copy(c, 0).start())

    def stage_combine(at):
        for i in range(plane // chunk):
            c = at * (plane // chunk) + i
            per_chunk(
                c,
                lambda c=c: wait_in(ret.at[other_blocks(c)], ret_recv.at[c]),
                lambda c=c: wait_in(ret.at[chunk_rows(c)], ret_recv.at[c]),
            )
        back = ret[pl.ds(pl.multiple_of(at * plane, plane), plane), :]
        total = acc[...]
        for k in range(2):
            total = total + jnp.dot(scales[at, k], back, preferred_element_type=f32)
        acc[...] = total

    def stage_scales(at):
        sel = spread(at, 0, plane)
        taken = chosen(sel)
        for k, part in enumerate((ghi_ref, glo_ref)):
            scale = jnp.dot(sel, part[...], preferred_element_type=f32)
            scales[at, k] = jnp.where(taken, scale, 0.0).T.astype(bf16)

    hid[:chunk, :] = jnp.zeros((chunk, hid.shape[1]), bf16)
    hid[(packed + 1) * chunk :, :] = jnp.zeros((chunk, hid.shape[1]), bf16)
    acc[...] = jnp.zeros_like(acc)

    def head(h, carry):
        scores = jnp.dot(keys[...], query[h], preferred_element_type=f32) * score_scale + bias[...]
        lifted = jnp.exp(scores - jnp.max(scores, axis=0, keepdims=True))
        probs = (lifted / jnp.sum(lifted, axis=0, keepdims=True)).astype(bf16)
        value = lax.dot_general(
            probs, keys[:, :LAT], (((0,), (0,)), ((), ())), preferred_element_type=f32
        )
        for k in range(LAT // LANES):
            wide[k, pl.ds(h, tokens, stride=heads), :] = value[:, k * LANES : (k + 1) * LANES]
        return carry

    parts = min(4, sent)
    attn_copy = pltpu.make_async_copy(attn, attn_ref, q_sem.at[1])
    early = min(5, nz)

    def step(t, carry):
        def at(delay, stage, count):
            @pl.when((t >= delay) & (t < delay + count))
            def _():
                stage(t - delay)

        at(0, stage_pack, packed)

        @pl.when(t + ahead < sent)
        def _():
            build(t + ahead)
            dispatch(t + ahead)

        at(1, stage_relay, packed)

        @pl.when(t == 2)
        def _():
            wait_in(relay_dn.at[0], w_recv.at[4])
            wait_in(relay_dn.at[1], w_recv.at[5])
            for copy in relays:
                copy.start()

        @pl.when(t == 1)
        def _():
            local_query.wait()
            wait_in(keys.at[pl.ds(0, tokens)], lat_recv.at[0])

        @pl.when((t >= 1) & (t < 1 + parts))
        def _():
            lax.fori_loop((t - 1) * (heads // parts), t * (heads // parts), head, 0)

        at(2, stage_scales, nz)

        @pl.when(t == 1 + parts)
        def _():
            def narrow(i, carry):
                some = pl.ds(pl.multiple_of(i * tokens, tokens), tokens)
                for k in range(LAT // LANES):
                    attn[some, k * LANES : (k + 1) * LANES] = wide[k, some, :].astype(bf16)
                return carry

            lax.fori_loop(0, heads, narrow, 0)
            attn_copy.start()

        @pl.when(t == 2)
        def _():
            local_gate.wait()
            local_up.wait()
            wait_in(gu.at[mate_in, gate_cols], w_recv.at[0])
            wait_in(gu.at[mate_in, up_cols], w_recv.at[1])

        at(2, stage_up, packed)
        at(3, stage_hid, packed)

        @pl.when(t == 3)
        def _():
            local_down.wait()
            wait_in(dn.at[unit_rows(left, 0, units), own_out], w_recv.at[2])
            wait_in(dn.at[unit_rows(right, 0, units), own_out], w_recv.at[3])
            wait_in(dn.at[unit_rows(opposite, 0, halfu), own_out], w_recv.at[6])
            wait_in(dn.at[unit_rows(opposite, halfu, halfu), own_out], w_recv.at[7])
            down_to_mate.start()

        @pl.when(t == 4)
        def _():
            wait_in(dn.at[:, mate_out], w_recv.at[8])

        at(4, stage_down, sent)

        @pl.when(lax.rem(t, 2) == 0)
        def _():
            @pl.when((t >= 10) & (t < 10 + 2 * early))
            def _():
                stage_combine(lax.div(t - 10, 2))

        return carry

    lax.fori_loop(0, sent + 4, step, 0)

    def finish(at, carry):
        stage_combine(at)
        return carry

    lax.fori_loop(early, nz, finish, 0)
    out_ref[...] = acc[...].astype(out_ref.dtype)

    attn_copy.wait()
    lat_copy.wait_send()
    for copy in to_side + to_mate + relays + [down_to_mate]:
        copy.wait_send()

    def drain(c, carry):
        for copy in x_copies(c) + x_relays(c) + h_copies(c) + h_relays(c):
            copy.wait_send()
        return carry

    lax.fori_loop(0, packed, drain, 0)

    def drain_sent(c, carry):
        def some():
            wait_in(disp.at[other_blocks(c)], disp_send.at[c])
            wait_in(outb.at[other_blocks(c)], ret_send.at[c])

        def whole():
            wait_in(disp.at[chunk_rows(c)], disp_send.at[c])
            wait_in(outb.at[chunk_rows(c)], ret_send.at[c])

        per_chunk(c, some, whole)
        return carry

    lax.fori_loop(0, sent, drain_sent, 0)


def layer(nz, ny, ids, scores, tok, gate, up, down, query, latent, docs):
    tokens, width = tok.shape
    units = gate.shape[1]
    piece = down.shape[1] // NX
    experts = nz * ny
    count, packed = experts * SLOTS, experts * CAP
    sent_n, packed_n = count // CHUNK, packed // CHUNK
    heads, feats, _ = query.shape
    vmem = pl.BlockSpec(memory_space=pltpu.VMEM)
    away = pl.BlockSpec(memory_space=pl.ANY)
    bf16 = jnp.bfloat16
    dma = pltpu.SemaphoreType.DMA
    return pl.pallas_call(
        functools.partial(layer_kernel, nz, ny),
        out_shape=(
            jax.ShapeDtypeStruct((tokens, width), bf16),
            jax.ShapeDtypeStruct((tokens * heads, LAT), bf16),
        ),
        in_specs=[away] * 9,
        out_specs=(vmem, away),
        scratch_shapes=[
            pltpu.VMEM((count, width), bf16),
            pltpu.VMEM((count, width), bf16),
            pltpu.VMEM((NX, packed, width), bf16),
            pltpu.VMEM((NX * width, 2 * units), bf16),
            pltpu.VMEM((NX * units, width), bf16),
            pltpu.VMEM((2, units // 2, piece), bf16),
            pltpu.VMEM((packed + 2 * CHUNK, NX * units), bf16),
            pltpu.VMEM((count, width), bf16),
            pltpu.VMEM((count, width), bf16),
            pltpu.VMEM((tokens, width), jnp.float32),
            pltpu.VMEM((experts, tokens), bf16),
            pltpu.VMEM((experts, tokens), bf16),
            pltpu.VMEM((experts, tokens), bf16),
            pltpu.VMEM((nz, 2, tokens, ny * SLOTS), bf16),
            pltpu.VMEM((heads, feats, tokens), bf16),
            pltpu.VMEM((LAT // LANES, tokens * heads, LANES), jnp.float32),
            pltpu.VMEM((tokens * heads, LAT), bf16),
            pltpu.VMEM((2 * tokens, feats), bf16),
            pltpu.VMEM((2 * tokens, tokens), jnp.float32),
            pltpu.VMEM(ids.shape, ids.dtype),
            pltpu.VMEM(scores.shape, scores.dtype),
            pltpu.VMEM(tok.shape, tok.dtype),
            pltpu.VMEM(latent.shape, latent.dtype),
            pltpu.VMEM(docs.shape, docs.dtype),
            dma((5,)),
            dma((3,)),
            dma((2,)),
            dma((1,)),
            dma((1,)),
            dma((9,)),
            dma((9,)),
            dma((sent_n,)),
            dma((sent_n,)),
            dma((4, packed_n)),
            dma((4, packed_n)),
            dma((4, packed_n)),
            dma((4, packed_n)),
            dma((sent_n,)),
            dma((sent_n,)),
        ],
        compiler_params=pltpu.CompilerParams(
            collective_id=0, has_side_effects=True, vmem_limit_bytes=58 * 1024 * 1024
        ),
        name="layer",
    )(ids, scores, tok, gate, up, down, query, latent, docs)


def copy_kernel(first_in, second_in, first_out, second_out, first, second, in_sem, out_sem):
    rows = first_in.shape[0] // PIECES
    pieces = []
    for k in range(PIECES):
        part = pl.ds(k * rows, rows)
        pieces.append((first_in.at[part], first.at[part], first_out.at[part]))
    pieces.append((second_in, second, second_out))
    into, out = [], []
    for k, (source, held, target) in enumerate(pieces):
        into.append(pltpu.make_async_copy(source, held, in_sem.at[k]))
        out.append(pltpu.make_async_copy(held, target, out_sem.at[k]))
    for copy in into:
        copy.start()
    for arrival, departure in zip(into, out):
        arrival.wait()
        departure.start()
    for copy in out:
        copy.wait()


def handed_over(first, second):
    away = pl.BlockSpec(memory_space=pl.ANY)
    dma = pltpu.SemaphoreType.DMA
    return pl.pallas_call(
        copy_kernel,
        out_shape=tuple(jax.ShapeDtypeStruct(a.shape, a.dtype) for a in (first, second)),
        in_specs=[away, away],
        out_specs=(away, away),
        scratch_shapes=[
            pltpu.VMEM(first.shape, first.dtype),
            pltpu.VMEM(second.shape, second.dtype),
            dma((PIECES + 1,)),
            dma((PIECES + 1,)),
        ],
        compiler_params=pltpu.CompilerParams(vmem_limit_bytes=58 * 1024 * 1024),
        name="handed_over",
    )(first, second)


def shards(
    queries,
    latents,
    doc_ids,
    hidden_rows,
    expert_ids,
    gate_scores,
    gate_weight,
    up_weight,
    down_weight,
):
    length = lax.axis_size("dp")
    moe_out, attn_out = layer(
        length // (2 * NY),
        NY,
        expert_ids.T,
        gate_scores.T,
        hidden_rows,
        gate_weight[0],
        up_weight[0],
        down_weight[0],
        queries.transpose(1, 2, 0),
        latents.T,
        doc_ids.reshape(length, -1),
    )
    attn_out, moe_out = handed_over(attn_out, moe_out)
    return (attn_out.reshape(queries.shape[:2] + (LAT,)), moe_out)


def solution(mesh):
    placed = (
        P("dp", "mp", None),
        P("dp", None),
        P(),
        P("dp", "mp"),
        P("dp", None),
        P("dp", None),
        P("dp", None, "mp"),
        P("dp", None, "mp"),
        P("dp", "mp", None),
    )
    return jax.shard_map(
        shards,
        mesh=mesh,
        in_specs=placed,
        out_specs=(P("dp", "mp", None), P("dp", "mp")),
        check_vma=False,
    )
```

```python
import functools
import math

import jax
import jax.numpy as jnp
from jax import lax
from jax.experimental import pallas as pl
from jax.experimental.pallas import tpu as pltpu
from jax.sharding import PartitionSpec as P

LAT = 512
LANES = 128
PIECES = 8
SLOTS = 32
CAP = 30
SLOT_BITS = 5
CAP_TIMES, CAP_SHIFT = 34953, 20
assert all(n * CAP_TIMES >> CAP_SHIFT == n // CAP for n in range(2048))
CHUNK = 64
NX = 4
NY = 4
COMBINE_AT = ((10, 0), (13, 1), (17, 3))
COMBINE_LAST = (2, 4, 5, 6, 7)
Z_ORDER = {8: (1, -2, 4, 2, -3, 3, -1, 0), 4: (0, 2, 1, -1), 2: (0, 1)}

score_scale = 1.0 / math.sqrt(192.0)
neg_large = -1e30
MESH = pl.DeviceIdType.MESH


def layer_kernel(
    nz,
    ny,
    ids_in,
    score_in,
    tok_in,
    gate_ref,
    up_ref,
    down_ref,
    query_ref,
    latent_in,
    doc_in,
    out_ref,
    attn_ref,
    disp,
    land,
    rows,
    gu,
    dn,
    relay_dn,
    hid,
    outb,
    ret,
    acc,
    place_ref,
    ghi_ref,
    glo_ref,
    scales,
    query,
    wide,
    attn,
    keys,
    bias,
    ids_ref,
    score_ref,
    tok_ref,
    latent_ref,
    doc_ref,
    in_sem,
    local_sem,
    q_sem,
    lat_send,
    lat_recv,
    w_send,
    w_recv,
    disp_send,
    disp_recv,
    x_send,
    x_recv,
    h_send,
    h_recv,
    ret_send,
    ret_recv,
):
    top, tokens = ids_in.shape
    heads = query_ref.shape[0]
    width = tok_in.shape[1]
    half_in, units = gate_ref.shape
    piece = down_ref.shape[1] // NX
    experts = nz * ny
    plane = ny * SLOTS
    chunk, half = CHUNK, CHUNK // 2
    per = CHUNK // SLOTS
    sent, packed = experts * SLOTS // chunk, experts * CAP // chunk
    own_chunk = Z_ORDER[nz].index(0) * (plane // chunk)
    f32, bf16 = jnp.float32, jnp.bfloat16

    d = lax.axis_index("dp")
    x = lax.axis_index("mp")
    s = lax.rem(d, 2)
    p = lax.div(d, 2)
    z = lax.div(p, ny)
    y = lax.rem(p, ny)
    right = lax.rem(x + 1, NX)
    left = lax.rem(x + NX - 1, NX)
    opposite = lax.rem(x + 2, NX)
    mate = d + 1 - 2 * s

    def dev(zz, yy):
        return (zz * ny + yy) * 2 + s

    def entry(table, i):
        total = 0
        for at, value in enumerate(table):
            total = total + jnp.where(i == at, value, 0)
        return total

    def offset(at):
        return entry(Z_ORDER[nz], at)

    def remote(src, dst, send, recv, dd, xx):
        return pltpu.make_async_remote_copy(
            src_ref=src, dst_ref=dst, send_sem=send, recv_sem=recv,
            device_id=(dd, xx), device_id_type=MESH,
        )

    def wait_in(ref, sem):
        pltpu.make_async_copy(ref, ref, sem).wait()

    own_in = pl.ds(pl.multiple_of(s * half_in, half_in), half_in)
    mate_in = pl.ds(pl.multiple_of((1 - s) * half_in, half_in), half_in)
    own_out = pl.ds(pl.multiple_of(s * piece, piece), piece)
    mate_out = pl.ds(pl.multiple_of((1 - s) * piece, piece), piece)
    gate_cols, up_cols = pl.ds(0, units), pl.ds(units, units)

    def unit_rows(q, start, count):
        return pl.ds(pl.multiple_of(q * units + start, units // 2), count)

    def unit_cols(q):
        return pl.ds(pl.multiple_of(q * units, units), units)

    def down_cols(q):
        return pl.ds(pl.multiple_of(q * piece, piece), piece)

    local_gate = pltpu.make_async_copy(gate_ref, gu.at[own_in, gate_cols], local_sem.at[0])
    local_up = pltpu.make_async_copy(up_ref, gu.at[own_in, up_cols], local_sem.at[1])
    local_down = pltpu.make_async_copy(
        down_ref.at[:, down_cols(x)], dn.at[unit_rows(x, 0, units), own_out], local_sem.at[2]
    )
    local_query = pltpu.make_async_copy(query_ref, query, q_sem.at[0])
    inputs = [
        pltpu.make_async_copy(source, held, in_sem.at[k])
        for k, (source, held) in enumerate(
            (
                (ids_in, ids_ref),
                (score_in, score_ref),
                (tok_in, tok_ref),
                (latent_in, latent_ref),
                (doc_in, doc_ref),
            )
        )
    ]
    for copy in inputs:
        copy.start()

    barrier = pltpu.get_barrier_semaphore()

    def greet(dd, xx):
        pl.semaphore_signal(barrier, inc=1, device_id=(dd, xx), device_id_type=MESH)

    ring = experts * 2
    beside = lax.rem(d + 2 * s - 1 + ring, ring)
    following = lax.rem(d + 1, ring)
    greet(mate, x)
    greet(beside, x)
    greet(d, right)
    greet(d, left)

    def greet_peer(k, carry):
        greet(lax.rem(p + k, experts) * 2 + s, x)
        return carry

    lax.fori_loop(1, experts, greet_peer, 0)
    for copy in [local_gate, local_up, local_down, local_query]:
        copy.start()

    to_mate = [
        remote(gate_ref, gu.at[own_in, gate_cols], w_send.at[0], w_recv.at[0], mate, x),
        remote(up_ref, gu.at[own_in, up_cols], w_send.at[1], w_recv.at[1], mate, x),
    ]
    halfu = units // 2
    to_side = [
        remote(
            down_ref.at[:, down_cols(right)], dn.at[unit_rows(x, 0, units), own_out],
            w_send.at[2], w_recv.at[2], d, right,
        ),
        remote(
            down_ref.at[:, down_cols(left)], dn.at[unit_rows(x, 0, units), own_out],
            w_send.at[3], w_recv.at[3], d, left,
        ),
        remote(
            down_ref.at[pl.ds(0, halfu), down_cols(opposite)], relay_dn.at[0],
            w_send.at[4], w_recv.at[4], d, right,
        ),
        remote(
            down_ref.at[pl.ds(halfu, halfu), down_cols(opposite)], relay_dn.at[1],
            w_send.at[5], w_recv.at[5], d, left,
        ),
    ]
    relays = [
        remote(
            relay_dn.at[0], dn.at[unit_rows(left, 0, halfu), own_out],
            w_send.at[6], w_recv.at[6], d, right,
        ),
        remote(
            relay_dn.at[1], dn.at[unit_rows(right, halfu, halfu), own_out],
            w_send.at[7], w_recv.at[7], d, left,
        ),
    ]
    down_to_mate = remote(
        dn.at[:, own_out], dn.at[:, own_out], w_send.at[8], w_recv.at[8], mate, x
    )

    pl.semaphore_wait(barrier, experts - 1 + 4)
    for copy in to_side[:2] + to_mate + to_side[2:]:
        copy.start()

    for copy in inputs:
        copy.wait()

    expert_at = lax.broadcasted_iota(jnp.int32, (experts, tokens), 0)
    named = jnp.zeros((experts, tokens), f32)
    weight = jnp.zeros((experts, tokens), f32)
    for k in range(top):
        hit = ids_ref[k : k + 1, :] == expert_at
        named = named + jnp.where(hit, 1.0, 0.0)
        weight = weight + jnp.where(hit, score_ref[k : k + 1, :], 0.0)
    row_at = lax.broadcasted_iota(jnp.int32, (tokens, tokens), 0)
    col_at = lax.broadcasted_iota(jnp.int32, (tokens, tokens), 1)
    before = jnp.dot(
        named.astype(bf16),
        jnp.where(row_at < col_at, 1.0, 0.0).astype(bf16),
        preferred_element_type=f32,
    )
    place_ref[...] = jnp.where(named > 0.5, before, -1.0).astype(bf16)
    whole = weight.astype(bf16)
    ghi_ref[...] = whole
    glo_ref[...] = (weight - whole.astype(f32)).astype(bf16)

    def chunk_rows(c):
        return pl.ds(pl.multiple_of(c * chunk, chunk), chunk)

    def block_rows(b):
        return pl.ds(pl.multiple_of(b * SLOTS, SLOTS), SLOTS)

    def peer(b, way):
        zz = lax.rem(z + way * offset(lax.div(b, ny)) + nz, nz)
        return dev(zz, lax.rem(y + way * lax.rem(b, ny) + ny, ny))

    def spread(at, first, count):
        zz = lax.rem(z + offset(at) + nz, nz)
        row = lax.broadcasted_iota(jnp.int32, (count, experts), 0)
        dest = zz * ny + ((y + first + (row >> SLOT_BITS)) & (ny - 1))
        return jnp.where(
            lax.broadcasted_iota(jnp.int32, (count, experts), 1) == dest, 1.0, 0.0
        ).astype(bf16)

    def chosen(sel):
        count = sel.shape[0]
        slot = (lax.broadcasted_iota(jnp.int32, (count, tokens), 0) & (SLOTS - 1)).astype(f32)
        return jnp.dot(sel, place_ref[...], preferred_element_type=f32) == slot

    def build(c):
        first = c * per
        sel = spread(lax.div(first, ny), lax.rem(first, ny), chunk)
        pick = jnp.where(chosen(sel), 1.0, 0.0).astype(bf16)
        block = jnp.dot(pick, tok_ref[...], preferred_element_type=f32).astype(bf16)
        disp[chunk_rows(c), :] = block

    def disp_copy(c, i):
        b = c * per + i
        return remote(
            disp.at[block_rows(b)], land.at[block_rows(b)],
            disp_send.at[c], disp_recv.at[c], peer(b, 1), x,
        )

    def own_block(c):
        return pl.ds(pl.multiple_of(c * chunk, chunk), SLOTS)

    def other_blocks(c):
        return pl.ds(pl.multiple_of(c * chunk + SLOTS, SLOTS), chunk - SLOTS)

    def per_chunk(c, yes, no):
        pl.when(c == own_chunk)(yes)
        pl.when(c != own_chunk)(no)

    def dispatch(c):
        for i in range(1, per):
            disp_copy(c, i).start()

        def keep():
            land[own_block(c), :] = disp[own_block(c), :]

        per_chunk(c, keep, lambda: disp_copy(c, 0).start())

    ahead = min(6, sent)
    for c in range(ahead):
        build(jnp.int32(c))
        dispatch(jnp.int32(c))

    same = row_at == col_at
    keys[tokens:, :] = lax.dot_general(
        jnp.where(same, 1.0, 0.0).astype(bf16), latent_ref[...], (((1,), (1,)), ((), ())),
        preferred_element_type=f32,
    ).astype(bf16)
    lat_copy = remote(
        keys.at[pl.ds(tokens, tokens)], keys.at[pl.ds(0, tokens)],
        lat_send.at[0], lat_recv.at[0], following, x,
    )
    own_ids = doc_ref[pl.ds(d, 1), :]
    old_ids = doc_ref[pl.ds(lax.rem(d + ring - 1, ring), 1), :]
    own_col = jnp.sum(jnp.where(same, own_ids, 0).astype(f32), axis=1, keepdims=True)
    old_col = jnp.sum(jnp.where(same, old_ids, 0).astype(f32), axis=1, keepdims=True)
    old_col = old_col - jnp.where(d == 0, 1000.0, 0.0)
    ids_row = own_ids.astype(f32)
    bias[:tokens, :] = jnp.where(old_col == ids_row, 0.0, neg_large)
    bias[tokens:, :] = jnp.where((own_col == ids_row) & (row_at <= col_at), 0.0, neg_large)
    lat_copy.start()

    def first_half(c):
        return pl.ds(pl.multiple_of(c * chunk, chunk), half)

    def second_half(c):
        return pl.ds(pl.multiple_of(c * chunk + half, half), half)

    def x_copies(c):
        here = rows.at[x, chunk_rows(c)]
        return (
            remote(here, here, x_send.at[0, c], x_recv.at[0, c], d, right),
            remote(here, here, x_send.at[1, c], x_recv.at[1, c], d, left),
        )

    def x_relays(c):
        from_left, from_right = rows.at[left, first_half(c)], rows.at[right, second_half(c)]
        return (
            remote(from_left, from_left, x_send.at[2, c], x_recv.at[2, c], d, right),
            remote(from_right, from_right, x_send.at[3, c], x_recv.at[3, c], d, left),
        )

    def h_copies(c):
        here = hid.at[chunk_rows(c + 1), unit_cols(x)]
        return (
            remote(here, here, h_send.at[0, c], h_recv.at[0, c], d, right),
            remote(here, here, h_send.at[1, c], h_recv.at[1, c], d, left),
        )

    def h_relays(c):
        from_left = hid.at[first_half(c + 1), unit_cols(left)]
        from_right = hid.at[second_half(c + 1), unit_cols(right)]
        return (
            remote(from_left, from_left, h_send.at[2, c], h_recv.at[2, c], d, right),
            remote(from_right, from_right, h_send.at[3, c], h_recv.at[3, c], d, left),
        )

    def ret_copy(c, i):
        b = c * per + i
        return remote(
            outb.at[block_rows(b)], ret.at[block_rows(b)],
            ret_send.at[c], ret_recv.at[c], peer(b, -1), x,
        )

    def arrived(c):
        per_chunk(
            c,
            lambda: wait_in(land.at[other_blocks(c)], disp_recv.at[c]),
            lambda: wait_in(land.at[chunk_rows(c)], disp_recv.at[c]),
        )

    def stage_pack(c):
        @pl.when(c == 0)
        def _():
            arrived(c)

        arrived(c + 1)
        row = lax.broadcasted_iota(jnp.int32, (chunk, 2 * chunk), 0)
        col = lax.broadcasted_iota(jnp.int32, (chunk, 2 * chunk), 1)
        block = ((row + c * chunk) * CAP_TIMES) >> CAP_SHIFT
        take = col == row + (SLOTS - CAP) * block
        window = land[pl.ds(pl.multiple_of(c * chunk, chunk), 2 * chunk), :]
        rows[x, chunk_rows(c), :] = jnp.dot(
            jnp.where(take, 1.0, 0.0).astype(bf16), window, preferred_element_type=f32
        ).astype(bf16)
        for copy in x_copies(c):
            copy.start()

    def stage_relay(c):
        wait_in(rows.at[left, chunk_rows(c)], x_recv.at[0, c])
        wait_in(rows.at[right, chunk_rows(c)], x_recv.at[1, c])
        for copy in x_relays(c):
            copy.start()

    def stage_up(c):
        wait_in(rows.at[opposite, first_half(c)], x_recv.at[2, c])
        wait_in(rows.at[opposite, second_half(c)], x_recv.at[3, c])
        total = jnp.zeros((chunk, 2 * units), f32)
        for m in range(NX):
            total = total + jnp.dot(
                rows[m, chunk_rows(c), :], gu[m * width : (m + 1) * width, :],
                preferred_element_type=f32,
            )
        gate, upper = total[:, :units], total[:, units:]
        hid[chunk_rows(c + 1), unit_cols(x)] = (gate / (1.0 + jnp.exp(-gate)) * upper).astype(bf16)
        for copy in h_copies(c):
            copy.start()

    def stage_hid(c):
        wait_in(hid.at[chunk_rows(c + 1), unit_cols(left)], h_recv.at[0, c])
        wait_in(hid.at[chunk_rows(c + 1), unit_cols(right)], h_recv.at[1, c])
        for copy in h_relays(c):
            copy.start()

    def stage_down(c):
        @pl.when(c < packed)
        def _():
            wait_in(hid.at[first_half(c + 1), unit_cols(opposite)], h_recv.at[2, c])
            wait_in(hid.at[second_half(c + 1), unit_cols(opposite)], h_recv.at[3, c])

        row = lax.broadcasted_iota(jnp.int32, (chunk, 2 * chunk), 0)
        col = lax.broadcasted_iota(jnp.int32, (chunk, 2 * chunk), 1)
        place = c * chunk + row
        held = place - (SLOTS - CAP) * (place >> SLOT_BITS)
        take = (col + (c - 1) * chunk == held) & ((row & (SLOTS - 1)) < CAP)
        window = hid[pl.ds(pl.multiple_of(c * chunk, chunk), 2 * chunk), :]
        value = jnp.dot(
            jnp.where(take, 1.0, 0.0).astype(bf16), window, preferred_element_type=f32
        ).astype(bf16)
        outb[chunk_rows(c), :] = jnp.dot(value, dn[...], preferred_element_type=f32).astype(bf16)
        for i in range(1, per):
            ret_copy(c, i).start()

        def keep():
            ret[own_block(c), :] = outb[own_block(c), :]

        per_chunk(c, keep, lambda: ret_copy(c, 0).start())

    def stage_combine(at):
        for i in range(plane // chunk):
            c = at * (plane // chunk) + i
            per_chunk(
                c,
                lambda c=c: wait_in(ret.at[other_blocks(c)], ret_recv.at[c]),
                lambda c=c: wait_in(ret.at[chunk_rows(c)], ret_recv.at[c]),
            )
        back = ret[pl.ds(pl.multiple_of(at * plane, plane), plane), :]
        total = acc[...]
        for k in range(2):
            total = total + jnp.dot(scales[at, k], back, preferred_element_type=f32)
        acc[...] = total

    def stage_scales(at):
        sel = spread(at, 0, plane)
        taken = chosen(sel)
        for k, part in enumerate((ghi_ref, glo_ref)):
            scale = jnp.dot(sel, part[...], preferred_element_type=f32)
            scales[at, k] = jnp.where(taken, scale, 0.0).T.astype(bf16)

    hid[:chunk, :] = jnp.zeros((chunk, hid.shape[1]), bf16)
    hid[(packed + 1) * chunk :, :] = jnp.zeros((chunk, hid.shape[1]), bf16)
    acc[...] = jnp.zeros_like(acc)

    def head(h, carry):
        scores = jnp.dot(keys[...], query[h], preferred_element_type=f32) * score_scale + bias[...]
        lifted = jnp.exp(scores - jnp.max(scores, axis=0, keepdims=True))
        probs = (lifted / jnp.sum(lifted, axis=0, keepdims=True)).astype(bf16)
        value = lax.dot_general(
            probs, keys[:, :LAT], (((0,), (0,)), ((), ())), preferred_element_type=f32
        )
        for k in range(LAT // LANES):
            wide[k, pl.ds(h, tokens, stride=heads), :] = value[:, k * LANES : (k + 1) * LANES]
        return carry

    parts = min(4, sent)
    attn_copy = pltpu.make_async_copy(attn, attn_ref, q_sem.at[1])

    def step(t, carry):
        def at(delay, stage, count):
            @pl.when((t >= delay) & (t < delay + count))
            def _():
                stage(t - delay)

        at(0, stage_pack, packed)

        @pl.when(t + ahead < sent)
        def _():
            build(t + ahead)
            dispatch(t + ahead)

        at(1, stage_relay, packed)

        @pl.when(t == 2)
        def _():
            wait_in(relay_dn.at[0], w_recv.at[4])
            wait_in(relay_dn.at[1], w_recv.at[5])
            for copy in relays:
                copy.start()

        @pl.when(t == 1)
        def _():
            local_query.wait()
            wait_in(keys.at[pl.ds(0, tokens)], lat_recv.at[0])

        @pl.when((t >= 1) & (t < 1 + parts))
        def _():
            lax.fori_loop((t - 1) * (heads // parts), t * (heads // parts), head, 0)

        at(2, stage_scales, nz)

        @pl.when(t == 1 + parts)
        def _():
            def narrow(i, carry):
                some = pl.ds(pl.multiple_of(i * tokens, tokens), tokens)
                for k in range(LAT // LANES):
                    attn[some, k * LANES : (k + 1) * LANES] = wide[k, some, :].astype(bf16)
                return carry

            lax.fori_loop(0, heads, narrow, 0)
            attn_copy.start()

        @pl.when(t == 2)
        def _():
            local_gate.wait()
            local_up.wait()
            wait_in(gu.at[mate_in, gate_cols], w_recv.at[0])
            wait_in(gu.at[mate_in, up_cols], w_recv.at[1])

        at(2, stage_up, packed)
        at(3, stage_hid, packed)

        @pl.when(t == 3)
        def _():
            local_down.wait()
            wait_in(dn.at[unit_rows(left, 0, units), own_out], w_recv.at[2])
            wait_in(dn.at[unit_rows(right, 0, units), own_out], w_recv.at[3])
            wait_in(dn.at[unit_rows(opposite, 0, halfu), own_out], w_recv.at[6])
            wait_in(dn.at[unit_rows(opposite, halfu, halfu), own_out], w_recv.at[7])
            down_to_mate.start()

        @pl.when(t == 4)
        def _():
            wait_in(dn.at[:, mate_out], w_recv.at[8])

        at(4, stage_down, sent)

        for moment, k in COMBINE_AT:

            @pl.when(t == moment)
            def _(k=k):
                stage_combine(jnp.int32(k))

        return carry

    lax.fori_loop(0, sent + 4, step, 0)

    def finish(i, carry):
        stage_combine(entry(COMBINE_LAST, i))
        return carry

    lax.fori_loop(0, len(COMBINE_LAST), finish, 0)
    out_ref[...] = acc[...].astype(out_ref.dtype)

    attn_copy.wait()
    lat_copy.wait_send()
    for copy in to_side + to_mate + relays + [down_to_mate]:
        copy.wait_send()

    def drain(c, carry):
        for copy in x_copies(c) + x_relays(c) + h_copies(c) + h_relays(c):
            copy.wait_send()
        return carry

    lax.fori_loop(0, packed, drain, 0)

    def drain_sent(c, carry):
        def some():
            wait_in(disp.at[other_blocks(c)], disp_send.at[c])
            wait_in(outb.at[other_blocks(c)], ret_send.at[c])

        def whole():
            wait_in(disp.at[chunk_rows(c)], disp_send.at[c])
            wait_in(outb.at[chunk_rows(c)], ret_send.at[c])

        per_chunk(c, some, whole)
        return carry

    lax.fori_loop(0, sent, drain_sent, 0)


def layer(nz, ny, ids, scores, tok, gate, up, down, query, latent, docs):
    tokens, width = tok.shape
    units = gate.shape[1]
    piece = down.shape[1] // NX
    experts = nz * ny
    count, packed = experts * SLOTS, experts * CAP
    sent_n, packed_n = count // CHUNK, packed // CHUNK
    heads, feats, _ = query.shape
    vmem = pl.BlockSpec(memory_space=pltpu.VMEM)
    away = pl.BlockSpec(memory_space=pl.ANY)
    bf16 = jnp.bfloat16
    dma = pltpu.SemaphoreType.DMA
    return pl.pallas_call(
        functools.partial(layer_kernel, nz, ny),
        out_shape=(
            jax.ShapeDtypeStruct((tokens, width), bf16),
            jax.ShapeDtypeStruct((tokens * heads, LAT), bf16),
        ),
        in_specs=[away] * 9,
        out_specs=(vmem, away),
        scratch_shapes=[
            pltpu.VMEM((count, width), bf16),
            pltpu.VMEM((count, width), bf16),
            pltpu.VMEM((NX, packed, width), bf16),
            pltpu.VMEM((NX * width, 2 * units), bf16),
            pltpu.VMEM((NX * units, width), bf16),
            pltpu.VMEM((2, units // 2, piece), bf16),
            pltpu.VMEM((packed + 2 * CHUNK, NX * units), bf16),
            pltpu.VMEM((count, width), bf16),
            pltpu.VMEM((count, width), bf16),
            pltpu.VMEM((tokens, width), jnp.float32),
            pltpu.VMEM((experts, tokens), bf16),
            pltpu.VMEM((experts, tokens), bf16),
            pltpu.VMEM((experts, tokens), bf16),
            pltpu.VMEM((nz, 2, tokens, ny * SLOTS), bf16),
            pltpu.VMEM((heads, feats, tokens), bf16),
            pltpu.VMEM((LAT // LANES, tokens * heads, LANES), jnp.float32),
            pltpu.VMEM((tokens * heads, LAT), bf16),
            pltpu.VMEM((2 * tokens, feats), bf16),
            pltpu.VMEM((2 * tokens, tokens), jnp.float32),
            pltpu.VMEM(ids.shape, ids.dtype),
            pltpu.VMEM(scores.shape, scores.dtype),
            pltpu.VMEM(tok.shape, tok.dtype),
            pltpu.VMEM(latent.shape, latent.dtype),
            pltpu.VMEM(docs.shape, docs.dtype),
            dma((5,)),
            dma((3,)),
            dma((2,)),
            dma((1,)),
            dma((1,)),
            dma((9,)),
            dma((9,)),
            dma((sent_n,)),
            dma((sent_n,)),
            dma((4, packed_n)),
            dma((4, packed_n)),
            dma((4, packed_n)),
            dma((4, packed_n)),
            dma((sent_n,)),
            dma((sent_n,)),
        ],
        compiler_params=pltpu.CompilerParams(
            collective_id=0, has_side_effects=True, vmem_limit_bytes=58 * 1024 * 1024
        ),
        name="layer",
    )(ids, scores, tok, gate, up, down, query, latent, docs)


def copy_kernel(first_in, second_in, first_out, second_out, first, second, in_sem, out_sem):
    rows = first_in.shape[0] // PIECES
    pieces = []
    for k in range(PIECES):
        part = pl.ds(k * rows, rows)
        pieces.append((first_in.at[part], first.at[part], first_out.at[part]))
    pieces.append((second_in, second, second_out))
    into, out = [], []
    for k, (source, held, target) in enumerate(pieces):
        into.append(pltpu.make_async_copy(source, held, in_sem.at[k]))
        out.append(pltpu.make_async_copy(held, target, out_sem.at[k]))
    for copy in into:
        copy.start()
    for arrival, departure in zip(into, out):
        arrival.wait()
        departure.start()
    for copy in out:
        copy.wait()


def handed_over(first, second):
    away = pl.BlockSpec(memory_space=pl.ANY)
    dma = pltpu.SemaphoreType.DMA
    return pl.pallas_call(
        copy_kernel,
        out_shape=tuple(jax.ShapeDtypeStruct(a.shape, a.dtype) for a in (first, second)),
        in_specs=[away, away],
        out_specs=(away, away),
        scratch_shapes=[
            pltpu.VMEM(first.shape, first.dtype),
            pltpu.VMEM(second.shape, second.dtype),
            dma((PIECES + 1,)),
            dma((PIECES + 1,)),
        ],
        compiler_params=pltpu.CompilerParams(vmem_limit_bytes=58 * 1024 * 1024),
        name="handed_over",
    )(first, second)


def shards(
    queries,
    latents,
    doc_ids,
    hidden_rows,
    expert_ids,
    gate_scores,
    gate_weight,
    up_weight,
    down_weight,
):
    length = lax.axis_size("dp")
    moe_out, attn_out = layer(
        length // (2 * NY),
        NY,
        expert_ids.T,
        gate_scores.T,
        hidden_rows,
        gate_weight[0],
        up_weight[0],
        down_weight[0],
        queries.transpose(1, 2, 0),
        latents.T,
        doc_ids.reshape(length, -1),
    )
    attn_out, moe_out = handed_over(attn_out, moe_out)
    return (attn_out.reshape(queries.shape[:2] + (LAT,)), moe_out)


def solution(mesh):
    placed = (
        P("dp", "mp", None),
        P("dp", None),
        P(),
        P("dp", "mp"),
        P("dp", None),
        P("dp", None),
        P("dp", None, "mp"),
        P("dp", None, "mp"),
        P("dp", "mp", None),
    )
    return jax.shard_map(
        shards,
        mesh=mesh,
        in_specs=placed,
        out_specs=(P("dp", "mp", None), P("dp", "mp")),
        check_vma=False,
    )
```

```python
import functools
import math

import jax
import jax.numpy as jnp
from jax import lax
from jax.experimental import pallas as pl
from jax.experimental.pallas import tpu as pltpu
from jax.sharding import PartitionSpec as P

LAT = 512
LANES = 128
PIECES = 8
SLOTS = 32
CAP = 30
SLOT_BITS = 5
CAP_TIMES, CAP_SHIFT = 34953, 20
assert all(n * CAP_TIMES >> CAP_SHIFT == n // CAP for n in range(2048))
CHUNK = 64
NX = 4
NY = 4
COMBINE_AT = ((10, 0), (12, 1), (14, 2), (16, 3), (18, 4))
COMBINE_LAST = (5, 6, 7)
Z_ORDER = {8: (1, -2, 4, 3, -3, 2, -1, 0), 4: (0, 2, 1, -1), 2: (0, 1)}

score_scale = 1.0 / math.sqrt(192.0)
neg_large = -1e30
MESH = pl.DeviceIdType.MESH


def layer_kernel(
    nz,
    ny,
    ids_in,
    score_in,
    tok_in,
    gate_ref,
    up_ref,
    down_ref,
    query_ref,
    latent_in,
    doc_in,
    out_ref,
    attn_ref,
    disp,
    land,
    rows,
    gu,
    dn,
    relay_dn,
    hid,
    outb,
    ret,
    acc,
    place_ref,
    ghi_ref,
    glo_ref,
    scales,
    query,
    wide,
    attn,
    keys,
    bias,
    ids_ref,
    score_ref,
    tok_ref,
    latent_ref,
    doc_ref,
    in_sem,
    local_sem,
    q_sem,
    lat_send,
    lat_recv,
    w_send,
    w_recv,
    disp_send,
    disp_recv,
    x_send,
    x_recv,
    h_send,
    h_recv,
    ret_send,
    ret_recv,
):
    top, tokens = ids_in.shape
    heads = query_ref.shape[0]
    width = tok_in.shape[1]
    half_in, units = gate_ref.shape
    piece = down_ref.shape[1] // NX
    experts = nz * ny
    plane = ny * SLOTS
    chunk, half = CHUNK, CHUNK // 2
    per = CHUNK // SLOTS
    sent, packed = experts * SLOTS // chunk, experts * CAP // chunk
    own_chunk = Z_ORDER[nz].index(0) * (plane // chunk)
    f32, bf16 = jnp.float32, jnp.bfloat16

    d = lax.axis_index("dp")
    x = lax.axis_index("mp")
    s = lax.rem(d, 2)
    p = lax.div(d, 2)
    z = lax.div(p, ny)
    y = lax.rem(p, ny)
    right = lax.rem(x + 1, NX)
    left = lax.rem(x + NX - 1, NX)
    opposite = lax.rem(x + 2, NX)
    mate = d + 1 - 2 * s

    def dev(zz, yy):
        return (zz * ny + yy) * 2 + s

    def entry(table, i):
        total = 0
        for at, value in enumerate(table):
            total = total + jnp.where(i == at, value, 0)
        return total

    def offset(at):
        return entry(Z_ORDER[nz], at)

    def remote(src, dst, send, recv, dd, xx):
        return pltpu.make_async_remote_copy(
            src_ref=src, dst_ref=dst, send_sem=send, recv_sem=recv,
            device_id=(dd, xx), device_id_type=MESH,
        )

    def wait_in(ref, sem):
        pltpu.make_async_copy(ref, ref, sem).wait()

    own_in = pl.ds(pl.multiple_of(s * half_in, half_in), half_in)
    mate_in = pl.ds(pl.multiple_of((1 - s) * half_in, half_in), half_in)
    own_out = pl.ds(pl.multiple_of(s * piece, piece), piece)
    mate_out = pl.ds(pl.multiple_of((1 - s) * piece, piece), piece)
    gate_cols, up_cols = pl.ds(0, units), pl.ds(units, units)

    def unit_rows(q, start, count):
        return pl.ds(pl.multiple_of(q * units + start, units // 2), count)

    def unit_cols(q):
        return pl.ds(pl.multiple_of(q * units, units), units)

    def down_cols(q):
        return pl.ds(pl.multiple_of(q * piece, piece), piece)

    local_gate = pltpu.make_async_copy(gate_ref, gu.at[own_in, gate_cols], local_sem.at[0])
    local_up = pltpu.make_async_copy(up_ref, gu.at[own_in, up_cols], local_sem.at[1])
    local_down = pltpu.make_async_copy(
        down_ref.at[:, down_cols(x)], dn.at[unit_rows(x, 0, units), own_out], local_sem.at[2]
    )
    local_query = pltpu.make_async_copy(query_ref, query, q_sem.at[0])
    inputs = [
        pltpu.make_async_copy(source, held, in_sem.at[k])
        for k, (source, held) in enumerate(
            (
                (ids_in, ids_ref),
                (score_in, score_ref),
                (tok_in, tok_ref),
                (latent_in, latent_ref),
                (doc_in, doc_ref),
            )
        )
    ]
    for copy in inputs:
        copy.start()

    barrier = pltpu.get_barrier_semaphore()

    def greet(dd, xx):
        pl.semaphore_signal(barrier, inc=1, device_id=(dd, xx), device_id_type=MESH)

    ring = experts * 2
    beside = lax.rem(d + 2 * s - 1 + ring, ring)
    following = lax.rem(d + 1, ring)
    greet(mate, x)
    greet(beside, x)
    greet(d, right)
    greet(d, left)

    def greet_peer(k, carry):
        greet(lax.rem(p + k, experts) * 2 + s, x)
        return carry

    lax.fori_loop(1, experts, greet_peer, 0)
    for copy in [local_gate, local_up, local_down, local_query]:
        copy.start()

    to_mate = [
        remote(gate_ref, gu.at[own_in, gate_cols], w_send.at[0], w_recv.at[0], mate, x),
        remote(up_ref, gu.at[own_in, up_cols], w_send.at[1], w_recv.at[1], mate, x),
    ]
    halfu = units // 2
    to_side = [
        remote(
            down_ref.at[:, down_cols(right)], dn.at[unit_rows(x, 0, units), own_out],
            w_send.at[2], w_recv.at[2], d, right,
        ),
        remote(
            down_ref.at[:, down_cols(left)], dn.at[unit_rows(x, 0, units), own_out],
            w_send.at[3], w_recv.at[3], d, left,
        ),
        remote(
            down_ref.at[pl.ds(0, halfu), down_cols(opposite)], relay_dn.at[0],
            w_send.at[4], w_recv.at[4], d, right,
        ),
        remote(
            down_ref.at[pl.ds(halfu, halfu), down_cols(opposite)], relay_dn.at[1],
            w_send.at[5], w_recv.at[5], d, left,
        ),
    ]
    relays = [
        remote(
            relay_dn.at[0], dn.at[unit_rows(left, 0, halfu), own_out],
            w_send.at[6], w_recv.at[6], d, right,
        ),
        remote(
            relay_dn.at[1], dn.at[unit_rows(right, halfu, halfu), own_out],
            w_send.at[7], w_recv.at[7], d, left,
        ),
    ]
    down_to_mate = remote(
        dn.at[:, own_out], dn.at[:, own_out], w_send.at[8], w_recv.at[8], mate, x
    )

    pl.semaphore_wait(barrier, experts - 1 + 4)
    for copy in to_side[:2] + to_mate + to_side[2:]:
        copy.start()

    for copy in inputs:
        copy.wait()

    expert_at = lax.broadcasted_iota(jnp.int32, (experts, tokens), 0)
    named = jnp.zeros((experts, tokens), f32)
    weight = jnp.zeros((experts, tokens), f32)
    for k in range(top):
        hit = ids_ref[k : k + 1, :] == expert_at
        named = named + jnp.where(hit, 1.0, 0.0)
        weight = weight + jnp.where(hit, score_ref[k : k + 1, :], 0.0)
    row_at = lax.broadcasted_iota(jnp.int32, (tokens, tokens), 0)
    col_at = lax.broadcasted_iota(jnp.int32, (tokens, tokens), 1)
    before = jnp.dot(
        named.astype(bf16),
        jnp.where(row_at < col_at, 1.0, 0.0).astype(bf16),
        preferred_element_type=f32,
    )
    place_ref[...] = jnp.where(named > 0.5, before, -1.0).astype(bf16)
    whole = weight.astype(bf16)
    ghi_ref[...] = whole
    glo_ref[...] = (weight - whole.astype(f32)).astype(bf16)

    def chunk_rows(c):
        return pl.ds(pl.multiple_of(c * chunk, chunk), chunk)

    def block_rows(b):
        return pl.ds(pl.multiple_of(b * SLOTS, SLOTS), SLOTS)

    def peer(b, way):
        zz = lax.rem(z + way * offset(lax.div(b, ny)) + nz, nz)
        return dev(zz, lax.rem(y + way * lax.rem(b, ny) + ny, ny))

    def spread(at, first, count):
        zz = lax.rem(z + offset(at) + nz, nz)
        row = lax.broadcasted_iota(jnp.int32, (count, experts), 0)
        dest = zz * ny + ((y + first + (row >> SLOT_BITS)) & (ny - 1))
        return jnp.where(
            lax.broadcasted_iota(jnp.int32, (count, experts), 1) == dest, 1.0, 0.0
        ).astype(bf16)

    def chosen(sel):
        count = sel.shape[0]
        slot = (lax.broadcasted_iota(jnp.int32, (count, tokens), 0) & (SLOTS - 1)).astype(f32)
        return jnp.dot(sel, place_ref[...], preferred_element_type=f32) == slot

    def build(c):
        first = c * per
        sel = spread(lax.div(first, ny), lax.rem(first, ny), chunk)
        pick = jnp.where(chosen(sel), 1.0, 0.0).astype(bf16)
        block = jnp.dot(pick, tok_ref[...], preferred_element_type=f32).astype(bf16)
        disp[chunk_rows(c), :] = block

    def disp_copy(c, i):
        b = c * per + i
        return remote(
            disp.at[block_rows(b)], land.at[block_rows(b)],
            disp_send.at[c], disp_recv.at[c], peer(b, 1), x,
        )

    def own_block(c):
        return pl.ds(pl.multiple_of(c * chunk, chunk), SLOTS)

    def other_blocks(c):
        return pl.ds(pl.multiple_of(c * chunk + SLOTS, SLOTS), chunk - SLOTS)

    def per_chunk(c, yes, no):
        pl.when(c == own_chunk)(yes)
        pl.when(c != own_chunk)(no)

    def dispatch(c):
        for i in range(1, per):
            disp_copy(c, i).start()

        def keep():
            land[own_block(c), :] = disp[own_block(c), :]

        per_chunk(c, keep, lambda: disp_copy(c, 0).start())

    ahead = min(6, sent)
    for c in range(ahead):
        build(jnp.int32(c))
        dispatch(jnp.int32(c))

    same = row_at == col_at
    keys[tokens:, :] = lax.dot_general(
        jnp.where(same, 1.0, 0.0).astype(bf16), latent_ref[...], (((1,), (1,)), ((), ())),
        preferred_element_type=f32,
    ).astype(bf16)
    lat_copy = remote(
        keys.at[pl.ds(tokens, tokens)], keys.at[pl.ds(0, tokens)],
        lat_send.at[0], lat_recv.at[0], following, x,
    )
    own_ids = doc_ref[pl.ds(d, 1), :]
    old_ids = doc_ref[pl.ds(lax.rem(d + ring - 1, ring), 1), :]
    own_col = jnp.sum(jnp.where(same, own_ids, 0).astype(f32), axis=1, keepdims=True)
    old_col = jnp.sum(jnp.where(same, old_ids, 0).astype(f32), axis=1, keepdims=True)
    old_col = old_col - jnp.where(d == 0, 1000.0, 0.0)
    ids_row = own_ids.astype(f32)
    bias[:tokens, :] = jnp.where(old_col == ids_row, 0.0, neg_large)
    bias[tokens:, :] = jnp.where((own_col == ids_row) & (row_at <= col_at), 0.0, neg_large)
    lat_copy.start()

    def first_half(c):
        return pl.ds(pl.multiple_of(c * chunk, chunk), half)

    def second_half(c):
        return pl.ds(pl.multiple_of(c * chunk + half, half), half)

    def x_copies(c):
        here = rows.at[x, chunk_rows(c)]
        return (
            remote(here, here, x_send.at[0, c], x_recv.at[0, c], d, right),
            remote(here, here, x_send.at[1, c], x_recv.at[1, c], d, left),
        )

    def x_relays(c):
        from_left, from_right = rows.at[left, first_half(c)], rows.at[right, second_half(c)]
        return (
            remote(from_left, from_left, x_send.at[2, c], x_recv.at[2, c], d, right),
            remote(from_right, from_right, x_send.at[3, c], x_recv.at[3, c], d, left),
        )

    def h_copies(c):
        here = hid.at[chunk_rows(c + 1), unit_cols(x)]
        return (
            remote(here, here, h_send.at[0, c], h_recv.at[0, c], d, right),
            remote(here, here, h_send.at[1, c], h_recv.at[1, c], d, left),
        )

    def h_relays(c):
        from_left = hid.at[first_half(c + 1), unit_cols(left)]
        from_right = hid.at[second_half(c + 1), unit_cols(right)]
        return (
            remote(from_left, from_left, h_send.at[2, c], h_recv.at[2, c], d, right),
            remote(from_right, from_right, h_send.at[3, c], h_recv.at[3, c], d, left),
        )

    def ret_copy(c, i):
        b = c * per + i
        return remote(
            outb.at[block_rows(b)], ret.at[block_rows(b)],
            ret_send.at[c], ret_recv.at[c], peer(b, -1), x,
        )

    def arrived(c):
        per_chunk(
            c,
            lambda: wait_in(land.at[other_blocks(c)], disp_recv.at[c]),
            lambda: wait_in(land.at[chunk_rows(c)], disp_recv.at[c]),
        )

    def stage_pack(c):
        @pl.when(c == 0)
        def _():
            arrived(c)

        arrived(c + 1)
        row = lax.broadcasted_iota(jnp.int32, (chunk, 2 * chunk), 0)
        col = lax.broadcasted_iota(jnp.int32, (chunk, 2 * chunk), 1)
        block = ((row + c * chunk) * CAP_TIMES) >> CAP_SHIFT
        take = col == row + (SLOTS - CAP) * block
        window = land[pl.ds(pl.multiple_of(c * chunk, chunk), 2 * chunk), :]
        rows[x, chunk_rows(c), :] = jnp.dot(
            jnp.where(take, 1.0, 0.0).astype(bf16), window, preferred_element_type=f32
        ).astype(bf16)
        for copy in x_copies(c):
            copy.start()

    def stage_relay(c):
        wait_in(rows.at[left, chunk_rows(c)], x_recv.at[0, c])
        wait_in(rows.at[right, chunk_rows(c)], x_recv.at[1, c])
        for copy in x_relays(c):
            copy.start()

    def stage_up(c):
        wait_in(rows.at[opposite, first_half(c)], x_recv.at[2, c])
        wait_in(rows.at[opposite, second_half(c)], x_recv.at[3, c])
        total = jnp.zeros((chunk, 2 * units), f32)
        for m in range(NX):
            total = total + jnp.dot(
                rows[m, chunk_rows(c), :], gu[m * width : (m + 1) * width, :],
                preferred_element_type=f32,
            )
        gate, upper = total[:, :units], total[:, units:]
        hid[chunk_rows(c + 1), unit_cols(x)] = (gate / (1.0 + jnp.exp(-gate)) * upper).astype(bf16)
        for copy in h_copies(c):
            copy.start()

    def stage_hid(c):
        wait_in(hid.at[chunk_rows(c + 1), unit_cols(left)], h_recv.at[0, c])
        wait_in(hid.at[chunk_rows(c + 1), unit_cols(right)], h_recv.at[1, c])
        for copy in h_relays(c):
            copy.start()

    def stage_down(c):
        @pl.when(c < packed)
        def _():
            wait_in(hid.at[first_half(c + 1), unit_cols(opposite)], h_recv.at[2, c])
            wait_in(hid.at[second_half(c + 1), unit_cols(opposite)], h_recv.at[3, c])

        row = lax.broadcasted_iota(jnp.int32, (chunk, 2 * chunk), 0)
        col = lax.broadcasted_iota(jnp.int32, (chunk, 2 * chunk), 1)
        place = c * chunk + row
        held = place - (SLOTS - CAP) * (place >> SLOT_BITS)
        take = (col + (c - 1) * chunk == held) & ((row & (SLOTS - 1)) < CAP)
        window = hid[pl.ds(pl.multiple_of(c * chunk, chunk), 2 * chunk), :]
        value = jnp.dot(
            jnp.where(take, 1.0, 0.0).astype(bf16), window, preferred_element_type=f32
        ).astype(bf16)
        outb[chunk_rows(c), :] = jnp.dot(value, dn[...], preferred_element_type=f32).astype(bf16)
        for i in range(1, per):
            ret_copy(c, i).start()

        def keep():
            ret[own_block(c), :] = outb[own_block(c), :]

        per_chunk(c, keep, lambda: ret_copy(c, 0).start())

    def stage_combine(at):
        for i in range(plane // chunk):
            c = at * (plane // chunk) + i
            per_chunk(
                c,
                lambda c=c: wait_in(ret.at[other_blocks(c)], ret_recv.at[c]),
                lambda c=c: wait_in(ret.at[chunk_rows(c)], ret_recv.at[c]),
            )
        back = ret[pl.ds(pl.multiple_of(at * plane, plane), plane), :]
        total = acc[...]
        for k in range(2):
            total = total + jnp.dot(scales[at, k], back, preferred_element_type=f32)
        acc[...] = total

    def stage_scales(at):
        sel = spread(at, 0, plane)
        taken = chosen(sel)
        for k, part in enumerate((ghi_ref, glo_ref)):
            scale = jnp.dot(sel, part[...], preferred_element_type=f32)
            scales[at, k] = jnp.where(taken, scale, 0.0).T.astype(bf16)

    hid[:chunk, :] = jnp.zeros((chunk, hid.shape[1]), bf16)
    hid[(packed + 1) * chunk :, :] = jnp.zeros((chunk, hid.shape[1]), bf16)
    acc[...] = jnp.zeros_like(acc)

    def head(h, carry):
        scores = jnp.dot(keys[...], query[h], preferred_element_type=f32) * score_scale + bias[...]
        lifted = jnp.exp(scores - jnp.max(scores, axis=0, keepdims=True))
        probs = (lifted / jnp.sum(lifted, axis=0, keepdims=True)).astype(bf16)
        value = lax.dot_general(
            probs, keys[:, :LAT], (((0,), (0,)), ((), ())), preferred_element_type=f32
        )
        for k in range(LAT // LANES):
            wide[k, pl.ds(h, tokens, stride=heads), :] = value[:, k * LANES : (k + 1) * LANES]
        return carry

    parts = min(4, sent)
    attn_copy = pltpu.make_async_copy(attn, attn_ref, q_sem.at[1])

    def drain_x(c):
        for copy in x_copies(c) + x_relays(c):
            copy.wait_send()

    def drain_h(c):
        for copy in h_copies(c) + h_relays(c):
            copy.wait_send()

    def drain_disp(c):
        per_chunk(
            c,
            lambda: wait_in(disp.at[other_blocks(c)], disp_send.at[c]),
            lambda: wait_in(disp.at[chunk_rows(c)], disp_send.at[c]),
        )

    def drain_ret(c, carry=0):
        per_chunk(
            c,
            lambda: wait_in(outb.at[other_blocks(c)], ret_send.at[c]),
            lambda: wait_in(outb.at[chunk_rows(c)], ret_send.at[c]),
        )
        return carry

    def step(t, carry):
        def at(delay, stage, count):
            @pl.when((t >= delay) & (t < delay + count))
            def _():
                stage(t - delay)

        at(0, stage_pack, packed)

        @pl.when(t + ahead < sent)
        def _():
            build(t + ahead)
            dispatch(t + ahead)

        at(1, stage_relay, packed)

        @pl.when(t == 2)
        def _():
            wait_in(relay_dn.at[0], w_recv.at[4])
            wait_in(relay_dn.at[1], w_recv.at[5])
            for copy in relays:
                copy.start()

        @pl.when(t == 1)
        def _():
            local_query.wait()
            wait_in(keys.at[pl.ds(0, tokens)], lat_recv.at[0])

        @pl.when((t >= 1) & (t < 1 + parts))
        def _():
            lax.fori_loop((t - 1) * (heads // parts), t * (heads // parts), head, 0)

        at(2, stage_scales, nz)

        @pl.when(t == 1 + parts)
        def _():
            def narrow(i, carry):
                some = pl.ds(pl.multiple_of(i * tokens, tokens), tokens)
                for k in range(LAT // LANES):
                    attn[some, k * LANES : (k + 1) * LANES] = wide[k, some, :].astype(bf16)
                return carry

            lax.fori_loop(0, heads, narrow, 0)
            attn_copy.start()

        @pl.when(t == 2)
        def _():
            local_gate.wait()
            local_up.wait()
            wait_in(gu.at[mate_in, gate_cols], w_recv.at[0])
            wait_in(gu.at[mate_in, up_cols], w_recv.at[1])

        at(2, stage_up, packed)
        at(3, stage_hid, packed)

        @pl.when(t == 3)
        def _():
            local_down.wait()
            wait_in(dn.at[unit_rows(left, 0, units), own_out], w_recv.at[2])
            wait_in(dn.at[unit_rows(right, 0, units), own_out], w_recv.at[3])
            wait_in(dn.at[unit_rows(opposite, 0, halfu), own_out], w_recv.at[6])
            wait_in(dn.at[unit_rows(opposite, halfu, halfu), own_out], w_recv.at[7])
            down_to_mate.start()

        @pl.when(t == 4)
        def _():
            wait_in(dn.at[:, mate_out], w_recv.at[8])

        at(4, stage_down, sent)

        at(6, drain_x, packed)
        at(7, drain_h, packed)
        at(4, drain_disp, sent)
        at(10, drain_ret, sent)

        @pl.when(t == 12)
        def _():
            attn_copy.wait()
            lat_copy.wait_send()
            for copy in to_side + to_mate + relays + [down_to_mate]:
                copy.wait_send()

        for moment, k in COMBINE_AT:

            @pl.when(t == moment)
            def _(k=k):
                stage_combine(jnp.int32(k))

        return carry

    lax.fori_loop(0, sent + 4, step, 0)
    for c in range(sent + 4 - 6, packed):
        drain_x(c)
    for c in range(sent + 4 - 7, packed):
        drain_h(c)

    def finish(i, carry):
        stage_combine(entry(COMBINE_LAST, i))
        return carry

    lax.fori_loop(0, len(COMBINE_LAST), finish, 0)
    out_ref[...] = acc[...].astype(out_ref.dtype)
    lax.fori_loop(sent + 4 - 10, sent, drain_ret, 0)


def layer(nz, ny, ids, scores, tok, gate, up, down, query, latent, docs):
    tokens, width = tok.shape
    units = gate.shape[1]
    piece = down.shape[1] // NX
    experts = nz * ny
    count, packed = experts * SLOTS, experts * CAP
    sent_n, packed_n = count // CHUNK, packed // CHUNK
    heads, feats, _ = query.shape
    vmem = pl.BlockSpec(memory_space=pltpu.VMEM)
    away = pl.BlockSpec(memory_space=pl.ANY)
    bf16 = jnp.bfloat16
    dma = pltpu.SemaphoreType.DMA
    return pl.pallas_call(
        functools.partial(layer_kernel, nz, ny),
        out_shape=(
            jax.ShapeDtypeStruct((tokens, width), bf16),
            jax.ShapeDtypeStruct((tokens * heads, LAT), bf16),
        ),
        in_specs=[away] * 9,
        out_specs=(vmem, away),
        scratch_shapes=[
            pltpu.VMEM((count, width), bf16),
            pltpu.VMEM((count, width), bf16),
            pltpu.VMEM((NX, packed, width), bf16),
            pltpu.VMEM((NX * width, 2 * units), bf16),
            pltpu.VMEM((NX * units, width), bf16),
            pltpu.VMEM((2, units // 2, piece), bf16),
            pltpu.VMEM((packed + 2 * CHUNK, NX * units), bf16),
            pltpu.VMEM((count, width), bf16),
            pltpu.VMEM((count, width), bf16),
            pltpu.VMEM((tokens, width), jnp.float32),
            pltpu.VMEM((experts, tokens), bf16),
            pltpu.VMEM((experts, tokens), bf16),
            pltpu.VMEM((experts, tokens), bf16),
            pltpu.VMEM((nz, 2, tokens, ny * SLOTS), bf16),
            pltpu.VMEM((heads, feats, tokens), bf16),
            pltpu.VMEM((LAT // LANES, tokens * heads, LANES), jnp.float32),
            pltpu.VMEM((tokens * heads, LAT), bf16),
            pltpu.VMEM((2 * tokens, feats), bf16),
            pltpu.VMEM((2 * tokens, tokens), jnp.float32),
            pltpu.VMEM(ids.shape, ids.dtype),
            pltpu.VMEM(scores.shape, scores.dtype),
            pltpu.VMEM(tok.shape, tok.dtype),
            pltpu.VMEM(latent.shape, latent.dtype),
            pltpu.VMEM(docs.shape, docs.dtype),
            dma((5,)),
            dma((3,)),
            dma((2,)),
            dma((1,)),
            dma((1,)),
            dma((9,)),
            dma((9,)),
            dma((sent_n,)),
            dma((sent_n,)),
            dma((4, packed_n)),
            dma((4, packed_n)),
            dma((4, packed_n)),
            dma((4, packed_n)),
            dma((sent_n,)),
            dma((sent_n,)),
        ],
        compiler_params=pltpu.CompilerParams(
            collective_id=0, has_side_effects=True, vmem_limit_bytes=58 * 1024 * 1024
        ),
        name="layer",
    )(ids, scores, tok, gate, up, down, query, latent, docs)


def copy_kernel(first_in, second_in, first_out, second_out, first, second, in_sem, out_sem):
    rows = first_in.shape[0] // PIECES
    pieces = []
    for k in range(PIECES):
        part = pl.ds(k * rows, rows)
        pieces.append((first_in.at[part], first.at[part], first_out.at[part]))
    pieces.append((second_in, second, second_out))
    into, out = [], []
    for k, (source, held, target) in enumerate(pieces):
        into.append(pltpu.make_async_copy(source, held, in_sem.at[k]))
        out.append(pltpu.make_async_copy(held, target, out_sem.at[k]))
    for copy in into:
        copy.start()
    for arrival, departure in zip(into, out):
        arrival.wait()
        departure.start()
    for copy in out:
        copy.wait()


def handed_over(first, second):
    away = pl.BlockSpec(memory_space=pl.ANY)
    dma = pltpu.SemaphoreType.DMA
    return pl.pallas_call(
        copy_kernel,
        out_shape=tuple(jax.ShapeDtypeStruct(a.shape, a.dtype) for a in (first, second)),
        in_specs=[away, away],
        out_specs=(away, away),
        scratch_shapes=[
            pltpu.VMEM(first.shape, first.dtype),
            pltpu.VMEM(second.shape, second.dtype),
            dma((PIECES + 1,)),
            dma((PIECES + 1,)),
        ],
        compiler_params=pltpu.CompilerParams(vmem_limit_bytes=58 * 1024 * 1024),
        name="handed_over",
    )(first, second)


def shards(
    queries,
    latents,
    doc_ids,
    hidden_rows,
    expert_ids,
    gate_scores,
    gate_weight,
    up_weight,
    down_weight,
):
    length = lax.axis_size("dp")
    moe_out, attn_out = layer(
        length // (2 * NY),
        NY,
        expert_ids.T,
        gate_scores.T,
        hidden_rows,
        gate_weight[0],
        up_weight[0],
        down_weight[0],
        queries.transpose(1, 2, 0),
        latents.T,
        doc_ids.reshape(length, -1),
    )
    attn_out, moe_out = handed_over(attn_out, moe_out)
    return (attn_out.reshape(queries.shape[:2] + (LAT,)), moe_out)


def solution(mesh):
    placed = (
        P("dp", "mp", None),
        P("dp", None),
        P(),
        P("dp", "mp"),
        P("dp", None),
        P("dp", None),
        P("dp", None, "mp"),
        P("dp", None, "mp"),
        P("dp", "mp", None),
    )
    return jax.shard_map(
        shards,
        mesh=mesh,
        in_specs=placed,
        out_specs=(P("dp", "mp", None), P("dp", "mp")),
        check_vma=False,
    )
```

```python
import functools
import math

import jax
import jax.numpy as jnp
from jax import lax
from jax.experimental import pallas as pl
from jax.experimental.pallas import tpu as pltpu
from jax.sharding import PartitionSpec as P

LAT = 512
LANES = 128
PIECES = 8
SLOTS = 32
CAP = 30
CHUNK = 64
NX = 4
NY = 4
Z_ORDER = {8: (1, -2, 4, 3, -3, 2, -1, 0), 4: (0, 2, 1, -1), 2: (0, 1)}

score_scale = 1.0 / math.sqrt(192.0)
neg_large = -1e30
MESH = pl.DeviceIdType.MESH


def layer_kernel(
    nz,
    ny,
    ids_in,
    score_in,
    tok_in,
    gate_ref,
    up_ref,
    down_ref,
    query_ref,
    latent_in,
    doc_in,
    out_ref,
    attn_ref,
    disp,
    land,
    rows,
    gu,
    dn,
    relay_dn,
    hid,
    outb,
    ret,
    acc,
    place_ref,
    ghi_ref,
    glo_ref,
    query,
    wide,
    attn,
    keys,
    bias,
    ids_ref,
    score_ref,
    tok_ref,
    latent_ref,
    doc_ref,
    in_sem,
    local_sem,
    q_sem,
    lat_send,
    lat_recv,
    w_send,
    w_recv,
    disp_send,
    disp_recv,
    x_send,
    x_recv,
    h_send,
    h_recv,
    ret_send,
    ret_recv,
):
    top, tokens = ids_in.shape
    heads = query_ref.shape[0]
    width = tok_in.shape[1]
    half_in, units = gate_ref.shape
    piece = down_ref.shape[1] // NX
    experts = nz * ny
    plane = ny * SLOTS
    chunk, half = CHUNK, CHUNK // 2
    per = CHUNK // SLOTS
    sent, packed = experts * SLOTS // chunk, experts * CAP // chunk
    own_chunk = Z_ORDER[nz].index(0) * (plane // chunk)
    f32, bf16 = jnp.float32, jnp.bfloat16

    d = lax.axis_index("dp")
    x = lax.axis_index("mp")
    s = lax.rem(d, 2)
    p = lax.div(d, 2)
    z = lax.div(p, ny)
    y = lax.rem(p, ny)
    right = lax.rem(x + 1, NX)
    left = lax.rem(x + NX - 1, NX)
    opposite = lax.rem(x + 2, NX)
    mate = d + 1 - 2 * s

    def dev(zz, yy):
        return (zz * ny + yy) * 2 + s

    def offset(c):
        total = 0
        for at, by in enumerate(Z_ORDER[nz]):
            total = total + jnp.where(c == at, by, 0)
        return total

    def remote(src, dst, send, recv, dd, xx):
        return pltpu.make_async_remote_copy(
            src_ref=src, dst_ref=dst, send_sem=send, recv_sem=recv,
            device_id=(dd, xx), device_id_type=MESH,
        )

    def wait_in(ref, sem):
        pltpu.make_async_copy(ref, ref, sem).wait()

    own_in = pl.ds(pl.multiple_of(s * half_in, half_in), half_in)
    mate_in = pl.ds(pl.multiple_of((1 - s) * half_in, half_in), half_in)
    own_out = pl.ds(pl.multiple_of(s * piece, piece), piece)
    mate_out = pl.ds(pl.multiple_of((1 - s) * piece, piece), piece)
    gate_cols, up_cols = pl.ds(0, units), pl.ds(units, units)

    def unit_rows(q, start, count):
        return pl.ds(pl.multiple_of(q * units + start, units // 2), count)

    def unit_cols(q):
        return pl.ds(pl.multiple_of(q * units, units), units)

    def down_cols(q):
        return pl.ds(pl.multiple_of(q * piece, piece), piece)

    local_gate = pltpu.make_async_copy(gate_ref, gu.at[own_in, gate_cols], local_sem.at[0])
    local_up = pltpu.make_async_copy(up_ref, gu.at[own_in, up_cols], local_sem.at[1])
    local_down = pltpu.make_async_copy(
        down_ref.at[:, down_cols(x)], dn.at[unit_rows(x, 0, units), own_out], local_sem.at[2]
    )
    local_query = pltpu.make_async_copy(query_ref, query, q_sem.at[0])
    inputs = [
        pltpu.make_async_copy(source, held, in_sem.at[k])
        for k, (source, held) in enumerate(
            (
                (ids_in, ids_ref),
                (score_in, score_ref),
                (tok_in, tok_ref),
                (latent_in, latent_ref),
                (doc_in, doc_ref),
            )
        )
    ]
    for copy in inputs:
        copy.start()

    barrier = pltpu.get_barrier_semaphore()

    def greet(dd, xx):
        pl.semaphore_signal(barrier, inc=1, device_id=(dd, xx), device_id_type=MESH)

    ring = experts * 2
    beside = lax.rem(d + 2 * s - 1 + ring, ring)
    following = lax.rem(d + 1, ring)
    greet(mate, x)
    greet(beside, x)
    greet(d, right)
    greet(d, left)

    def greet_peer(k, carry):
        greet(lax.rem(p + k, experts) * 2 + s, x)
        return carry

    lax.fori_loop(1, experts, greet_peer, 0)
    for copy in [local_gate, local_up, local_down, local_query]:
        copy.start()
    for copy in inputs:
        copy.wait()

    expert_at = lax.broadcasted_iota(jnp.int32, (experts, tokens), 0)
    named = jnp.zeros((experts, tokens), f32)
    weight = jnp.zeros((experts, tokens), f32)
    for k in range(top):
        hit = ids_ref[k : k + 1, :] == expert_at
        named = named + jnp.where(hit, 1.0, 0.0)
        weight = weight + jnp.where(hit, score_ref[k : k + 1, :], 0.0)
    row_at = lax.broadcasted_iota(jnp.int32, (tokens, tokens), 0)
    col_at = lax.broadcasted_iota(jnp.int32, (tokens, tokens), 1)
    before = jnp.dot(
        named.astype(bf16),
        jnp.where(row_at < col_at, 1.0, 0.0).astype(bf16),
        preferred_element_type=f32,
    )
    place_ref[...] = jnp.where(named > 0.5, before, -1.0).astype(bf16)
    whole = weight.astype(bf16)
    ghi_ref[...] = whole
    glo_ref[...] = (weight - whole.astype(f32)).astype(bf16)

    same = row_at == col_at
    keys[tokens:, :] = lax.dot_general(
        jnp.where(same, 1.0, 0.0).astype(bf16), latent_ref[...], (((1,), (1,)), ((), ())),
        preferred_element_type=f32,
    ).astype(bf16)
    lat_copy = remote(
        keys.at[pl.ds(tokens, tokens)], keys.at[pl.ds(0, tokens)],
        lat_send.at[0], lat_recv.at[0], following, x,
    )
    own_ids = doc_ref[pl.ds(d, 1), :]
    old_ids = doc_ref[pl.ds(lax.rem(d + ring - 1, ring), 1), :]
    own_col = jnp.sum(jnp.where(same, own_ids, 0).astype(f32), axis=1, keepdims=True)
    old_col = jnp.sum(jnp.where(same, old_ids, 0).astype(f32), axis=1, keepdims=True)
    old_col = old_col - jnp.where(d == 0, 1000.0, 0.0)
    ids_row = own_ids.astype(f32)
    bias[:tokens, :] = jnp.where(old_col == ids_row, 0.0, neg_large)
    bias[tokens:, :] = jnp.where((own_col == ids_row) & (row_at <= col_at), 0.0, neg_large)

    to_mate = [
        remote(gate_ref, gu.at[own_in, gate_cols], w_send.at[0], w_recv.at[0], mate, x),
        remote(up_ref, gu.at[own_in, up_cols], w_send.at[1], w_recv.at[1], mate, x),
    ]
    halfu = units // 2
    to_side = [
        remote(
            down_ref.at[:, down_cols(right)], dn.at[unit_rows(x, 0, units), own_out],
            w_send.at[2], w_recv.at[2], d, right,
        ),
        remote(
            down_ref.at[:, down_cols(left)], dn.at[unit_rows(x, 0, units), own_out],
            w_send.at[3], w_recv.at[3], d, left,
        ),
        remote(
            down_ref.at[pl.ds(0, halfu), down_cols(opposite)], relay_dn.at[0],
            w_send.at[4], w_recv.at[4], d, right,
        ),
        remote(
            down_ref.at[pl.ds(halfu, halfu), down_cols(opposite)], relay_dn.at[1],
            w_send.at[5], w_recv.at[5], d, left,
        ),
    ]
    relays = [
        remote(
            relay_dn.at[0], dn.at[unit_rows(left, 0, halfu), own_out],
            w_send.at[6], w_recv.at[6], d, right,
        ),
        remote(
            relay_dn.at[1], dn.at[unit_rows(right, halfu, halfu), own_out],
            w_send.at[7], w_recv.at[7], d, left,
        ),
    ]
    down_to_mate = remote(
        dn.at[:, own_out], dn.at[:, own_out], w_send.at[8], w_recv.at[8], mate, x
    )

    def chunk_rows(c):
        return pl.ds(pl.multiple_of(c * chunk, chunk), chunk)

    def block_rows(b):
        return pl.ds(pl.multiple_of(b * SLOTS, SLOTS), SLOTS)

    def peer(b, way):
        zz = lax.rem(z + way * offset(lax.div(b, ny)) + nz, nz)
        return dev(zz, lax.rem(y + way * lax.rem(b, ny) + ny, ny))

    def spread(at, first, count):
        zz = lax.rem(z + offset(at) + nz, nz)
        row = lax.broadcasted_iota(jnp.int32, (count, experts), 0)
        dest = zz * ny + ((y + first + (row // SLOTS)) % ny)
        return jnp.where(
            lax.broadcasted_iota(jnp.int32, (count, experts), 1) == dest, 1.0, 0.0
        ).astype(bf16)

    def chosen(sel):
        count = sel.shape[0]
        slot = (lax.broadcasted_iota(jnp.int32, (count, tokens), 0) % SLOTS).astype(f32)
        return jnp.dot(sel, place_ref[...], preferred_element_type=f32) == slot

    def build(c):
        first = c * per
        sel = spread(lax.div(first, ny), lax.rem(first, ny), chunk)
        pick = jnp.where(chosen(sel), 1.0, 0.0).astype(bf16)
        block = jnp.dot(pick, tok_ref[...], preferred_element_type=f32).astype(bf16)
        disp[chunk_rows(c), :] = block

    def disp_copy(c, i):
        b = c * per + i
        return remote(
            disp.at[block_rows(b)], land.at[block_rows(b)],
            disp_send.at[c], disp_recv.at[c], peer(b, 1), x,
        )

    def own_block(c):
        return pl.ds(pl.multiple_of(c * chunk, chunk), SLOTS)

    def other_blocks(c):
        return pl.ds(pl.multiple_of(c * chunk + SLOTS, SLOTS), chunk - SLOTS)

    def per_chunk(c, yes, no):
        pl.when(c == own_chunk)(yes)
        pl.when(c != own_chunk)(no)

    def dispatch(c):
        for i in range(1, per):
            disp_copy(c, i).start()

        def keep():
            land[own_block(c), :] = disp[own_block(c), :]

        per_chunk(c, keep, lambda: disp_copy(c, 0).start())

    ahead = min(6, sent)
    for c in range(4):
        build(jnp.int32(c))

    pl.semaphore_wait(barrier, experts - 1 + 4)

    for copy in to_side[:2]:
        copy.start()
    for c in range(ahead):
        if c >= 4:
            build(jnp.int32(c))
        dispatch(jnp.int32(c))
        if c == 1:
            for copy in to_side[2:] + [lat_copy] + to_mate:
                copy.start()

    def first_half(c):
        return pl.ds(pl.multiple_of(c * chunk, chunk), half)

    def second_half(c):
        return pl.ds(pl.multiple_of(c * chunk + half, half), half)

    def x_copies(c):
        here = rows.at[x, chunk_rows(c)]
        return (
            remote(here, here, x_send.at[0, c], x_recv.at[0, c], d, right),
            remote(here, here, x_send.at[1, c], x_recv.at[1, c], d, left),
        )

    def x_relays(c):
        from_left, from_right = rows.at[left, first_half(c)], rows.at[right, second_half(c)]
        return (
            remote(from_left, from_left, x_send.at[2, c], x_recv.at[2, c], d, right),
            remote(from_right, from_right, x_send.at[3, c], x_recv.at[3, c], d, left),
        )

    def h_copies(c):
        here = hid.at[chunk_rows(c + 1), unit_cols(x)]
        return (
            remote(here, here, h_send.at[0, c], h_recv.at[0, c], d, right),
            remote(here, here, h_send.at[1, c], h_recv.at[1, c], d, left),
        )

    def h_relays(c):
        from_left = hid.at[first_half(c + 1), unit_cols(left)]
        from_right = hid.at[second_half(c + 1), unit_cols(right)]
        return (
            remote(from_left, from_left, h_send.at[2, c], h_recv.at[2, c], d, right),
            remote(from_right, from_right, h_send.at[3, c], h_recv.at[3, c], d, left),
        )

    def ret_copy(c, i):
        b = c * per + i
        return remote(
            outb.at[block_rows(b)], ret.at[block_rows(b)],
            ret_send.at[c], ret_recv.at[c], peer(b, -1), x,
        )

    def arrived(c):
        per_chunk(
            c,
            lambda: wait_in(land.at[other_blocks(c)], disp_recv.at[c]),
            lambda: wait_in(land.at[chunk_rows(c)], disp_recv.at[c]),
        )

    def stage_pack(c):
        @pl.when(c == 0)
        def _():
            arrived(c)

        arrived(c + 1)
        row = lax.broadcasted_iota(jnp.int32, (chunk, 2 * chunk), 0)
        col = lax.broadcasted_iota(jnp.int32, (chunk, 2 * chunk), 1)
        take = col == row + (SLOTS - CAP) * ((row + c * chunk) // CAP)
        window = land[pl.ds(pl.multiple_of(c * chunk, chunk), 2 * chunk), :]
        rows[x, chunk_rows(c), :] = jnp.dot(
            jnp.where(take, 1.0, 0.0).astype(bf16), window, preferred_element_type=f32
        ).astype(bf16)
        for copy in x_copies(c):
            copy.start()

    def stage_relay(c):
        wait_in(rows.at[left, chunk_rows(c)], x_recv.at[0, c])
        wait_in(rows.at[right, chunk_rows(c)], x_recv.at[1, c])
        for copy in x_relays(c):
            copy.start()

    def stage_up(c):
        wait_in(rows.at[opposite, first_half(c)], x_recv.at[2, c])
        wait_in(rows.at[opposite, second_half(c)], x_recv.at[3, c])
        total = jnp.zeros((chunk, 2 * units), f32)
        for m in range(NX):
            total = total + jnp.dot(
                rows[m, chunk_rows(c), :], gu[m * width : (m + 1) * width, :],
                preferred_element_type=f32,
            )
        gate, upper = total[:, :units], total[:, units:]
        hid[chunk_rows(c + 1), unit_cols(x)] = (gate / (1.0 + jnp.exp(-gate)) * upper).astype(bf16)
        for copy in h_copies(c):
            copy.start()

    def stage_hid(c):
        wait_in(hid.at[chunk_rows(c + 1), unit_cols(left)], h_recv.at[0, c])
        wait_in(hid.at[chunk_rows(c + 1), unit_cols(right)], h_recv.at[1, c])
        for copy in h_relays(c):
            copy.start()

    def stage_down(c):
        @pl.when(c < packed)
        def _():
            wait_in(hid.at[first_half(c + 1), unit_cols(opposite)], h_recv.at[2, c])
            wait_in(hid.at[second_half(c + 1), unit_cols(opposite)], h_recv.at[3, c])

        row = lax.broadcasted_iota(jnp.int32, (chunk, 2 * chunk), 0)
        col = lax.broadcasted_iota(jnp.int32, (chunk, 2 * chunk), 1)
        place = c * chunk + row
        take = (col + (c - 1) * chunk == place - (SLOTS - CAP) * (place // SLOTS)) & (row % SLOTS < CAP)
        window = hid[pl.ds(pl.multiple_of(c * chunk, chunk), 2 * chunk), :]
        value = jnp.dot(
            jnp.where(take, 1.0, 0.0).astype(bf16), window, preferred_element_type=f32
        ).astype(bf16)
        outb[chunk_rows(c), :] = jnp.dot(value, dn[...], preferred_element_type=f32).astype(bf16)
        for i in range(1, per):
            ret_copy(c, i).start()

        def keep():
            ret[own_block(c), :] = outb[own_block(c), :]

        per_chunk(c, keep, lambda: ret_copy(c, 0).start())

    def stage_combine(at):
        for i in range(plane // chunk):
            c = at * (plane // chunk) + i
            per_chunk(
                c,
                lambda c=c: wait_in(ret.at[other_blocks(c)], ret_recv.at[c]),
                lambda c=c: wait_in(ret.at[chunk_rows(c)], ret_recv.at[c]),
            )
        sel = spread(at, 0, plane)
        taken = chosen(sel)
        back = ret[pl.ds(pl.multiple_of(at * plane, plane), plane), :]
        total = acc[...]
        for part in (ghi_ref, glo_ref):
            scale = jnp.dot(sel, part[...], preferred_element_type=f32)
            scale = jnp.where(taken, scale, 0.0).astype(bf16)
            total = total + lax.dot_general(
                scale, back, (((0,), (0,)), ((), ())), preferred_element_type=f32
            )
        acc[...] = total

    hid[:chunk, :] = jnp.zeros((chunk, hid.shape[1]), bf16)
    hid[(packed + 1) * chunk :, :] = jnp.zeros((chunk, hid.shape[1]), bf16)
    acc[...] = jnp.zeros_like(acc)

    def head(h, carry):
        scores = jnp.dot(keys[...], query[h], preferred_element_type=f32) * score_scale + bias[...]
        lifted = jnp.exp(scores - jnp.max(scores, axis=0, keepdims=True))
        probs = (lifted / jnp.sum(lifted, axis=0, keepdims=True)).astype(bf16)
        value = lax.dot_general(
            probs, keys[:, :LAT], (((0,), (0,)), ((), ())), preferred_element_type=f32
        )
        for k in range(LAT // LANES):
            wide[k, pl.ds(h, tokens, stride=heads), :] = value[:, k * LANES : (k + 1) * LANES]
        return carry

    parts = min(4, sent)
    attn_copy = pltpu.make_async_copy(attn, attn_ref, q_sem.at[1])
    early = min(5, nz)

    def step(t, carry):
        def at(delay, stage, count):
            @pl.when((t >= delay) & (t < delay + count))
            def _():
                stage(t - delay)

        at(0, stage_pack, packed)

        @pl.when(t + ahead < sent)
        def _():
            build(t + ahead)
            dispatch(t + ahead)

        at(1, stage_relay, packed)

        @pl.when(t == 2)
        def _():
            wait_in(relay_dn.at[0], w_recv.at[4])
            wait_in(relay_dn.at[1], w_recv.at[5])
            for copy in relays:
                copy.start()

        @pl.when(t == 0)
        def _():
            local_query.wait()
            wait_in(keys.at[pl.ds(0, tokens)], lat_recv.at[0])

        @pl.when(t < parts)
        def _():
            lax.fori_loop(t * (heads // parts), (t + 1) * (heads // parts), head, 0)

        @pl.when(t == parts)
        def _():
            def narrow(i, carry):
                some = pl.ds(pl.multiple_of(i * tokens, tokens), tokens)
                for k in range(LAT // LANES):
                    attn[some, k * LANES : (k + 1) * LANES] = wide[k, some, :].astype(bf16)
                return carry

            lax.fori_loop(0, heads, narrow, 0)
            attn_copy.start()

        @pl.when(t == 2)
        def _():
            local_gate.wait()
            local_up.wait()
            wait_in(gu.at[mate_in, gate_cols], w_recv.at[0])
            wait_in(gu.at[mate_in, up_cols], w_recv.at[1])

        at(2, stage_up, packed)
        at(3, stage_hid, packed)

        @pl.when(t == 3)
        def _():
            local_down.wait()
            wait_in(dn.at[unit_rows(left, 0, units), own_out], w_recv.at[2])
            wait_in(dn.at[unit_rows(right, 0, units), own_out], w_recv.at[3])
            wait_in(dn.at[unit_rows(opposite, 0, halfu), own_out], w_recv.at[6])
            wait_in(dn.at[unit_rows(opposite, halfu, halfu), own_out], w_recv.at[7])
            down_to_mate.start()

        @pl.when(t == 4)
        def _():
            wait_in(dn.at[:, mate_out], w_recv.at[8])

        at(4, stage_down, sent)

        @pl.when(lax.rem(t, 2) == 0)
        def _():
            @pl.when((t >= 10) & (t < 10 + 2 * early))
            def _():
                stage_combine(lax.div(t - 10, 2))

        return carry

    lax.fori_loop(0, sent + 4, step, 0)

    def finish(at, carry):
        stage_combine(at)
        return carry

    lax.fori_loop(early, nz, finish, 0)
    out_ref[...] = acc[...].astype(out_ref.dtype)

    attn_copy.wait()
    lat_copy.wait_send()
    for copy in to_side + to_mate + relays + [down_to_mate]:
        copy.wait_send()

    def drain(c, carry):
        for copy in x_copies(c) + x_relays(c) + h_copies(c) + h_relays(c):
            copy.wait_send()
        return carry

    lax.fori_loop(0, packed, drain, 0)

    def drain_sent(c, carry):
        def some():
            wait_in(disp.at[other_blocks(c)], disp_send.at[c])
            wait_in(outb.at[other_blocks(c)], ret_send.at[c])

        def whole():
            wait_in(disp.at[chunk_rows(c)], disp_send.at[c])
            wait_in(outb.at[chunk_rows(c)], ret_send.at[c])

        per_chunk(c, some, whole)
        return carry

    lax.fori_loop(0, sent, drain_sent, 0)


def layer(nz, ny, ids, scores, tok, gate, up, down, query, latent, docs):
    tokens, width = tok.shape
    units = gate.shape[1]
    piece = down.shape[1] // NX
    experts = nz * ny
    count, packed = experts * SLOTS, experts * CAP
    sent_n, packed_n = count // CHUNK, packed // CHUNK
    heads, feats, _ = query.shape
    vmem = pl.BlockSpec(memory_space=pltpu.VMEM)
    away = pl.BlockSpec(memory_space=pl.ANY)
    bf16 = jnp.bfloat16
    dma = pltpu.SemaphoreType.DMA
    return pl.pallas_call(
        functools.partial(layer_kernel, nz, ny),
        out_shape=(
            jax.ShapeDtypeStruct((tokens, width), bf16),
            jax.ShapeDtypeStruct((tokens * heads, LAT), bf16),
        ),
        in_specs=[away] * 9,
        out_specs=(vmem, away),
        scratch_shapes=[
            pltpu.VMEM((count, width), bf16),
            pltpu.VMEM((count, width), bf16),
            pltpu.VMEM((NX, packed, width), bf16),
            pltpu.VMEM((NX * width, 2 * units), bf16),
            pltpu.VMEM((NX * units, width), bf16),
            pltpu.VMEM((2, units // 2, piece), bf16),
            pltpu.VMEM((packed + 2 * CHUNK, NX * units), bf16),
            pltpu.VMEM((count, width), bf16),
            pltpu.VMEM((count, width), bf16),
            pltpu.VMEM((tokens, width), jnp.float32),
            pltpu.VMEM((experts, tokens), bf16),
            pltpu.VMEM((experts, tokens), bf16),
            pltpu.VMEM((experts, tokens), bf16),
            pltpu.VMEM((heads, feats, tokens), bf16),
            pltpu.VMEM((LAT // LANES, (tokens + 1) * heads, LANES), jnp.float32),
            pltpu.VMEM((tokens * heads, LAT), bf16),
            pltpu.VMEM((2 * tokens, feats), bf16),
            pltpu.VMEM((2 * tokens, tokens), jnp.float32),
            pltpu.VMEM(ids.shape, ids.dtype),
            pltpu.VMEM(scores.shape, scores.dtype),
            pltpu.VMEM(tok.shape, tok.dtype),
            pltpu.VMEM(latent.shape, latent.dtype),
            pltpu.VMEM(docs.shape, docs.dtype),
            dma((5,)),
            dma((3,)),
            dma((2,)),
            dma((1,)),
            dma((1,)),
            dma((9,)),
            dma((9,)),
            dma((sent_n,)),
            dma((sent_n,)),
            dma((4, packed_n)),
            dma((4, packed_n)),
            dma((4, packed_n)),
            dma((4, packed_n)),
            dma((sent_n,)),
            dma((sent_n,)),
        ],
        compiler_params=pltpu.CompilerParams(
            collective_id=0, has_side_effects=True, vmem_limit_bytes=58 * 1024 * 1024
        ),
        name="layer",
    )(ids, scores, tok, gate, up, down, query, latent, docs)


def copy_kernel(first_in, second_in, first_out, second_out, first, second, in_sem, out_sem):
    rows = first_in.shape[0] // PIECES
    pieces = []
    for k in range(PIECES):
        part = pl.ds(k * rows, rows)
        pieces.append((first_in.at[part], first.at[part], first_out.at[part]))
    pieces.append((second_in, second, second_out))
    into, out = [], []
    for k, (source, held, target) in enumerate(pieces):
        into.append(pltpu.make_async_copy(source, held, in_sem.at[k]))
        out.append(pltpu.make_async_copy(held, target, out_sem.at[k]))
    for copy in into:
        copy.start()
    for arrival, departure in zip(into, out):
        arrival.wait()
        departure.start()
    for copy in out:
        copy.wait()


def handed_over(first, second):
    away = pl.BlockSpec(memory_space=pl.ANY)
    dma = pltpu.SemaphoreType.DMA
    return pl.pallas_call(
        copy_kernel,
        out_shape=tuple(jax.ShapeDtypeStruct(a.shape, a.dtype) for a in (first, second)),
        in_specs=[away, away],
        out_specs=(away, away),
        scratch_shapes=[
            pltpu.VMEM(first.shape, first.dtype),
            pltpu.VMEM(second.shape, second.dtype),
            dma((PIECES + 1,)),
            dma((PIECES + 1,)),
        ],
        compiler_params=pltpu.CompilerParams(vmem_limit_bytes=58 * 1024 * 1024),
        name="handed_over",
    )(first, second)


def shards(
    queries,
    latents,
    doc_ids,
    hidden_rows,
    expert_ids,
    gate_scores,
    gate_weight,
    up_weight,
    down_weight,
):
    length = lax.axis_size("dp")
    moe_out, attn_out = layer(
        length // (2 * NY),
        NY,
        expert_ids.T,
        gate_scores.T,
        hidden_rows,
        gate_weight[0],
        up_weight[0],
        down_weight[0],
        queries.transpose(1, 2, 0),
        latents.T,
        doc_ids.reshape(length, -1),
    )
    attn_out, moe_out = handed_over(attn_out, moe_out)
    return (attn_out.reshape(queries.shape[:2] + (LAT,)), moe_out)


def solution(mesh):
    placed = (
        P("dp", "mp", None),
        P("dp", None),
        P(),
        P("dp", "mp"),
        P("dp", None),
        P("dp", None),
        P("dp", None, "mp"),
        P("dp", None, "mp"),
        P("dp", "mp", None),
    )
    return jax.shard_map(
        shards,
        mesh=mesh,
        in_specs=placed,
        out_specs=(P("dp", "mp", None), P("dp", "mp")),
        check_vma=False,
    )
```
